256 devices in a mesh: seq: 32 (over z, y), prompt: 8 (over x, core).
Axes of the slice: x: 4, y: 4, z: 8, core: 2. Of those that a mesh axis runs over, the one named last changes fastest.
Arguments:
- queries: bfloat16 [65536, 1024], P(('prompt', 'seq')), parts along dimension 0, may hold values from -6 to 6
- keys: bfloat16 [65536, 1024], P(('prompt', 'seq')), parts along dimension 0, may hold values from -6 to 6
- values: bfloat16 [65536, 1024], P(('prompt', 'seq')), parts along dimension 0, may hold values from -6 to 6
- cotangent: bfloat16 [65536, 1024], P(('prompt', 'seq')), parts along dimension 0, may hold values from -6 to 6
- restrict_one: bfloat16 [8, 256], replicated, may hold values from -0.375 to 0.375
- restrict_two: bfloat16 [4, 256], replicated, may hold values from -0.375 to 0.375
Outputs:
- attended: bfloat16 [65536, 1024], P(('prompt', 'seq')), parts along dimension 0
- grad_q: bfloat16 [65536, 1024], P(('prompt', 'seq')), parts along dimension 0
- grad_k: bfloat16 [65536, 1024], P(('prompt', 'seq')), parts along dimension 0
- grad_v: bfloat16 [65536, 1024], P(('prompt', 'seq')), parts along dimension 0
The draws below stay inside these ranges and needn't reach their ends.
There are 8 independent parts, one for each index of `prompt`. The reference program is written for one: setup_inputs(seed, part) draws one part's arguments, and reference() takes and returns one part's arrays. A program takes and returns all parts, laid end to end along the dimension named above; an argument that names none is the same for every part. Nothing has to cross between parts.
All inputs are finite; a program needn't handle non-finite values.
Results may differ from the reference program's by a relative error of at most 0.02.
Values may be sent and summed in bfloat16 or wider, within the bound.
A program may use at most 128 MiB of HBM per device.

```python
import math
import jax
import jax.numpy as jnp
from jax import lax

D = 1024
HEADS = 16
HEAD_DIM = 64
BLOCK = 256
COARSE_ONE = 8
COARSE_TWO = 4
SEQ = 8192
N_SEQ = 32


def draw_queries(key, part):
    key = jax.random.fold_in(key, 11)
    return jnp.clip(1.5 * jax.random.normal(key, (SEQ, D), jnp.float32), -6.0, 6.0).astype(jnp.bfloat16)


def draw_keys(key, part):
    key = jax.random.fold_in(key, 12)
    return jnp.clip(1.5 * jax.random.normal(key, (SEQ, D), jnp.float32), -6.0, 6.0).astype(jnp.bfloat16)


def level_of(key, shape, pieces, smallest, top_value):
    def one(position, blocks):
        draws = jax.random.uniform(jax.random.fold_in(jax.random.fold_in(key, 6), position), (blocks,), jnp.float32, smallest / len(pieces), top_value / len(pieces))
        return jnp.repeat(jnp.exp(draws), shape[position] // blocks).reshape((-1,) + (1,) * (len(shape) - position - 1))

    gain = one(*pieces[0])
    for cut in pieces[1:]:
        gain = gain * one(*cut)
    return gain


def normal_values(stream_key, extent, scale, reach, cuts=(), kind=jnp.bfloat16):
    values = jax.random.normal(stream_key, extent, jnp.float32) * scale
    if len(cuts) > 0:
        values = level_of(stream_key, extent, cuts, -0.22, 0.18) * values
    return jnp.clip(values, min=-reach, max=reach).astype(kind)


def setup_inputs(seed: int = 0, part: int = 0) -> dict:
    key_list = jax.random.split(jax.random.key(seed), 7)
    part_keys = jax.random.split(jax.random.fold_in(key_list[6], part), 7)
    return {
        "queries": draw_queries(jax.random.fold_in(jax.random.fold_in(key_list[6], part), 71), part),
        "keys": draw_keys(jax.random.fold_in(jax.random.fold_in(key_list[6], part), 71), part),
        "values": normal_values(part_keys[2], (SEQ, D), 1.0, 6.0, ((0, 32),)),
        "cotangent": normal_values(part_keys[3], (SEQ, D), 1.0, 6.0, ((0, 32),)),
        "restrict_one": normal_values(key_list[4], (COARSE_ONE, BLOCK), BLOCK ** -0.5, 0.375),
        "restrict_two": normal_values(key_list[5], (COARSE_TWO, BLOCK), BLOCK ** -0.5, 0.375),
    }


level_one_bias = math.log(32.0)
level_two_bias = math.log(64.0)
masked_bias = -1e+30

def attend_block(query_block, cotangent_block, key_rows, key_bias):
    row_count = query_block.shape[0]
    key_count = key_rows.shape[0]
    scaling = 1.0 / math.sqrt(HEAD_DIM)
    query_heads = query_block.astype(jnp.float32).reshape(row_count, HEADS, HEAD_DIM)
    cotangent_heads = cotangent_block.astype(jnp.float32).reshape(row_count, HEADS, HEAD_DIM)
    key_heads = key_rows[:, :D].astype(jnp.float32).reshape(key_count, HEADS, HEAD_DIM)
    value_heads = key_rows[:, D:].astype(jnp.float32).reshape(key_count, HEADS, HEAD_DIM)
    scores = jnp.einsum('qhd,khd->hqk', query_heads, key_heads) * scaling + key_bias[None, None, :]
    highest = lax.optimization_barrier(jnp.max(scores, axis=2))
    log_total = highest + jnp.log(lax.optimization_barrier(jnp.sum(jnp.exp(scores - highest[:, :, None]), axis=2)))
    probs = jnp.exp(scores - log_total[:, :, None])
    weights = lax.optimization_barrier(probs.astype(jnp.bfloat16)).astype(jnp.float32)
    attended = jnp.einsum('hqk,khd->qhd', weights, value_heads).astype(jnp.bfloat16)
    attended_wide = lax.optimization_barrier(attended).astype(jnp.float32)
    delta = jnp.einsum('qhd,qhd->hq', cotangent_heads, attended_wide)
    dots = jnp.einsum('qhd,khd->hqk', cotangent_heads, value_heads)
    score_grad = lax.optimization_barrier((probs * (dots - delta[:, :, None])).astype(jnp.bfloat16)).astype(jnp.float32)
    grad_query = (jnp.einsum('hqk,khd->qhd', score_grad, key_heads) * scaling).reshape(row_count, D)
    grad_key = (jnp.einsum('hqk,qhd->khd', score_grad, query_heads) * scaling).reshape(key_count, D)
    grad_value = jnp.einsum('hqk,qhd->khd', weights, cotangent_heads).reshape(key_count, D)
    return (attended.reshape(row_count, D), grad_query.astype(jnp.bfloat16), jnp.concatenate([grad_key, grad_value], axis=1))

def reference(queries, keys, values, cotangent, restrict_one, restrict_two):
    width = 2 * D
    paired = jnp.concatenate([keys, values], axis=1)
    blocks = paired.reshape(N_SEQ, BLOCK, width).astype(jnp.float32)
    coarse_one = jnp.einsum('fb,nbc->nfc', restrict_one.astype(jnp.float32), blocks).astype(jnp.bfloat16)
    coarse_two = jnp.einsum('fb,nbc->nfc', restrict_two.astype(jnp.float32), blocks).astype(jnp.bfloat16)
    paired_padded = jnp.pad(paired, ((BLOCK, BLOCK), (0, 0)))
    one_padded = jnp.pad(coarse_one.reshape(N_SEQ * COARSE_ONE, width), ((3 * COARSE_ONE, 3 * COARSE_ONE), (0, 0)))
    two_all = coarse_two.reshape(N_SEQ * COARSE_TWO, width)
    near_offset = jnp.repeat(jnp.array([-1, 0, 1], dtype=jnp.int32), BLOCK)
    middle_offset = jnp.repeat(jnp.array([-3, -2, 2, 3], dtype=jnp.int32), COARSE_ONE)
    far_block = jnp.repeat(jnp.arange(N_SEQ, dtype=jnp.int32), COARSE_TWO)

    def step(carry, block_index):
        grad_near, grad_middle, grad_far = carry
        start = (block_index * BLOCK).astype(jnp.int32)
        near_keys = lax.dynamic_slice_in_dim(paired_padded, start, 3 * BLOCK, 0)
        window = lax.dynamic_slice_in_dim(one_padded, (block_index * COARSE_ONE).astype(jnp.int32), 7 * COARSE_ONE, 0)
        middle_keys = jnp.concatenate([window[:2 * COARSE_ONE], window[5 * COARSE_ONE:]], axis=0)
        key_rows = jnp.concatenate([near_keys, middle_keys, two_all], axis=0)
        near_place = block_index + near_offset
        middle_place = block_index + middle_offset
        near_valid = (near_place >= 0) & (near_place < N_SEQ)
        middle_valid = (middle_place >= 0) & (middle_place < N_SEQ)
        far_valid = jnp.abs(far_block - block_index) >= 4
        key_bias = jnp.concatenate([jnp.where(near_valid, 0.0, masked_bias), jnp.where(middle_valid, level_one_bias, masked_bias), jnp.where(far_valid, level_two_bias, masked_bias)]).astype(jnp.float32)
        query_block = lax.dynamic_slice_in_dim(queries, start, BLOCK, 0)
        cotangent_block = lax.dynamic_slice_in_dim(cotangent, start, BLOCK, 0)
        attended, grad_query, key_grads = attend_block(query_block, cotangent_block, key_rows, key_bias)
        near_sum = lax.dynamic_slice_in_dim(grad_near, start, 3 * BLOCK, 0) + key_grads[:3 * BLOCK]
        grad_near = lax.dynamic_update_slice_in_dim(grad_near, near_sum, start, 0)
        middle_grads = key_grads[3 * BLOCK:3 * BLOCK + 4 * COARSE_ONE]
        window_grads = jnp.concatenate([middle_grads[:2 * COARSE_ONE], jnp.zeros((3 * COARSE_ONE, width), jnp.float32), middle_grads[2 * COARSE_ONE:]], axis=0)
        middle_start = (block_index * COARSE_ONE).astype(jnp.int32)
        middle_sum = lax.dynamic_slice_in_dim(grad_middle, middle_start, 7 * COARSE_ONE, 0) + window_grads
        grad_middle = lax.dynamic_update_slice_in_dim(grad_middle, middle_sum, middle_start, 0)
        grad_far = grad_far + key_grads[3 * BLOCK + 4 * COARSE_ONE:]
        return ((grad_near, grad_middle, grad_far), (attended, grad_query))
    initial = (jnp.zeros((SEQ + 2 * BLOCK, width), jnp.float32), jnp.zeros(((N_SEQ + 6) * COARSE_ONE, width), jnp.float32), jnp.zeros((N_SEQ * COARSE_TWO, width), jnp.float32))
    (grad_near, grad_middle, grad_far), (attended_blocks, grad_q_blocks) = lax.scan(step, initial, jnp.arange(N_SEQ, dtype=jnp.int32))
    attended = attended_blocks.reshape(SEQ, D)
    grad_q = grad_q_blocks.reshape(SEQ, D)
    fine_grads = grad_near[BLOCK:BLOCK + SEQ].reshape(N_SEQ, BLOCK, width)
    middle_own = grad_middle[3 * COARSE_ONE:3 * COARSE_ONE + N_SEQ * COARSE_ONE].reshape(N_SEQ, COARSE_ONE, width)
    far_own = grad_far.reshape(N_SEQ, COARSE_TWO, width)
    total = fine_grads + jnp.einsum('fb,nfc->nbc', restrict_one.astype(jnp.float32), middle_own, precision=lax.Precision.HIGHEST)
    total = total + jnp.einsum('fb,nfc->nbc', restrict_two.astype(jnp.float32), far_own, precision=lax.Precision.HIGHEST)
    total = total.reshape(SEQ, width)
    return (attended, grad_q, total[:, :D].astype(jnp.bfloat16), total[:, D:].astype(jnp.bfloat16))
```

```python
import functools
import math

import jax
import jax.numpy as jnp
from jax import lax
from jax.experimental import pallas as pl
from jax.experimental.pallas import tpu as pltpu
from jax.sharding import PartitionSpec as P

HEAD_DIM = 64
ROWS = 256
PAIR = 128
Y = 4
Z = 8
BLOCKS = Y * Z
ONE = 8
TWO = 4
MID = (-3, -2, 2, 3)
MID_ROWS = len(MID) * ONE
FAR_ROWS = (Z - 1) * Y * TWO
COARSE = MID_ROWS + FAR_ROWS
NEAR = 3 * ROWS
KEYS = NEAR + COARSE
PADDED = 4 * ROWS
CHUNK = 48
MASKED = -1e30
F32 = jnp.float32
BF16 = jnp.bfloat16
MESH = pl.DeviceIdType.MESH


def dot(a, b, ca, cb):
    return lax.dot_general(a, b, (((ca,), (cb,)), ((), ())), preferred_element_type=F32)


def group_max(x):
    return jnp.max(x.reshape(x.shape[0] // 8, 8, x.shape[1]), axis=0)


def group_sum(x):
    return jnp.sum(x.reshape(x.shape[0] // 8, 8, x.shape[1]), axis=0)


def kernel(
    groups, parts,
    q_hbm, k_hbm, v_hbm, do_hbm, r1_ref, r2_ref,
    att_hbm, gq_hbm, gk_hbm, gv_hbm,
    own_in, near_kv, near_send, near_recv, own_grad, coarse,
    c1_send, c1_recv, c2_send, c2_recv, z_send, mg_send, mg_recv, fg_send, fg_recv, yg_send, yg_recv,
    restrict, pack, gathered, bias, q_stack, do_stack, key_t, value_t, do_t, score, dots, prob, grad,
    att_t, gq_t, stage, coarse_sum, restrict_t,
    load_sem, near_send_sem, near_recv_sem, grad_send_sem, grad_recv_sem,
    c1_send_sem, c1_recv_sem, c2_send_sem, c2_recv_sem, z_send_sem, z_recv_sem,
    mg_send_sem, mg_recv_sem, fg_send_sem, fg_recv_sem, yg_send_sem, yg_recv_sem, out_sem,
):
    width = groups * PAIR
    half = width // 2
    part_groups = groups // parts
    part_width = width // parts
    me = lax.axis_index("seq")
    z = me // Y
    y = me % Y

    def at_block(offset):
        return lax.rem(me + offset + BLOCKS, BLOCKS)

    def at_y(offset):
        return z * Y + lax.rem(y + offset + Y, Y)

    def at_z(offset):
        return lax.rem(z + offset + Z, Z) * Y + y

    def remote(src, dst, send_sem, recv_sem, to):
        return pltpu.make_async_remote_copy(
            src_ref=src, dst_ref=dst, send_sem=send_sem, recv_sem=recv_sem,
            device_id={"seq": to}, device_id_type=MESH,
        )

    def columns(index, size):
        return pl.ds(pl.multiple_of(index * size, size), size)

    loads = [
        pltpu.make_async_copy(src, own_in.at[i], load_sem.at[i])
        for i, src in enumerate((k_hbm, v_hbm, q_hbm, do_hbm))
    ]
    for load in loads:
        load.start()

    barrier = pltpu.get_barrier_semaphore()
    partners = [at_block(o) for o in (-1, 1) + MID]
    partners += [at_y(j) for j in range(1, Y)] + [at_z(k) for k in range(1, Z)]
    for partner in partners:
        pl.semaphore_signal(barrier, inc=1, device_id={"seq": partner}, device_id_type=MESH)
    pl.semaphore_wait(barrier, len(partners))

    def near_copy(side, which, g):
        src = (k_hbm, v_hbm)[which].at[:, columns(g, PAIR)]
        return remote(
            src, near_kv.at[side, g, pl.ds(which * ROWS, ROWS)],
            near_send_sem.at[side, which, g], near_recv_sem.at[side, which, g],
            at_block(1 if side == 0 else -1),
        )

    def send_near(g, carry):
        for side in range(2):
            for which in range(2):
                near_copy(side, which, g).start()
        return carry

    lax.fori_loop(0, groups, send_near, 0)

    restrict[...] = jnp.zeros_like(restrict)
    restrict[0:ONE, :] = r1_ref[...].astype(F32)
    restrict[ONE:ONE + TWO, :] = r2_ref[...].astype(F32)
    restrict_b = restrict[...].astype(BF16)
    restrict_t[...] = restrict[...].T.astype(BF16)
    loads[0].wait()
    loads[1].wait()
    coarse_k = dot(restrict_b, own_in[0], 1, 0)
    coarse_v = dot(restrict_b, own_in[1], 1, 0)
    gathered[0] = coarse_k
    gathered[1] = coarse_v

    def pack_rows(first):
        for which in range(2):
            for side in range(2):
                row = TWO * (2 * which + side)
                pack[row:row + TWO, :] = gathered[which, first:first + TWO, side * half:(side + 1) * half]
        return pack[...].astype(BF16)

    c2_send[...] = pack_rows(ONE)
    c2_copies = [
        remote(c2_send, c2_recv.at[j - 1], c2_send_sem.at[j - 1], c2_recv_sem.at[j - 1], at_y(j))
        for j in range(1, Y)
    ]
    for copy in c2_copies:
        copy.start()
    c1_send[...] = jnp.concatenate([coarse_k[0:ONE], coarse_v[0:ONE]], axis=0).astype(BF16)
    c1_copies = [
        remote(c1_send, c1_recv.at[s], c1_send_sem.at[s], c1_recv_sem.at[s], at_block(-o))
        for s, o in enumerate(MID)
    ]
    for copy in c1_copies:
        copy.start()

    row = lax.broadcasted_iota(jnp.int32, (COARSE, ROWS), 0)
    slot = row >> 3
    offset = jnp.where(slot == 0, -3, jnp.where(slot == 1, -2, jnp.where(slot == 2, 2, 3)))
    place = me + offset
    middle = jnp.where((place >= 0) & (place < BLOCKS), math.log(32.0), MASKED)
    far_row = row - MID_ROWS
    far_z = (z - 1 - (far_row >> 4)) & (Z - 1)
    far_y = (y - ((far_row >> 2) & 3)) & (Y - 1)
    distance = jnp.abs(far_z * Y + far_y - me)
    far = jnp.where(distance >= 4, math.log(64.0), MASKED)
    bias[...] = jnp.where(row < MID_ROWS, middle, far)
    left_bias = jnp.where(me >= 1, 0.0, MASKED).astype(F32)
    right_bias = jnp.where(me < BLOCKS - 1, 0.0, MASKED).astype(F32)
    for which in range(2):
        coarse[which, COARSE:ROWS, :] = jnp.zeros((ROWS - COARSE, width), BF16)
    prob[KEYS:PADDED, :] = jnp.zeros((PADDED - KEYS, 2 * ROWS), BF16)
    grad[KEYS:PADDED, :] = jnp.zeros((PADDED - KEYS, 2 * ROWS), BF16)

    for j in range(Y):
        if j == 0:
            block = c2_send[...]
        else:
            c2_copies[j - 1].wait_recv()
            block = c2_recv[j - 1]
        pack[...] = block.astype(F32)
        for which in range(2):
            for side in range(2):
                first = TWO * (2 * which + side)
                gathered[which, TWO * j:TWO * (j + 1), side * half:(side + 1) * half] = pack[first:first + TWO, :]
    z_send[...] = gathered[...].astype(BF16)

    def z_copy(k, part):
        cols = columns(part, part_width)
        return remote(
            z_send.at[:, :, cols],
            coarse.at[:, pl.ds(MID_ROWS + (k - 1) * Y * TWO, Y * TWO), cols],
            z_send_sem.at[part, k - 1], z_recv_sem.at[part, k - 1], at_z(k),
        )

    for part in range(parts):
        for k in range(1, Z):
            z_copy(k, part).start()

    for copy in c1_copies:
        copy.wait_recv()
    for which in range(2):
        rows = [c1_recv[s].astype(F32)[which * ONE:(which + 1) * ONE] for s in range(len(MID))]
        coarse[which, 0:MID_ROWS, :] = jnp.concatenate(rows, axis=0).astype(BF16)
    loads[2].wait()
    loads[3].wait()

    def grad_copy(side, g):
        return remote(
            near_send.at[side, g], near_recv.at[1 - side, g],
            grad_send_sem.at[side, g], grad_recv_sem.at[1 - side, g],
            at_block(-1 if side == 0 else 1),
        )

    def mg_copy(s, part):
        cols = columns(part, part_width)
        return remote(
            mg_send.at[s, :, cols], mg_recv.at[s, :, cols],
            mg_send_sem.at[part, s], mg_recv_sem.at[part, s], at_block(MID[s]),
        )

    def fg_copy(k, part):
        cols = columns(part, part_width)
        return remote(
            fg_send.at[k - 1, :, :, cols], fg_recv.at[k - 1, :, :, cols],
            fg_send_sem.at[part, k - 1], fg_recv_sem.at[part, k - 1], at_z(-k),
        )

    def out_copy(which, g):
        out = (att_hbm, gq_hbm, gk_hbm, gv_hbm)[which]
        return pltpu.make_async_copy(stage.at[which, g], out.at[:, columns(g, PAIR)], out_sem.at[which, g])

    def pair(g, carry):
        cols = columns(g, PAIR)
        part = g // part_groups

        @pl.when(g % part_groups == 0)
        def _():
            for k in range(1, Z):
                z_copy(k, part).wait_recv()

        for side in range(2):
            for which in range(2):
                near_copy(side, which, g).wait_recv()

        def key_value(which):
            first = which * ROWS
            return (
                near_kv[0, g, first:first + ROWS, :],
                own_in[which, :, cols],
                near_kv[1, g, first:first + ROWS, :],
                coarse[which, :, cols],
            )

        q = own_in[2, :, cols].astype(F32) * (1.0 / math.sqrt(HEAD_DIM))
        do = own_in[3, :, cols].astype(F32)
        lane = lax.broadcasted_iota(jnp.int32, (ROWS, PAIR), 1)
        for h in range(2):
            mine = (lane >= HEAD_DIM) if h else (lane < HEAD_DIM)
            q_stack[h * ROWS:(h + 1) * ROWS, :] = jnp.where(mine, q, 0.0).astype(BF16)
            do_stack[h * ROWS:(h + 1) * ROWS, :] = jnp.where(mine, do, 0.0).astype(BF16)
        do_t[...] = do.T
        keys = key_value(0)
        values = key_value(1)
        for i in range(4):
            key_t[:, i * ROWS:(i + 1) * ROWS] = keys[i].T
            value_t[:, i * ROWS:(i + 1) * ROWS] = values[i].T
        counts = (ROWS, ROWS, ROWS, COARSE)
        biases = (left_bias, None, right_bias, bias)
        for h in range(2):
            qh = q_stack[h * ROWS:(h + 1) * ROWS, :]
            doh = do_stack[h * ROWS:(h + 1) * ROWS, :]
            lanes = slice(h * ROWS, (h + 1) * ROWS)
            top = None
            for i in range(4):
                n = counts[i]
                s = dot(keys[i][:n], qh, 1, 1)
                if i == 3:
                    s = s + bias[...]
                elif biases[i] is not None:
                    s = s + biases[i]
                score[h, i * ROWS:i * ROWS + n, :] = s
                m = group_max(s)
                top = m if top is None else jnp.maximum(top, m)
                dots[h, i * ROWS:i * ROWS + n, :] = dot(values[i][:n], doh, 1, 1)
            top = jnp.max(top, axis=0, keepdims=True)
            total = jnp.zeros((8, ROWS), F32)
            for c in range(0, KEYS, CHUNK):
                p = jnp.exp(score[h, c:c + CHUNK, :] - top)
                score[h, c:c + CHUNK, :] = p
                total = total + group_sum(p)
            inverse = 1.0 / jnp.sum(total, axis=0, keepdims=True)
            for c in range(0, KEYS, CHUNK):
                p = score[h, c:c + CHUNK, :] * inverse
                prob[c:c + CHUNK, lanes] = p.astype(BF16)
            head = slice(h * HEAD_DIM, (h + 1) * HEAD_DIM)
            att = dot(value_t[head, :], prob[:, lanes], 1, 0).astype(BF16).astype(F32)
            att_t[head, :] = att
            delta = jnp.sum(att * do_t[head, :], axis=0, keepdims=True)
            for c in range(0, KEYS, CHUNK):
                p = score[h, c:c + CHUNK, :] * inverse
                grad[c:c + CHUNK, lanes] = (p * (dots[h, c:c + CHUNK, :] - delta)).astype(BF16)
            gq_t[head, :] = dot(key_t[head, :], grad[:, lanes], 1, 0) * (1.0 / math.sqrt(HEAD_DIM))
        stage[0, g] = att_t[...].T.astype(BF16)
        stage[1, g] = gq_t[...].T.astype(BF16)
        out_copy(0, g).start()
        out_copy(1, g).start()

        def key_grads(first, n):
            return (
                dot(grad[first:first + n, :], q_stack[...], 1, 0),
                dot(prob[first:first + n, :], do_stack[...], 1, 0),
            )

        for side in range(2):
            dk, dv = key_grads(2 * ROWS * side, ROWS)
            near_send[side, g, 0:ROWS, :] = dk.astype(BF16)
            near_send[side, g, ROWS:2 * ROWS, :] = dv.astype(BF16)
            grad_copy(side, g).start()
        dk, dv = key_grads(ROWS, ROWS)
        own_grad[g, 0:ROWS, :] = dk
        own_grad[g, ROWS:2 * ROWS, :] = dv
        dk, dv = key_grads(NEAR, COARSE)
        for s in range(len(MID)):
            both = jnp.concatenate([dk[s * ONE:(s + 1) * ONE], dv[s * ONE:(s + 1) * ONE]], axis=0)
            mg_send[s, :, cols] = both.astype(BF16)
        for k in range(1, Z):
            first = MID_ROWS + (k - 1) * Y * TWO
            fg_send[k - 1, 0, :, cols] = dk[first:first + Y * TWO].astype(BF16)
            fg_send[k - 1, 1, :, cols] = dv[first:first + Y * TWO].astype(BF16)

        @pl.when(g % part_groups == part_groups - 1)
        def _():
            for k in range(1, Z):
                fg_copy(k, part).start()
            for s in range(len(MID)):
                mg_copy(s, part).start()

        return carry

    lax.fori_loop(0, groups, pair, 0)

    for part in range(parts):
        for k in range(1, Z):
            fg_copy(k, part).wait_recv()
    for which in range(2):
        total = fg_recv[0, which].astype(F32)
        for k in range(2, Z):
            total = total + fg_recv[k - 1, which].astype(F32)
        gathered[which] = total
    yg_copies = [
        remote(yg_send.at[j - 1], yg_recv.at[j - 1], yg_send_sem.at[j - 1], yg_recv_sem.at[j - 1], at_y(-j))
        for j in range(1, Y)
    ]
    for j in range(1, Y):
        yg_send[j - 1] = pack_rows(TWO * j)
        yg_copies[j - 1].start()
    for part in range(parts):
        for s in range(len(MID)):
            mg_copy(s, part).wait_recv()
    middle_sum = mg_recv[0].astype(F32)
    for s in range(1, len(MID)):
        middle_sum = middle_sum + mg_recv[s].astype(F32)
    coarse_sum[...] = jnp.zeros_like(coarse_sum)
    for which in range(2):
        coarse_sum[which, 0:ONE, :] = middle_sum[which * ONE:(which + 1) * ONE]
        coarse_sum[which, ONE:ONE + TWO, :] = gathered[which, 0:TWO, :]
    for j in range(1, Y):
        yg_copies[j - 1].wait_recv()
        pack[...] = yg_recv[j - 1].astype(F32)
        for which in range(2):
            for side in range(2):
                first = TWO * (2 * which + side)
                cols = slice(side * half, (side + 1) * half)
                coarse_sum[which, ONE:ONE + TWO, cols] = (
                    coarse_sum[which, ONE:ONE + TWO, cols] + pack[first:first + TWO, :]
                )

    def finish(g, carry):
        cols = columns(g, PAIR)
        for side in range(2):
            grad_copy(side, g).wait_recv()
        for which in range(2):
            rows = slice(which * ROWS, (which + 1) * ROWS)
            wide = coarse_sum[which, :, cols]
            high = wide.astype(BF16)
            low = (wide - high.astype(F32)).astype(BF16)
            total = own_grad[g, rows, :] + dot(restrict_t[...], high, 1, 0) + dot(restrict_t[...], low, 1, 0)
            total = total + near_recv[0, g, rows, :].astype(F32) + near_recv[1, g, rows, :].astype(F32)
            stage[2 + which, g] = total.astype(BF16)
            out_copy(2 + which, g).start()
        return carry

    lax.fori_loop(0, groups, finish, 0)

    def drain(g, carry):
        for side in range(2):
            for which in range(2):
                near_copy(side, which, g).wait_send()
            grad_copy(side, g).wait_send()
        for which in range(4):
            out_copy(which, g).wait()
        return carry

    lax.fori_loop(0, groups, drain, 0)
    for copy in c1_copies + c2_copies + yg_copies:
        copy.wait_send()
    for part in range(parts):
        for k in range(1, Z):
            z_copy(k, part).wait_send()
            fg_copy(k, part).wait_send()
        for s in range(len(MID)):
            mg_copy(s, part).wait_send()


def per_device(queries, keys, values, cotangent, restrict_one, restrict_two):
    rows, width = queries.shape
    groups = width // PAIR
    parts = 2
    shape = jax.ShapeDtypeStruct((rows, width), BF16)
    hbm = pl.BlockSpec(memory_space=pl.ANY)
    vmem = pl.BlockSpec(memory_space=pltpu.VMEM)
    dma = pltpu.SemaphoreType.DMA
    mid = len(MID)
    scratch = [
        pltpu.VMEM((4, ROWS, width), BF16),
        pltpu.VMEM((2, groups, 2 * ROWS, PAIR), BF16),
        pltpu.VMEM((2, groups, 2 * ROWS, PAIR), BF16),
        pltpu.VMEM((2, groups, 2 * ROWS, PAIR), BF16),
        pltpu.VMEM((groups, 2 * ROWS, PAIR), F32),
        pltpu.VMEM((2, ROWS, width), BF16),
        pltpu.VMEM((16, width), BF16),
        pltpu.VMEM((mid, 16, width), BF16),
        pltpu.VMEM((16, width // 2), BF16),
        pltpu.VMEM((Y - 1, 16, width // 2), BF16),
        pltpu.VMEM((2, 16, width), BF16),
        pltpu.VMEM((mid, 16, width), BF16),
        pltpu.VMEM((mid, 16, width), BF16),
        pltpu.VMEM((Z - 1, 2, 16, width), BF16),
        pltpu.VMEM((Z - 1, 2, 16, width), BF16),
        pltpu.VMEM((Y - 1, 16, width // 2), BF16),
        pltpu.VMEM((Y - 1, 16, width // 2), BF16),
        pltpu.VMEM((16, ROWS), F32),
        pltpu.VMEM((16, width // 2), F32),
        pltpu.VMEM((2, 16, width), F32),
        pltpu.VMEM((COARSE, ROWS), F32),
        pltpu.VMEM((2 * ROWS, PAIR), BF16),
        pltpu.VMEM((2 * ROWS, PAIR), BF16),
        pltpu.VMEM((PAIR, PADDED), BF16),
        pltpu.VMEM((PAIR, PADDED), BF16),
        pltpu.VMEM((PAIR, ROWS), F32),
        pltpu.VMEM((2, KEYS, ROWS), F32),
        pltpu.VMEM((2, KEYS, ROWS), F32),
        pltpu.VMEM((PADDED, 2 * ROWS), BF16),
        pltpu.VMEM((PADDED, 2 * ROWS), BF16),
        pltpu.VMEM((PAIR, ROWS), F32),
        pltpu.VMEM((PAIR, ROWS), F32),
        pltpu.VMEM((4, groups, ROWS, PAIR), BF16),
        pltpu.VMEM((2, 16, width), F32),
        pltpu.VMEM((ROWS, 16), BF16),
        dma((4,)),
        dma((2, 2, groups)), dma((2, 2, groups)),
        dma((2, groups)), dma((2, groups)),
        dma((mid,)), dma((mid,)),
        dma((Y - 1,)), dma((Y - 1,)),
        dma((parts, Z - 1)), dma((parts, Z - 1)),
        dma((parts, mid)), dma((parts, mid)),
        dma((parts, Z - 1)), dma((parts, Z - 1)),
        dma((Y - 1,)), dma((Y - 1,)),
        dma((4, groups)),
    ]
    return pl.pallas_call(
        functools.partial(kernel, groups, parts),
        out_shape=[shape] * 4,
        in_specs=[hbm] * 4 + [vmem] * 2,
        out_specs=[hbm] * 4,
        scratch_shapes=scratch,
        compiler_params=pltpu.CompilerParams(
            collective_id=0, has_side_effects=True, vmem_limit_bytes=56 * 1024 * 1024
        ),
    )(queries, keys, values, cotangent, restrict_one, restrict_two)


def solution(mesh):
    rows = P(("prompt", "seq"), None)
    return jax.shard_map(
        per_device, mesh=mesh, in_specs=(rows, rows, rows, rows, P(), P()),
        out_specs=(rows, rows, rows, rows), check_vma=False,
    )
```

```python
import functools
import math

import jax
import jax.numpy as jnp
from jax import lax
from jax.experimental import pallas as pl
from jax.experimental.pallas import tpu as pltpu
from jax.sharding import PartitionSpec as P

HEAD_DIM = 64
ROWS = 256
PAIR = 128
Y = 4
Z = 8
BLOCKS = Y * Z
ONE = 8
TWO = 4
MID = (-3, -2, 2, 3)
MID_ROWS = len(MID) * ONE
FAR_ROWS = (Z - 1) * Y * TWO
COARSE = MID_ROWS + FAR_ROWS
NEAR = 3 * ROWS
KEYS = NEAR + COARSE
PADDED = 4 * ROWS
CHUNK = 48
MASKED = -1e30
F32 = jnp.float32
BF16 = jnp.bfloat16
MESH = pl.DeviceIdType.MESH


def dot(a, b, ca, cb):
    return lax.dot_general(a, b, (((ca,), (cb,)), ((), ())), preferred_element_type=F32)


def group_max(x):
    return jnp.max(x.reshape(x.shape[0] // 8, 8, x.shape[1]), axis=0)


def group_sum(x):
    return jnp.sum(x.reshape(x.shape[0] // 8, 8, x.shape[1]), axis=0)


def kernel(
    groups, parts,
    q_hbm, k_hbm, v_hbm, do_hbm, r1_ref, r2_ref,
    stage,
    own_in, near_kv, near_send, near_recv, own_grad, coarse,
    c1_send, c1_recv, c2_send, c2_recv, z_send, mg_send, mg_recv, fg_send, fg_recv, yg_send, yg_recv,
    fg_own, restrict, pack, gathered, bias, q_stack, do_stack, key_t, value_t, do_t, score, dots, prob, grad,
    att_t, gq_t, coarse_sum, restrict_t,
    load_sem, near_send_sem, near_recv_sem, grad_send_sem, grad_recv_sem,
    c1_send_sem, c1_recv_sem, c2_send_sem, c2_recv_sem, z_send_sem, z_recv_sem,
    mg_send_sem, mg_recv_sem, fg_send_sem, fg_recv_sem, yg_send_sem, yg_recv_sem,
):
    width = groups * PAIR
    half = width // 2
    part_groups = groups // parts
    part_width = width // parts
    me = lax.axis_index("seq")
    z = me // Y
    y = me % Y
    way = 1 - 2 * (y // 2)

    def at_block(offset):
        return lax.rem(me + offset + BLOCKS, BLOCKS)

    def at_y(offset):
        return z * Y + lax.rem(y + offset + Y, Y)

    def at_z(offset):
        return lax.rem(z + offset + Z, Z) * Y + y

    def remote(src, dst, send_sem, recv_sem, to):
        return pltpu.make_async_remote_copy(
            src_ref=src, dst_ref=dst, send_sem=send_sem, recv_sem=recv_sem,
            device_id={"seq": to}, device_id_type=MESH,
        )

    def columns(index, size):
        return pl.ds(pl.multiple_of(index * size, size), size)

    loads = [
        pltpu.make_async_copy(src, own_in.at[i], load_sem.at[i])
        for i, src in enumerate((k_hbm, v_hbm, q_hbm, do_hbm))
    ]
    for load in loads:
        load.start()

    restrict[...] = jnp.zeros_like(restrict)
    restrict[0:ONE, :] = r1_ref[...].astype(F32)
    restrict[ONE:ONE + TWO, :] = r2_ref[...].astype(F32)
    restrict_b = restrict[...].astype(BF16)
    restrict_t[...] = restrict[...].T.astype(BF16)
    loads[0].wait()
    loads[1].wait()
    coarse_k = dot(restrict_b, own_in[0], 1, 0)
    coarse_v = dot(restrict_b, own_in[1], 1, 0)
    gathered[0] = coarse_k
    gathered[1] = coarse_v

    def pack_rows(first):
        for which in range(2):
            for side in range(2):
                row = TWO * (2 * which + side)
                pack[row:row + TWO, :] = gathered[which, first:first + TWO, side * half:(side + 1) * half]
        return pack[...].astype(BF16)

    c2_send[...] = pack_rows(ONE)
    c1_send[...] = jnp.concatenate([coarse_k[0:ONE], coarse_v[0:ONE]], axis=0).astype(BF16)

    row = lax.broadcasted_iota(jnp.int32, (COARSE, ROWS), 0)
    slot = row >> 3
    offset = jnp.where(slot == 0, -3, jnp.where(slot == 1, -2, jnp.where(slot == 2, 2, 3)))
    place = me + offset
    middle = jnp.where((place >= 0) & (place < BLOCKS), math.log(32.0), MASKED)
    far_row = row - MID_ROWS
    far_z = (z - way * ((far_row >> 4) + 1)) & (Z - 1)
    far_y = (y - ((far_row >> 2) & 3)) & (Y - 1)
    distance = jnp.abs(far_z * Y + far_y - me)
    far = jnp.where(distance >= 4, math.log(64.0), MASKED)
    bias[...] = jnp.where(row < MID_ROWS, middle, far)
    left_bias = jnp.where(me >= 1, 0.0, MASKED).astype(F32)
    right_bias = jnp.where(me < BLOCKS - 1, 0.0, MASKED).astype(F32)
    for which in range(2):
        coarse[which, COARSE:ROWS, :] = jnp.zeros((ROWS - COARSE, width), BF16)
    prob[KEYS:PADDED, :] = jnp.zeros((PADDED - KEYS, 2 * ROWS), BF16)
    grad[KEYS:PADDED, :] = jnp.zeros((PADDED - KEYS, 2 * ROWS), BF16)

    barrier = pltpu.get_barrier_semaphore()
    partners = [at_block(o) for o in (-1, 1) + MID]
    partners += [at_y(j) for j in range(1, Y)] + [at_z(-1), at_z(1)]
    for partner in partners:
        pl.semaphore_signal(barrier, inc=1, device_id={"seq": partner}, device_id_type=MESH)
    pl.semaphore_wait(barrier, len(partners))

    c2_copies = [
        remote(c2_send, c2_recv.at[j - 1], c2_send_sem.at[j - 1], c2_recv_sem.at[j - 1], at_y(j))
        for j in range(1, Y)
    ]
    for copy in c2_copies:
        copy.start()
    c1_copies = [
        remote(c1_send, c1_recv.at[s], c1_send_sem.at[s], c1_recv_sem.at[s], at_block(-o))
        for s, o in enumerate(MID)
    ]
    for copy in c1_copies:
        copy.start()


    def near_copy(side, which, g):
        src = (k_hbm, v_hbm)[which].at[:, columns(g, PAIR)]
        return remote(
            src, near_kv.at[side, g, pl.ds(which * ROWS, ROWS)],
            near_send_sem.at[side, which, g], near_recv_sem.at[side, which, g],
            at_block(1 if side == 0 else -1),
        )

    def send_near(g, carry):
        for side in range(2):
            for which in range(2):
                near_copy(side, which, g).start()
        return carry

    lax.fori_loop(0, groups, send_near, 0)

    for j in range(Y):
        if j == 0:
            block = c2_send[...]
        else:
            c2_copies[j - 1].wait_recv()
            block = c2_recv[j - 1]
        pack[...] = block.astype(F32)
        for which in range(2):
            for side in range(2):
                first = TWO * (2 * which + side)
                gathered[which, TWO * j:TWO * (j + 1), side * half:(side + 1) * half] = pack[first:first + TWO, :]
    z_send[...] = gathered[...].astype(BF16)

    def far_slot(k):
        return pl.ds(MID_ROWS + (k - 1) * Y * TWO, Y * TWO)

    def z_copy(k, part):
        cols = columns(part, part_width)
        src = z_send.at[:, :, cols] if k == 1 else coarse.at[:, far_slot(k - 1), cols]
        return remote(
            src, coarse.at[:, far_slot(k), cols],
            z_send_sem.at[part, k - 1], z_recv_sem.at[part, k - 1], at_z(way),
        )

    for part in range(parts):
        z_copy(1, part).start()

    for copy in c1_copies:
        copy.wait_recv()
    for which in range(2):
        rows = [c1_recv[s].astype(F32)[which * ONE:(which + 1) * ONE] for s in range(len(MID))]
        coarse[which, 0:MID_ROWS, :] = jnp.concatenate(rows, axis=0).astype(BF16)
    loads[2].wait()
    loads[3].wait()
    for k in range(1, Z):
        for part in range(parts):
            z_copy(k, part).wait_recv()
            if k < Z - 1:
                z_copy(k + 1, part).start()

    def grad_copy(side, g):
        return remote(
            near_send.at[side, g], near_recv.at[1 - side, g],
            grad_send_sem.at[side, g], grad_recv_sem.at[1 - side, g],
            at_block(-1 if side == 0 else 1),
        )

    def mg_copy(s, part):
        cols = columns(part, part_width)
        return remote(
            mg_send.at[s, :, cols], mg_recv.at[s, :, cols],
            mg_send_sem.at[part, s], mg_recv_sem.at[part, s], at_block(MID[s]),
        )

    def fg_copy(t, g):
        cols = columns(g, PAIR)
        return remote(
            fg_send.at[t, :, :, cols], fg_recv.at[t, :, :, cols],
            fg_send_sem.at[t, g], fg_recv_sem.at[t, g], at_z(way),
        )

    def ring_step(t, g):
        cols = columns(g, PAIR)
        total = fg_own[t, :, :, cols]
        if t > 0:
            fg_copy(t - 1, g).wait_recv()
            total = total + fg_recv[t - 1, :, :, cols].astype(F32)
        fg_send[t, :, :, cols] = total.astype(BF16)
        fg_copy(t, g).start()

    def ring_steps(turn):
        for t in range(1, Z - 1):
            @pl.when((turn - t >= 0) & (turn - t < groups))
            def _(t=t):
                ring_step(t, turn - t)

    def pair(g, carry):
        cols = columns(g, PAIR)
        part = g // part_groups

        for side in range(2):
            for which in range(2):
                near_copy(side, which, g).wait_recv()

        def key_value(which):
            first = which * ROWS
            return (
                near_kv[0, g, first:first + ROWS, :],
                own_in[which, :, cols],
                near_kv[1, g, first:first + ROWS, :],
                coarse[which, :, cols],
            )

        q = own_in[2, :, cols].astype(F32) * (1.0 / math.sqrt(HEAD_DIM))
        do = own_in[3, :, cols].astype(F32)
        lane = lax.broadcasted_iota(jnp.int32, (ROWS, PAIR), 1)
        for h in range(2):
            mine = (lane >= HEAD_DIM) if h else (lane < HEAD_DIM)
            q_stack[h * ROWS:(h + 1) * ROWS, :] = jnp.where(mine, q, 0.0).astype(BF16)
            do_stack[h * ROWS:(h + 1) * ROWS, :] = jnp.where(mine, do, 0.0).astype(BF16)
        do_t[...] = do.T
        keys = key_value(0)
        values = key_value(1)
        for i in range(4):
            key_t[:, i * ROWS:(i + 1) * ROWS] = keys[i].T
            value_t[:, i * ROWS:(i + 1) * ROWS] = values[i].T
        counts = (ROWS, ROWS, ROWS, COARSE)
        biases = (left_bias, None, right_bias, bias)
        for h in range(2):
            qh = q_stack[h * ROWS:(h + 1) * ROWS, :]
            doh = do_stack[h * ROWS:(h + 1) * ROWS, :]
            lanes = slice(h * ROWS, (h + 1) * ROWS)
            top = None
            for i in range(4):
                n = counts[i]
                s = dot(keys[i][:n], qh, 1, 1)
                if i == 3:
                    s = s + bias[...]
                elif biases[i] is not None:
                    s = s + biases[i]
                score[h, i * ROWS:i * ROWS + n, :] = s
                m = group_max(s)
                top = m if top is None else jnp.maximum(top, m)
                dots[h, i * ROWS:i * ROWS + n, :] = dot(values[i][:n], doh, 1, 1)
            top = jnp.max(top, axis=0, keepdims=True)
            total = jnp.zeros((8, ROWS), F32)
            for c in range(0, KEYS, CHUNK):
                p = jnp.exp(score[h, c:c + CHUNK, :] - top)
                score[h, c:c + CHUNK, :] = p
                total = total + group_sum(p)
            inverse = 1.0 / jnp.sum(total, axis=0, keepdims=True)
            for c in range(0, KEYS, CHUNK):
                p = score[h, c:c + CHUNK, :] * inverse
                prob[c:c + CHUNK, lanes] = p.astype(BF16)
            head = slice(h * HEAD_DIM, (h + 1) * HEAD_DIM)
            att = dot(value_t[head, :], prob[:, lanes], 1, 0).astype(BF16).astype(F32)
            att_t[head, :] = att
            delta = jnp.sum(att * do_t[head, :], axis=0, keepdims=True)
            for c in range(0, KEYS, CHUNK):
                p = score[h, c:c + CHUNK, :] * inverse
                grad[c:c + CHUNK, lanes] = (p * (dots[h, c:c + CHUNK, :] - delta)).astype(BF16)
            gq_t[head, :] = dot(key_t[head, :], grad[:, lanes], 1, 0) * (1.0 / math.sqrt(HEAD_DIM))
        stage[0, g] = att_t[...].T.astype(BF16)
        stage[1, g] = gq_t[...].T.astype(BF16)

        def key_grads(first, n):
            return (
                dot(grad[first:first + n, :], q_stack[...], 1, 0),
                dot(prob[first:first + n, :], do_stack[...], 1, 0),
            )

        for side in range(2):
            dk, dv = key_grads(2 * ROWS * side, ROWS)
            near_send[side, g, 0:ROWS, :] = dk.astype(BF16)
            near_send[side, g, ROWS:2 * ROWS, :] = dv.astype(BF16)
            grad_copy(side, g).start()
        dk, dv = key_grads(ROWS, ROWS)
        own_grad[g, 0:ROWS, :] = dk
        own_grad[g, ROWS:2 * ROWS, :] = dv
        dk, dv = key_grads(NEAR, COARSE)
        for s in range(len(MID)):
            both = jnp.concatenate([dk[s * ONE:(s + 1) * ONE], dv[s * ONE:(s + 1) * ONE]], axis=0)
            mg_send[s, :, cols] = both.astype(BF16)
        for k in range(1, Z):
            first = MID_ROWS + (k - 1) * Y * TWO
            fg_own[k - 1, 0, :, cols] = dk[first:first + Y * TWO]
            fg_own[k - 1, 1, :, cols] = dv[first:first + Y * TWO]
        ring_step(0, g)
        ring_steps(g)

        @pl.when(g % part_groups == part_groups - 1)
        def _():
            for s in range(len(MID)):
                mg_copy(s, part).start()

        return carry

    lax.fori_loop(0, groups, pair, 0)

    def add_near(g):
        for side in range(2):
            grad_copy(side, g).wait_recv()
        own_grad[g] = own_grad[g] + near_recv[0, g].astype(F32) + near_recv[1, g].astype(F32)

    def tail(turn, carry):
        ring_steps(turn)
        add_near(turn - groups)
        return carry

    turns = min(groups, Z - 2)
    lax.fori_loop(groups, groups + turns, tail, 0)
    for turn in range(groups + turns, groups + Z - 2):
        ring_steps(jnp.int32(turn))

    def far_arrival(g, carry):
        fg_copy(Z - 2, g).wait_recv()
        return carry

    lax.fori_loop(0, groups, far_arrival, 0)
    for which in range(2):
        gathered[which] = fg_recv[Z - 2, which].astype(F32)
    yg_copies = [
        remote(yg_send.at[j - 1], yg_recv.at[j - 1], yg_send_sem.at[j - 1], yg_recv_sem.at[j - 1], at_y(-j))
        for j in range(1, Y)
    ]
    for j in range(1, Y):
        yg_send[j - 1] = pack_rows(TWO * j)
        yg_copies[j - 1].start()
    for part in range(parts):
        for s in range(len(MID)):
            mg_copy(s, part).wait_recv()
    middle_sum = mg_recv[0].astype(F32)
    for s in range(1, len(MID)):
        middle_sum = middle_sum + mg_recv[s].astype(F32)
    coarse_sum[...] = jnp.zeros_like(coarse_sum)
    for which in range(2):
        coarse_sum[which, 0:ONE, :] = middle_sum[which * ONE:(which + 1) * ONE]
        coarse_sum[which, ONE:ONE + TWO, :] = gathered[which, 0:TWO, :]
    for j in range(1, Y):
        yg_copies[j - 1].wait_recv()
        pack[...] = yg_recv[j - 1].astype(F32)
        for which in range(2):
            for side in range(2):
                first = TWO * (2 * which + side)
                cols = slice(side * half, (side + 1) * half)
                coarse_sum[which, ONE:ONE + TWO, cols] = (
                    coarse_sum[which, ONE:ONE + TWO, cols] + pack[first:first + TWO, :]
                )

    for g in range(turns, groups):
        add_near(g)

    def finish(g, carry):
        cols = columns(g, PAIR)
        for which in range(2):
            rows = slice(which * ROWS, (which + 1) * ROWS)
            wide = coarse_sum[which, :, cols]
            high = wide.astype(BF16)
            low = (wide - high.astype(F32)).astype(BF16)
            total = own_grad[g, rows, :] + dot(restrict_t[...], high, 1, 0) + dot(restrict_t[...], low, 1, 0)
            stage[2 + which, g] = total.astype(BF16)
        return carry

    lax.fori_loop(0, groups, finish, 0)

    def drain(g, carry):
        for side in range(2):
            for which in range(2):
                near_copy(side, which, g).wait_send()
            grad_copy(side, g).wait_send()
        for t in range(Z - 1):
            fg_copy(t, g).wait_send()
        return carry

    lax.fori_loop(0, groups, drain, 0)
    for copy in c1_copies + c2_copies + yg_copies:
        copy.wait_send()
    for part in range(parts):
        for k in range(1, Z):
            z_copy(k, part).wait_send()
        for s in range(len(MID)):
            mg_copy(s, part).wait_send()


def write_out(groups, stage, att, gq, gk, gv, sem):
    copies = [
        pltpu.make_async_copy(stage.at[i, g], out.at[:, pl.ds(g * PAIR, PAIR)], sem.at[i, g])
        for i, out in enumerate((att, gq, gk, gv))
        for g in range(groups)
    ]
    for copy in copies:
        copy.start()
    for copy in copies:
        copy.wait()


def per_device(queries, keys, values, cotangent, restrict_one, restrict_two):
    rows, width = queries.shape
    groups = width // PAIR
    parts = 2
    shape = jax.ShapeDtypeStruct((rows, width), BF16)
    hbm = pl.BlockSpec(memory_space=pl.ANY)
    vmem = pl.BlockSpec(memory_space=pltpu.VMEM)
    dma = pltpu.SemaphoreType.DMA
    mid = len(MID)
    scratch = [
        pltpu.VMEM((4, ROWS, width), BF16),
        pltpu.VMEM((2, groups, 2 * ROWS, PAIR), BF16),
        pltpu.VMEM((2, groups, 2 * ROWS, PAIR), BF16),
        pltpu.VMEM((2, groups, 2 * ROWS, PAIR), BF16),
        pltpu.VMEM((groups, 2 * ROWS, PAIR), F32),
        pltpu.VMEM((2, ROWS, width), BF16),
        pltpu.VMEM((16, width), BF16),
        pltpu.VMEM((mid, 16, width), BF16),
        pltpu.VMEM((16, width // 2), BF16),
        pltpu.VMEM((Y - 1, 16, width // 2), BF16),
        pltpu.VMEM((2, 16, width), BF16),
        pltpu.VMEM((mid, 16, width), BF16),
        pltpu.VMEM((mid, 16, width), BF16),
        pltpu.VMEM((Z - 1, 2, 16, width), BF16),
        pltpu.VMEM((Z - 1, 2, 16, width), BF16),
        pltpu.VMEM((Y - 1, 16, width // 2), BF16),
        pltpu.VMEM((Y - 1, 16, width // 2), BF16),
        pltpu.VMEM((Z - 1, 2, 16, width), F32),
        pltpu.VMEM((16, ROWS), F32),
        pltpu.VMEM((16, width // 2), F32),
        pltpu.VMEM((2, 16, width), F32),
        pltpu.VMEM((COARSE, ROWS), F32),
        pltpu.VMEM((2 * ROWS, PAIR), BF16),
        pltpu.VMEM((2 * ROWS, PAIR), BF16),
        pltpu.VMEM((PAIR, PADDED), BF16),
        pltpu.VMEM((PAIR, PADDED), BF16),
        pltpu.VMEM((PAIR, ROWS), F32),
        pltpu.VMEM((2, KEYS, ROWS), F32),
        pltpu.VMEM((2, KEYS, ROWS), F32),
        pltpu.VMEM((PADDED, 2 * ROWS), BF16),
        pltpu.VMEM((PADDED, 2 * ROWS), BF16),
        pltpu.VMEM((PAIR, ROWS), F32),
        pltpu.VMEM((PAIR, ROWS), F32),
        pltpu.VMEM((2, 16, width), F32),
        pltpu.VMEM((ROWS, 16), BF16),
        dma((4,)),
        dma((2, 2, groups)), dma((2, 2, groups)),
        dma((2, groups)), dma((2, groups)),
        dma((mid,)), dma((mid,)),
        dma((Y - 1,)), dma((Y - 1,)),
        dma((parts, Z - 1)), dma((parts, Z - 1)),
        dma((parts, mid)), dma((parts, mid)),
        dma((Z - 1, groups)), dma((Z - 1, groups)),
        dma((Y - 1,)), dma((Y - 1,)),
    ]
    stage = pl.pallas_call(
        functools.partial(kernel, groups, parts),
        out_shape=pltpu.VMEM((4, groups, ROWS, PAIR), BF16),
        in_specs=[hbm] * 4 + [vmem] * 2,
        out_specs=vmem,
        scratch_shapes=scratch,
        compiler_params=pltpu.CompilerParams(
            collective_id=0, has_side_effects=True, vmem_limit_bytes=56 * 1024 * 1024
        ),
    )(queries, keys, values, cotangent, restrict_one, restrict_two)
    return pl.pallas_call(
        functools.partial(write_out, groups),
        out_shape=[shape] * 4,
        in_specs=[vmem],
        out_specs=[hbm] * 4,
        scratch_shapes=[dma((4, groups))],
    )(stage)


def solution(mesh):
    rows = P(("prompt", "seq"), None)
    return jax.shard_map(
        per_device, mesh=mesh, in_specs=(rows, rows, rows, rows, P(), P()),
        out_specs=(rows, rows, rows, rows), check_vma=False,
    )
```

```python
import functools
import math

import jax
import jax.numpy as jnp
from jax import lax
from jax.experimental import pallas as pl
from jax.experimental.pallas import tpu as pltpu
from jax.sharding import PartitionSpec as P

HEAD_DIM = 64
ROWS = 256
PAIR = 128
Y = 4
Z = 8
BLOCKS = Y * Z
ONE = 8
TWO = 4
MID = (-3, -2, 2, 3)
FG_STEPS = (3, -1, 3, 2, 1)
Z_STEPS = {1: 1, 2: 2, 3: 3, 4: 1, 5: 2, 6: 3, 7: -1}
MID_ROWS = len(MID) * ONE
FAR_ROWS = (Z - 1) * Y * TWO
COARSE = MID_ROWS + FAR_ROWS
NEAR = 3 * ROWS
KEYS = NEAR + COARSE
PADDED = 4 * ROWS
CHUNK = 48
MASKED = -1e30
F32 = jnp.float32
BF16 = jnp.bfloat16
MESH = pl.DeviceIdType.MESH


def dot(a, b, ca, cb):
    return lax.dot_general(a, b, (((ca,), (cb,)), ((), ())), preferred_element_type=F32)


def group_max(x):
    return jnp.max(x.reshape(x.shape[0] // 8, 8, x.shape[1]), axis=0)


def group_sum(x):
    return jnp.sum(x.reshape(x.shape[0] // 8, 8, x.shape[1]), axis=0)


def kernel(
    groups, parts,
    q_hbm, k_hbm, v_hbm, do_hbm, r1_ref, r2_ref,
    stage,
    own_in, near_kv, near_send, near_recv, own_grad, coarse,
    c1_send, c1_recv, c2_send, c2_recv, z_send, mg_send, mg_recv, fg_send, fg_recv, yg_send, yg_recv,
    fg_own, restrict, pack, gathered, bias, q_stack, do_stack, key_t, value_t, do_t, score, dots, prob, grad,
    att_t, gq_t, coarse_sum, restrict_t,
    load_sem, near_send_sem, near_recv_sem, grad_send_sem, grad_recv_sem,
    c1_send_sem, c1_recv_sem, c2_send_sem, c2_recv_sem, z_send_sem, z_recv_sem,
    mg_send_sem, mg_recv_sem, fg_send_sem, fg_recv_sem, yg_send_sem, yg_recv_sem, go_sem,
):
    width = groups * PAIR
    half = width // 2
    part_groups = groups // parts
    part_width = width // parts
    me = lax.axis_index("seq")
    z = me // Y
    y = me % Y
    way = 1 - 2 * (y // 2)

    def at_block(offset):
        return lax.rem(me + offset + BLOCKS, BLOCKS)

    def at_y(offset):
        return z * Y + lax.rem(y + offset + Y, Y)

    def at_z(offset):
        return lax.rem(z + offset + Z, Z) * Y + y

    def remote(src, dst, send_sem, recv_sem, to):
        return pltpu.make_async_remote_copy(
            src_ref=src, dst_ref=dst, send_sem=send_sem, recv_sem=recv_sem,
            device_id={"seq": to}, device_id_type=MESH,
        )

    def columns(index, size):
        return pl.ds(pl.multiple_of(index * size, size), size)

    loads = [
        pltpu.make_async_copy(src, own_in.at[i], load_sem.at[i])
        for i, src in enumerate((k_hbm, v_hbm, q_hbm, do_hbm))
    ]
    for load in loads:
        load.start()

    barrier = pltpu.get_barrier_semaphore()
    partners = [at_block(o) for o in (-1, 1) + MID]
    partners += [at_y(j) for j in range(1, Y)] + [at_z(k) for k in (-3, -2, -1, 1, 2, 3)]
    for partner in partners:
        pl.semaphore_signal(barrier, inc=1, device_id={"seq": partner}, device_id_type=MESH)
    pl.semaphore_wait(barrier, len(partners))

    def near_copy(side, which, g):
        src = (k_hbm, v_hbm)[which].at[:, columns(g, PAIR)]
        return remote(
            src, near_kv.at[side, g, pl.ds(which * ROWS, ROWS)],
            near_send_sem.at[side, which, g], near_recv_sem.at[side, which, g],
            at_block(1 if side == 0 else -1),
        )

    def send_near(side, g, carry):
        for which in range(2):
            near_copy(side, which, g).start()
        return carry

    for side in range(2):
        send_near(side, 0, 0)

    restrict[...] = jnp.zeros_like(restrict)
    restrict[0:ONE, :] = r1_ref[...].astype(F32)
    restrict[ONE:ONE + TWO, :] = r2_ref[...].astype(F32)
    restrict_b = restrict[...].astype(BF16)
    restrict_t[...] = restrict[...].T.astype(BF16)
    loads[0].wait()
    loads[1].wait()
    coarse_k = dot(restrict_b, own_in[0], 1, 0)
    coarse_v = dot(restrict_b, own_in[1], 1, 0)
    gathered[0] = coarse_k
    gathered[1] = coarse_v

    def pack_rows(first):
        for which in range(2):
            for side in range(2):
                row = TWO * (2 * which + side)
                pack[row:row + TWO, :] = gathered[which, first:first + TWO, side * half:(side + 1) * half]
        return pack[...].astype(BF16)

    c2_send[...] = pack_rows(ONE)
    c1_send[...] = jnp.concatenate([coarse_k[0:ONE], coarse_v[0:ONE]], axis=0).astype(BF16)

    c2_copies = [
        remote(c2_send, c2_recv.at[j - 1], c2_send_sem.at[j - 1], c2_recv_sem.at[j - 1], at_y(j))
        for j in range(1, Y)
    ]
    for copy in c2_copies:
        copy.start()
    c1_copies = [
        remote(c1_send, c1_recv.at[s], c1_send_sem.at[s], c1_recv_sem.at[s], at_block(-o))
        for s, o in enumerate(MID)
    ]
    for copy in c1_copies:
        copy.start()

    wraps = (y == Y - 1, y == 0)
    for side in range(2):
        @pl.when(jnp.logical_not(wraps[side]))
        def _(side=side):
            lax.fori_loop(1, groups, functools.partial(send_near, side), 0)

    row = lax.broadcasted_iota(jnp.int32, (COARSE, ROWS), 0)
    slot = row >> 3
    offset = jnp.where(slot == 0, -3, jnp.where(slot == 1, -2, jnp.where(slot == 2, 2, 3)))
    place = me + offset
    middle = jnp.where((place >= 0) & (place < BLOCKS), math.log(32.0), MASKED)
    far_row = row - MID_ROWS
    far_z = (z - way * ((far_row >> 4) + 1)) & (Z - 1)
    far_y = (y - ((far_row >> 2) & 3)) & (Y - 1)
    distance = jnp.abs(far_z * Y + far_y - me)
    far = jnp.where(distance >= 4, math.log(64.0), MASKED)
    bias[...] = jnp.where(row < MID_ROWS, middle, far)
    left_bias = jnp.where(me >= 1, 0.0, MASKED).astype(F32)
    right_bias = jnp.where(me < BLOCKS - 1, 0.0, MASKED).astype(F32)
    for which in range(2):
        coarse[which, COARSE:ROWS, :] = jnp.zeros((ROWS - COARSE, width), BF16)
    prob[KEYS:PADDED, :] = jnp.zeros((PADDED - KEYS, 2 * ROWS), BF16)
    grad[KEYS:PADDED, :] = jnp.zeros((PADDED - KEYS, 2 * ROWS), BF16)

    for copy in c2_copies + c1_copies:
        copy.wait_recv()
    for side in range(2):
        pl.semaphore_signal(
            go_sem.at[side], inc=1, device_id={"seq": at_block(-1 if side == 0 else 1)}, device_id_type=MESH
        )

    for j in range(Y):
        if j == 0:
            block = c2_send[...]
        else:
            block = c2_recv[j - 1]
        pack[...] = block.astype(F32)
        for which in range(2):
            for side in range(2):
                first = TWO * (2 * which + side)
                gathered[which, TWO * j:TWO * (j + 1), side * half:(side + 1) * half] = pack[first:first + TWO, :]
    z_send[...] = gathered[...].astype(BF16)

    def far_slot(k):
        return pl.ds(MID_ROWS + (k - 1) * Y * TWO, Y * TWO)

    def z_copy(k, part):
        cols = columns(part, part_width)
        src = coarse.at[:, far_slot(3), cols] if k in (4, 5, 6) else z_send.at[:, :, cols]
        return remote(
            src, coarse.at[:, far_slot(k), cols],
            z_send_sem.at[part, k - 1], z_recv_sem.at[part, k - 1], at_z(way * Z_STEPS[k]),
        )

    def z_own(part):
        for k in (3, 2, 1, 7):
            z_copy(k, part).start()

    z_own(0)
    z_own(1)
    for side in range(2):
        @pl.when(wraps[side])
        def _(side=side):
            pl.semaphore_wait(go_sem.at[side], 1)
            lax.fori_loop(1, groups, functools.partial(send_near, side), 0)

    for which in range(2):
        rows = [c1_recv[s].astype(F32)[which * ONE:(which + 1) * ONE] for s in range(len(MID))]
        coarse[which, 0:MID_ROWS, :] = jnp.concatenate(rows, axis=0).astype(BF16)
    loads[2].wait()
    loads[3].wait()
    for part in range(parts):
        z_copy(3, part).wait_recv()
        for k in (6, 5, 4):
            z_copy(k, part).start()
        if part + 2 < parts:
            z_own(part + 2)

    def grad_copy(side, g):
        return remote(
            near_send.at[side, g], near_recv.at[1 - side, g],
            grad_send_sem.at[side, g], grad_recv_sem.at[1 - side, g],
            at_block(-1 if side == 0 else 1),
        )

    def mg_copy(s, part):
        cols = columns(part, part_width)
        return remote(
            mg_send.at[s, :, cols], mg_recv.at[s, :, cols],
            mg_send_sem.at[part, s], mg_recv_sem.at[part, s], at_block(MID[s]),
        )

    def fg_copy(i, g):
        cols = columns(g, PAIR)
        slots = pl.ds(0, 3) if i == 0 else pl.ds(2 + i, 1)
        return remote(
            fg_send.at[slots, :, :, cols], fg_recv.at[slots, :, :, cols],
            fg_send_sem.at[i, g], fg_recv_sem.at[i, g], at_z(way * FG_STEPS[i]),
        )

    def sum_first(g):
        cols = columns(g, PAIR)
        for i, k in enumerate((2, 3, 4, 1)):
            fg_send[i, :, :, cols] = fg_own[k - 1, :, :, cols].astype(BF16)
        for i in range(2):
            fg_copy(i, g).start()

    def sum_second(g):
        cols = columns(g, PAIR)
        fg_copy(0, g).wait_recv()
        for i in range(3):
            total = fg_own[4 + i, :, :, cols] + fg_recv[i, :, :, cols].astype(F32)
            fg_send[4 + i, :, :, cols] = total.astype(BF16)
            fg_copy(2 + i, g).start()

    def pair(g, carry):
        cols = columns(g, PAIR)
        part = g // part_groups

        @pl.when(g % part_groups == 0)
        def _():
            for k in (1, 2, 4, 5, 6, 7):
                z_copy(k, part).wait_recv()

        for side in range(2):
            for which in range(2):
                near_copy(side, which, g).wait_recv()

        def key_value(which):
            first = which * ROWS
            return (
                near_kv[0, g, first:first + ROWS, :],
                own_in[which, :, cols],
                near_kv[1, g, first:first + ROWS, :],
                coarse[which, :, cols],
            )

        q = own_in[2, :, cols].astype(F32) * (1.0 / math.sqrt(HEAD_DIM))
        do = own_in[3, :, cols].astype(F32)
        lane = lax.broadcasted_iota(jnp.int32, (ROWS, PAIR), 1)
        for h in range(2):
            mine = (lane >= HEAD_DIM) if h else (lane < HEAD_DIM)
            q_stack[h * ROWS:(h + 1) * ROWS, :] = jnp.where(mine, q, 0.0).astype(BF16)
            do_stack[h * ROWS:(h + 1) * ROWS, :] = jnp.where(mine, do, 0.0).astype(BF16)
        do_t[...] = do.T
        keys = key_value(0)
        values = key_value(1)
        for i in range(4):
            key_t[:, i * ROWS:(i + 1) * ROWS] = keys[i].T
            value_t[:, i * ROWS:(i + 1) * ROWS] = values[i].T
        counts = (ROWS, ROWS, ROWS, COARSE)
        biases = (left_bias, None, right_bias, bias)
        for h in range(2):
            qh = q_stack[h * ROWS:(h + 1) * ROWS, :]
            doh = do_stack[h * ROWS:(h + 1) * ROWS, :]
            lanes = slice(h * ROWS, (h + 1) * ROWS)
            top = None
            for i in range(4):
                n = counts[i]
                s = dot(keys[i][:n], qh, 1, 1)
                if i == 3:
                    s = s + bias[...]
                elif biases[i] is not None:
                    s = s + biases[i]
                score[h, i * ROWS:i * ROWS + n, :] = s
                m = group_max(s)
                top = m if top is None else jnp.maximum(top, m)
                dots[h, i * ROWS:i * ROWS + n, :] = dot(values[i][:n], doh, 1, 1)
            top = jnp.max(top, axis=0, keepdims=True)
            total = jnp.zeros((8, ROWS), F32)
            for c in range(0, KEYS, CHUNK):
                p = jnp.exp(score[h, c:c + CHUNK, :] - top)
                score[h, c:c + CHUNK, :] = p
                total = total + group_sum(p)
            inverse = 1.0 / jnp.sum(total, axis=0, keepdims=True)
            for c in range(0, KEYS, CHUNK):
                p = score[h, c:c + CHUNK, :] * inverse
                prob[c:c + CHUNK, lanes] = p.astype(BF16)
            head = slice(h * HEAD_DIM, (h + 1) * HEAD_DIM)
            att = dot(value_t[head, :], prob[:, lanes], 1, 0).astype(BF16).astype(F32)
            att_t[head, :] = att
            delta = jnp.sum(att * do_t[head, :], axis=0, keepdims=True)
            for c in range(0, KEYS, CHUNK):
                p = score[h, c:c + CHUNK, :] * inverse
                grad[c:c + CHUNK, lanes] = (p * (dots[h, c:c + CHUNK, :] - delta)).astype(BF16)
            gq_t[head, :] = dot(key_t[head, :], grad[:, lanes], 1, 0) * (1.0 / math.sqrt(HEAD_DIM))
        stage[0, :, cols] = att_t[...].T.astype(BF16)
        stage[1, :, cols] = gq_t[...].T.astype(BF16)

        def key_grads(first, n):
            return (
                dot(grad[first:first + n, :], q_stack[...], 1, 0),
                dot(prob[first:first + n, :], do_stack[...], 1, 0),
            )

        for side in range(2):
            dk, dv = key_grads(2 * ROWS * side, ROWS)
            near_send[side, g, 0:ROWS, :] = dk.astype(BF16)
            near_send[side, g, ROWS:2 * ROWS, :] = dv.astype(BF16)
            grad_copy(side, g).start()
        dk, dv = key_grads(ROWS, ROWS)
        own_grad[g, 0:ROWS, :] = dk
        own_grad[g, ROWS:2 * ROWS, :] = dv
        dk, dv = key_grads(NEAR, COARSE)
        for s in range(len(MID)):
            both = jnp.concatenate([dk[s * ONE:(s + 1) * ONE], dv[s * ONE:(s + 1) * ONE]], axis=0)
            mg_send[s, :, cols] = both.astype(BF16)
        for k in range(1, Z):
            first = MID_ROWS + (k - 1) * Y * TWO
            fg_own[k - 1, 0, :, cols] = dk[first:first + Y * TWO]
            fg_own[k - 1, 1, :, cols] = dv[first:first + Y * TWO]
        sum_first(g)

        @pl.when(g > 0)
        def _():
            sum_second(g - 1)


        @pl.when(g % part_groups == part_groups - 1)
        def _():
            for s in range(len(MID)):
                mg_copy(s, part).start()

        return carry

    lax.fori_loop(0, groups, pair, 0)

    def add_near(g):
        for side in range(2):
            grad_copy(side, g).wait_recv()
        own_grad[g] = own_grad[g] + near_recv[0, g].astype(F32) + near_recv[1, g].astype(F32)

    def far_arrival(g, carry):
        for i in range(1, 5):
            fg_copy(i, g).wait_recv()
        return carry

    sum_second(groups - 1)
    early = groups - 2
    for g in range(early):
        add_near(g)
    lax.fori_loop(0, groups, far_arrival, 0)
    for which in range(2):
        total = fg_recv[3, which].astype(F32)
        for i in range(4, 7):
            total = total + fg_recv[i, which].astype(F32)
        gathered[which] = total
    yg_copies = [
        remote(yg_send.at[j - 1], yg_recv.at[j - 1], yg_send_sem.at[j - 1], yg_recv_sem.at[j - 1], at_y(-j))
        for j in range(1, Y)
    ]
    for j in range(1, Y):
        yg_send[j - 1] = pack_rows(TWO * j)
        yg_copies[j - 1].start()
    for part in range(parts):
        for s in range(len(MID)):
            mg_copy(s, part).wait_recv()
    middle_sum = mg_recv[0].astype(F32)
    for s in range(1, len(MID)):
        middle_sum = middle_sum + mg_recv[s].astype(F32)
    coarse_sum[...] = jnp.zeros_like(coarse_sum)
    for which in range(2):
        coarse_sum[which, 0:ONE, :] = middle_sum[which * ONE:(which + 1) * ONE]
        coarse_sum[which, ONE:ONE + TWO, :] = gathered[which, 0:TWO, :]
    for j in range(1, Y):
        yg_copies[j - 1].wait_recv()
        pack[...] = yg_recv[j - 1].astype(F32)
        for which in range(2):
            for side in range(2):
                first = TWO * (2 * which + side)
                cols = slice(side * half, (side + 1) * half)
                coarse_sum[which, ONE:ONE + TWO, cols] = (
                    coarse_sum[which, ONE:ONE + TWO, cols] + pack[first:first + TWO, :]
                )

    for g in range(early, groups):
        add_near(g)

    def finish(g, carry):
        cols = columns(g, PAIR)
        for which in range(2):
            rows = slice(which * ROWS, (which + 1) * ROWS)
            wide = coarse_sum[which, :, cols]
            high = wide.astype(BF16)
            low = (wide - high.astype(F32)).astype(BF16)
            total = own_grad[g, rows, :] + dot(restrict_t[...], high, 1, 0) + dot(restrict_t[...], low, 1, 0)
            stage[2 + which, :, cols] = total.astype(BF16)
        return carry

    lax.fori_loop(0, groups, finish, 0)

    def drain(g, carry):
        for side in range(2):
            for which in range(2):
                near_copy(side, which, g).wait_send()
            grad_copy(side, g).wait_send()
        for i in range(5):
            fg_copy(i, g).wait_send()
        return carry

    lax.fori_loop(0, groups, drain, 0)
    for side in range(2):
        @pl.when(jnp.logical_not(wraps[side]))
        def _(side=side):
            pl.semaphore_wait(go_sem.at[side], 1)

    for copy in c1_copies + c2_copies + yg_copies:
        copy.wait_send()
    for part in range(parts):
        for k in range(1, Z):
            z_copy(k, part).wait_send()
        for s in range(len(MID)):
            mg_copy(s, part).wait_send()


def write_out(stage, att, gq, gk, gv, sem):
    copies = [
        pltpu.make_async_copy(stage.at[i], out, sem.at[i]) for i, out in enumerate((att, gq, gk, gv))
    ]
    for copy in copies:
        copy.start()
    for copy in copies:
        copy.wait()


def per_device(queries, keys, values, cotangent, restrict_one, restrict_two):
    rows, width = queries.shape
    groups = width // PAIR
    parts = 4 if groups % 4 == 0 else 2
    shape = jax.ShapeDtypeStruct((rows, width), BF16)
    hbm = pl.BlockSpec(memory_space=pl.ANY)
    vmem = pl.BlockSpec(memory_space=pltpu.VMEM)
    dma = pltpu.SemaphoreType.DMA
    mid = len(MID)
    scratch = [
        pltpu.VMEM((4, ROWS, width), BF16),
        pltpu.VMEM((2, groups, 2 * ROWS, PAIR), BF16),
        pltpu.VMEM((2, groups, 2 * ROWS, PAIR), BF16),
        pltpu.VMEM((2, groups, 2 * ROWS, PAIR), BF16),
        pltpu.VMEM((groups, 2 * ROWS, PAIR), F32),
        pltpu.VMEM((2, ROWS, width), BF16),
        pltpu.VMEM((16, width), BF16),
        pltpu.VMEM((mid, 16, width), BF16),
        pltpu.VMEM((16, width // 2), BF16),
        pltpu.VMEM((Y - 1, 16, width // 2), BF16),
        pltpu.VMEM((2, 16, width), BF16),
        pltpu.VMEM((mid, 16, width), BF16),
        pltpu.VMEM((mid, 16, width), BF16),
        pltpu.VMEM((Z - 1, 2, 16, width), BF16),
        pltpu.VMEM((Z - 1, 2, 16, width), BF16),
        pltpu.VMEM((Y - 1, 16, width // 2), BF16),
        pltpu.VMEM((Y - 1, 16, width // 2), BF16),
        pltpu.VMEM((Z - 1, 2, 16, width), F32),
        pltpu.VMEM((16, ROWS), F32),
        pltpu.VMEM((16, width // 2), F32),
        pltpu.VMEM((2, 16, width), F32),
        pltpu.VMEM((COARSE, ROWS), F32),
        pltpu.VMEM((2 * ROWS, PAIR), BF16),
        pltpu.VMEM((2 * ROWS, PAIR), BF16),
        pltpu.VMEM((PAIR, PADDED), BF16),
        pltpu.VMEM((PAIR, PADDED), BF16),
        pltpu.VMEM((PAIR, ROWS), F32),
        pltpu.VMEM((2, KEYS, ROWS), F32),
        pltpu.VMEM((2, KEYS, ROWS), F32),
        pltpu.VMEM((PADDED, 2 * ROWS), BF16),
        pltpu.VMEM((PADDED, 2 * ROWS), BF16),
        pltpu.VMEM((PAIR, ROWS), F32),
        pltpu.VMEM((PAIR, ROWS), F32),
        pltpu.VMEM((2, 16, width), F32),
        pltpu.VMEM((ROWS, 16), BF16),
        dma((4,)),
        dma((2, 2, groups)), dma((2, 2, groups)),
        dma((2, groups)), dma((2, groups)),
        dma((mid,)), dma((mid,)),
        dma((Y - 1,)), dma((Y - 1,)),
        dma((parts, Z - 1)), dma((parts, Z - 1)),
        dma((parts, mid)), dma((parts, mid)),
        dma((5, groups)), dma((5, groups)),
        dma((Y - 1,)), dma((Y - 1,)),
        pltpu.SemaphoreType.REGULAR((2,)),
    ]
    stage = pl.pallas_call(
        functools.partial(kernel, groups, parts),
        out_shape=pltpu.VMEM((4, ROWS, width), BF16),
        in_specs=[hbm] * 4 + [vmem] * 2,
        out_specs=vmem,
        scratch_shapes=scratch,
        compiler_params=pltpu.CompilerParams(
            collective_id=0, has_side_effects=True, vmem_limit_bytes=56 * 1024 * 1024
        ),
    )(queries, keys, values, cotangent, restrict_one, restrict_two)
    return pl.pallas_call(
        write_out,
        out_shape=[shape] * 4,
        in_specs=[vmem],
        out_specs=[hbm] * 4,
        scratch_shapes=[dma((4,))],
    )(stage)


def solution(mesh):
    rows = P(("prompt", "seq"), None)
    return jax.shard_map(
        per_device, mesh=mesh, in_specs=(rows, rows, rows, rows, P(), P()),
        out_specs=(rows, rows, rows, rows), check_vma=False,
    )
```

```python
import functools
import math

import jax
import jax.numpy as jnp
from jax import lax
from jax.experimental import pallas as pl
from jax.experimental.pallas import tpu as pltpu
from jax.sharding import PartitionSpec as P

HEAD_DIM = 64
ROWS = 256
PAIR = 128
Y = 4
Z = 8
BLOCKS = Y * Z
ONE = 8
TWO = 4
MID = (-3, -2, 2, 3)
LAG = 3
FG_STEPS = (3, -1, 3, 2, 1)
Z_STEPS = {1: 1, 2: 2, 3: 3, 4: 1, 5: 2, 6: 3}
MID_ROWS = len(MID) * ONE
FAR_ROWS = (Z - 1) * Y * TWO
COARSE = MID_ROWS + FAR_ROWS
NEAR = 3 * ROWS
KEYS = NEAR + COARSE
PADDED = 4 * ROWS
CHUNK = 48
MASKED = -1e30
F32 = jnp.float32
BF16 = jnp.bfloat16
MESH = pl.DeviceIdType.MESH


def dot(a, b, ca, cb):
    return lax.dot_general(a, b, (((ca,), (cb,)), ((), ())), preferred_element_type=F32)


def group_max(x):
    return jnp.max(x.reshape(x.shape[0] // 8, 8, x.shape[1]), axis=0)


def group_sum(x):
    return jnp.sum(x.reshape(x.shape[0] // 8, 8, x.shape[1]), axis=0)


def kernel(
    groups, parts, z_parts,
    q_hbm, k_hbm, v_hbm, do_hbm, r1_hbm, r2_hbm,
    stage,
    own_in, near_kv, near_send, near_recv, own_grad, coarse,
    c1_send, c1_recv, c2_send, c2_recv, z_send, mg_send, mg_recv, fg_send, fg_recv, yg_send, yg_recv,
    fg_own, r1_in, r2_in, restrict, pack, gathered, bias, q_stack, do_stack, key_t, value_t, do_t, score, dots, prob, grad,
    att_t, gq_t, coarse_sum, restrict_t,
    load_sem, near_send_sem, near_recv_sem, grad_send_sem, grad_recv_sem,
    c1_send_sem, c1_recv_sem, c2_send_sem, c2_recv_sem, z_send_sem, z_recv_sem, z_back_sem,
    mg_send_sem, mg_recv_sem, fg_send_sem, fg_recv_sem, yg_send_sem, yg_recv_sem, go_sem,
):
    width = groups * PAIR
    half = width // 2
    part_groups = groups // parts
    part_width = width // parts
    z_groups = groups // z_parts
    z_width = width // z_parts
    me = lax.axis_index("seq")
    z = me // Y
    y = me % Y
    way = 1 - 2 * (y // 2)

    def at_block(offset):
        return lax.rem(me + offset + BLOCKS, BLOCKS)

    def at_y(offset):
        return z * Y + lax.rem(y + offset + Y, Y)

    def at_z(offset):
        return lax.rem(z + offset + Z, Z) * Y + y

    def remote(src, dst, send_sem, recv_sem, to):
        return pltpu.make_async_remote_copy(
            src_ref=src, dst_ref=dst, send_sem=send_sem, recv_sem=recv_sem,
            device_id={"seq": to}, device_id_type=MESH,
        )

    def columns(index, size):
        return pl.ds(pl.multiple_of(index * size, size), size)

    loads = [
        pltpu.make_async_copy(src, own_in.at[i], load_sem.at[i])
        for i, src in enumerate((k_hbm, v_hbm, q_hbm, do_hbm))
    ]
    loads.append(pltpu.make_async_copy(r1_hbm, r1_in, load_sem.at[4]))
    loads.append(pltpu.make_async_copy(r2_hbm, r2_in, load_sem.at[5]))
    for load in loads:
        load.start()

    barrier = pltpu.get_barrier_semaphore()
    partners = [at_block(o) for o in (-1, 1) + MID]
    partners += [at_y(j) for j in range(1, Y)] + [at_z(k) for k in (-3, -2, -1, 1, 2, 3)]
    for partner in partners:
        pl.semaphore_signal(barrier, inc=1, device_id={"seq": partner}, device_id_type=MESH)
    pl.semaphore_wait(barrier, len(partners))

    def near_copy(side, which, g):
        src = (k_hbm, v_hbm)[which].at[:, columns(g, PAIR)]
        return remote(
            src, near_kv.at[side, g, pl.ds(which * ROWS, ROWS)],
            near_send_sem.at[side, which, g], near_recv_sem.at[side, which, g],
            at_block(1 if side == 0 else -1),
        )

    def send_near(side, g, carry):
        for which in range(2):
            near_copy(side, which, g).start()
        return carry

    for side in range(2):
        send_near(side, 0, 0)

    restrict[...] = jnp.zeros_like(restrict)
    loads[4].wait()
    loads[5].wait()
    restrict[0:ONE, :] = r1_in[...].astype(F32)
    restrict[ONE:ONE + TWO, :] = r2_in[...].astype(F32)
    restrict_b = restrict[...].astype(BF16)
    restrict_t[...] = restrict[...].T.astype(BF16)
    loads[0].wait()
    loads[1].wait()
    coarse_k = dot(restrict_b, own_in[0], 1, 0)
    coarse_v = dot(restrict_b, own_in[1], 1, 0)
    gathered[0] = coarse_k
    gathered[1] = coarse_v

    def pack_rows(first):
        for which in range(2):
            for side in range(2):
                row = TWO * (2 * which + side)
                pack[row:row + TWO, :] = gathered[which, first:first + TWO, side * half:(side + 1) * half]
        return pack[...].astype(BF16)

    c2_send[...] = pack_rows(ONE)
    c1_send[...] = jnp.concatenate([coarse_k[0:ONE], coarse_v[0:ONE]], axis=0).astype(BF16)

    c2_copies = [
        remote(c2_send, c2_recv.at[j - 1], c2_send_sem.at[j - 1], c2_recv_sem.at[j - 1], at_y(j))
        for j in range(1, Y)
    ]
    for copy in c2_copies:
        copy.start()
    c1_copies = [
        remote(c1_send, c1_recv.at[s], c1_send_sem.at[s], c1_recv_sem.at[s], at_block(-o))
        for s, o in enumerate(MID)
    ]
    for copy in c1_copies:
        copy.start()

    wraps = (y == Y - 1, y == 0)
    for side in range(2):
        @pl.when(jnp.logical_not(wraps[side]))
        def _(side=side):
            lax.fori_loop(1, groups, functools.partial(send_near, side), 0)

    row = lax.broadcasted_iota(jnp.int32, (COARSE, ROWS), 0)
    slot = row >> 3
    offset = jnp.where(slot == 0, -3, jnp.where(slot == 1, -2, jnp.where(slot == 2, 2, 3)))
    place = me + offset
    middle = jnp.where((place >= 0) & (place < BLOCKS), math.log(32.0), MASKED)
    far_row = row - MID_ROWS
    far_z = (z - way * ((far_row >> 4) + 1)) & (Z - 1)
    far_y = (y - ((far_row >> 2) & 3)) & (Y - 1)
    distance = jnp.abs(far_z * Y + far_y - me)
    far = jnp.where(distance >= 4, math.log(64.0), MASKED)
    bias[...] = jnp.where(row < MID_ROWS, middle, far)
    left_bias = jnp.where(me >= 1, 0.0, MASKED).astype(F32)
    right_bias = jnp.where(me < BLOCKS - 1, 0.0, MASKED).astype(F32)
    for which in range(2):
        coarse[which, COARSE:ROWS, :] = jnp.zeros((ROWS - COARSE, width), BF16)
    prob[KEYS:PADDED, :] = jnp.zeros((PADDED - KEYS, 2 * ROWS), BF16)
    grad[KEYS:PADDED, :] = jnp.zeros((PADDED - KEYS, 2 * ROWS), BF16)

    for copy in c2_copies + c1_copies:
        copy.wait_recv()
    for side in range(2):
        pl.semaphore_signal(
            go_sem.at[side], inc=1, device_id={"seq": at_block(-1 if side == 0 else 1)}, device_id_type=MESH
        )

    for j in range(Y):
        if j == 0:
            block = c2_send[...]
        else:
            block = c2_recv[j - 1]
        pack[...] = block.astype(F32)
        for which in range(2):
            for side in range(2):
                first = TWO * (2 * which + side)
                gathered[which, TWO * j:TWO * (j + 1), side * half:(side + 1) * half] = pack[first:first + TWO, :]
    z_send[...] = gathered[...].astype(BF16)

    def far_slot(k):
        return pl.ds(MID_ROWS + (k - 1) * Y * TWO, Y * TWO)

    z_back = remote(z_send, coarse.at[:, far_slot(7), :], z_back_sem.at[0], z_back_sem.at[1], at_z(-way))
    z_back.start()

    def z_copy(k, part):
        cols = columns(part, z_width)
        src = coarse.at[:, far_slot(3), cols] if k > 3 else z_send.at[:, :, cols]
        return remote(
            src, coarse.at[:, far_slot(k), cols],
            z_send_sem.at[k - 1, part], z_recv_sem.at[k - 1, part], at_z(way * Z_STEPS[k]),
        )

    def z_own(part):
        for k in (3, 2, 1):
            z_copy(k, part).start()

    def z_forward(part):
        z_copy(3, part).wait_recv()
        for k in (6, 5, 4):
            z_copy(k, part).start()

    z_own(0)
    z_own(1)
    for side in range(2):
        @pl.when(wraps[side])
        def _(side=side):
            pl.semaphore_wait(go_sem.at[side], 1)
            lax.fori_loop(1, groups, functools.partial(send_near, side), 0)

    for which in range(2):
        rows = [c1_recv[s].astype(F32)[which * ONE:(which + 1) * ONE] for s in range(len(MID))]
        coarse[which, 0:MID_ROWS, :] = jnp.concatenate(rows, axis=0).astype(BF16)
    loads[2].wait()
    loads[3].wait()
    for part in range(2):
        z_forward(part)
        if part + 2 < z_parts:
            z_own(part + 2)
    z_back.wait_recv()

    def grad_copy(side, g):
        return remote(
            near_send.at[side, g], near_recv.at[1 - side, g],
            grad_send_sem.at[side, g], grad_recv_sem.at[1 - side, g],
            at_block(-1 if side == 0 else 1),
        )

    def mg_copy(s, part):
        cols = columns(part, part_width)
        return remote(
            mg_send.at[s, :, cols], mg_recv.at[s, :, cols],
            mg_send_sem.at[part, s], mg_recv_sem.at[part, s], at_block(MID[s]),
        )

    def fg_copy(i, g):
        cols = columns(g, PAIR)
        slots = pl.ds(0, 3) if i == 0 else pl.ds(2 + i, 1)
        return remote(
            fg_send.at[slots, :, :, cols], fg_recv.at[slots, :, :, cols],
            fg_send_sem.at[i, g], fg_recv_sem.at[i, g], at_z(way * FG_STEPS[i]),
        )

    def sum_first(g):
        cols = columns(g, PAIR)
        for i, k in enumerate((2, 3, 4, 1)):
            fg_send[i, :, :, cols] = fg_own[k - 1, :, :, cols].astype(BF16)
        for i in range(2):
            fg_copy(i, g).start()

    def sum_second(g):
        cols = columns(g, PAIR)
        fg_copy(0, g).wait_recv()
        for i in range(3):
            total = fg_own[4 + i, :, :, cols] + fg_recv[i, :, :, cols].astype(F32)
            fg_send[4 + i, :, :, cols] = total.astype(BF16)
            fg_copy(2 + i, g).start()

    def pair(g, carry):
        cols = columns(g, PAIR)
        part = g // part_groups

        @pl.when(g % z_groups == 0)
        def _():
            for k in (1, 2, 4, 5, 6):
                z_copy(k, g // z_groups).wait_recv()

        @pl.when(g + 2 < z_parts)
        def _():
            z_forward(g + 2)

        for side in range(2):
            for which in range(2):
                near_copy(side, which, g).wait_recv()

        def key_value(which):
            first = which * ROWS
            return (
                near_kv[0, g, first:first + ROWS, :],
                own_in[which, :, cols],
                near_kv[1, g, first:first + ROWS, :],
                coarse[which, :, cols],
            )

        q = own_in[2, :, cols].astype(F32) * (1.0 / math.sqrt(HEAD_DIM))
        do = own_in[3, :, cols].astype(F32)
        lane = lax.broadcasted_iota(jnp.int32, (ROWS, PAIR), 1)
        for h in range(2):
            mine = (lane >= HEAD_DIM) if h else (lane < HEAD_DIM)
            q_stack[h * ROWS:(h + 1) * ROWS, :] = jnp.where(mine, q, 0.0).astype(BF16)
            do_stack[h * ROWS:(h + 1) * ROWS, :] = jnp.where(mine, do, 0.0).astype(BF16)
        do_t[...] = do.T
        keys = key_value(0)
        values = key_value(1)
        for i in range(4):
            key_t[:, i * ROWS:(i + 1) * ROWS] = keys[i].T
            value_t[:, i * ROWS:(i + 1) * ROWS] = values[i].T
        counts = (ROWS, ROWS, ROWS, COARSE)
        biases = (left_bias, None, right_bias, bias)
        for h in range(2):
            qh = q_stack[h * ROWS:(h + 1) * ROWS, :]
            doh = do_stack[h * ROWS:(h + 1) * ROWS, :]
            lanes = slice(h * ROWS, (h + 1) * ROWS)
            top = None
            for i in range(4):
                n = counts[i]
                s = dot(keys[i][:n], qh, 1, 1)
                if i == 3:
                    s = s + bias[...]
                elif biases[i] is not None:
                    s = s + biases[i]
                score[h, i * ROWS:i * ROWS + n, :] = s
                m = group_max(s)
                top = m if top is None else jnp.maximum(top, m)
                dots[h, i * ROWS:i * ROWS + n, :] = dot(values[i][:n], doh, 1, 1)
            top = jnp.max(top, axis=0, keepdims=True)
            total = jnp.zeros((8, ROWS), F32)
            for c in range(0, KEYS, CHUNK):
                p = jnp.exp(score[h, c:c + CHUNK, :] - top)
                score[h, c:c + CHUNK, :] = p
                total = total + group_sum(p)
            inverse = 1.0 / jnp.sum(total, axis=0, keepdims=True)
            for c in range(0, KEYS, CHUNK):
                p = score[h, c:c + CHUNK, :] * inverse
                prob[c:c + CHUNK, lanes] = p.astype(BF16)
            head = slice(h * HEAD_DIM, (h + 1) * HEAD_DIM)
            att = dot(value_t[head, :], prob[:, lanes], 1, 0).astype(BF16).astype(F32)
            att_t[head, :] = att
            delta = jnp.sum(att * do_t[head, :], axis=0, keepdims=True)
            for c in range(0, KEYS, CHUNK):
                p = score[h, c:c + CHUNK, :] * inverse
                grad[c:c + CHUNK, lanes] = (p * (dots[h, c:c + CHUNK, :] - delta)).astype(BF16)
            gq_t[head, :] = dot(key_t[head, :], grad[:, lanes], 1, 0) * (1.0 / math.sqrt(HEAD_DIM))
        stage[0, :, cols] = att_t[...].T.astype(BF16)
        stage[1, :, cols] = gq_t[...].T.astype(BF16)

        def key_grads(first, n):
            return (
                dot(grad[first:first + n, :], q_stack[...], 1, 0),
                dot(prob[first:first + n, :], do_stack[...], 1, 0),
            )

        dk, dv = key_grads(NEAR, COARSE)
        for s in range(len(MID)):
            both = jnp.concatenate([dk[s * ONE:(s + 1) * ONE], dv[s * ONE:(s + 1) * ONE]], axis=0)
            mg_send[s, :, cols] = both.astype(BF16)
        for k in range(1, Z):
            first = MID_ROWS + (k - 1) * Y * TWO
            fg_own[k - 1, 0, :, cols] = dk[first:first + Y * TWO]
            fg_own[k - 1, 1, :, cols] = dv[first:first + Y * TWO]
        sum_first(g)

        @pl.when(g >= LAG)
        def _():
            sum_second(g - LAG)


        for side in range(2):
            dk, dv = key_grads(2 * ROWS * side, ROWS)
            near_send[side, g, 0:ROWS, :] = dk.astype(BF16)
            near_send[side, g, ROWS:2 * ROWS, :] = dv.astype(BF16)
            grad_copy(side, g).start()
        dk, dv = key_grads(ROWS, ROWS)
        own_grad[g, 0:ROWS, :] = dk
        own_grad[g, ROWS:2 * ROWS, :] = dv
        @pl.when(g % part_groups == part_groups - 1)
        def _():
            for s in range(len(MID)):
                mg_copy(s, part).start()

        return carry

    lax.fori_loop(0, groups, pair, 0)

    def add_near(g):
        for side in range(2):
            grad_copy(side, g).wait_recv()
        own_grad[g] = own_grad[g] + near_recv[0, g].astype(F32) + near_recv[1, g].astype(F32)

    def far_arrival(g, carry):
        for i in range(1, 5):
            fg_copy(i, g).wait_recv()
        return carry

    for g in range(max(groups - LAG, 0), groups):
        sum_second(g)
    lax.fori_loop(0, groups, far_arrival, 0)
    for which in range(2):
        total = fg_recv[3, which].astype(F32)
        for i in range(4, 7):
            total = total + fg_recv[i, which].astype(F32)
        gathered[which] = total
    yg_copies = [
        remote(yg_send.at[j - 1], yg_recv.at[j - 1], yg_send_sem.at[j - 1], yg_recv_sem.at[j - 1], at_y(-j))
        for j in range(1, Y)
    ]
    for j in range(1, Y):
        yg_send[j - 1] = pack_rows(TWO * j)
        yg_copies[j - 1].start()
    early = max(groups - 2, 0)
    for g in range(early):
        add_near(g)
    for part in range(parts):
        for s in range(len(MID)):
            mg_copy(s, part).wait_recv()
    middle_sum = mg_recv[0].astype(F32)
    for s in range(1, len(MID)):
        middle_sum = middle_sum + mg_recv[s].astype(F32)
    coarse_sum[...] = jnp.zeros_like(coarse_sum)
    for which in range(2):
        coarse_sum[which, 0:ONE, :] = middle_sum[which * ONE:(which + 1) * ONE]
        coarse_sum[which, ONE:ONE + TWO, :] = gathered[which, 0:TWO, :]
    for j in range(1, Y):
        yg_copies[j - 1].wait_recv()
        pack[...] = yg_recv[j - 1].astype(F32)
        for which in range(2):
            for side in range(2):
                first = TWO * (2 * which + side)
                cols = slice(side * half, (side + 1) * half)
                coarse_sum[which, ONE:ONE + TWO, cols] = (
                    coarse_sum[which, ONE:ONE + TWO, cols] + pack[first:first + TWO, :]
                )


    for g in range(early, groups):
        add_near(g)

    def finish(g, carry):
        cols = columns(g, PAIR)
        for which in range(2):
            rows = slice(which * ROWS, (which + 1) * ROWS)
            wide = coarse_sum[which, :, cols]
            high = wide.astype(BF16)
            low = (wide - high.astype(F32)).astype(BF16)
            total = own_grad[g, rows, :] + dot(restrict_t[...], high, 1, 0) + dot(restrict_t[...], low, 1, 0)
            stage[2 + which, :, cols] = total.astype(BF16)
        return carry

    lax.fori_loop(0, groups, finish, 0)

    def drain(g, carry):
        for side in range(2):
            for which in range(2):
                near_copy(side, which, g).wait_send()
            grad_copy(side, g).wait_send()
        for i in range(5):
            fg_copy(i, g).wait_send()
        return carry

    lax.fori_loop(0, groups, drain, 0)
    z_back.wait_send()
    for part in range(z_parts):
        for k in range(1, Z - 1):
            z_copy(k, part).wait_send()
    for side in range(2):
        @pl.when(jnp.logical_not(wraps[side]))
        def _(side=side):
            pl.semaphore_wait(go_sem.at[side], 1)

    for copy in c1_copies + c2_copies + yg_copies:
        copy.wait_send()
    for part in range(parts):
        for s in range(len(MID)):
            mg_copy(s, part).wait_send()


def write_out(stage, att, gq, gk, gv, sem):
    copies = [
        pltpu.make_async_copy(stage.at[i], out, sem.at[i]) for i, out in enumerate((att, gq, gk, gv))
    ]
    for copy in copies:
        copy.start()
    for copy in copies:
        copy.wait()


def per_device(queries, keys, values, cotangent, restrict_one, restrict_two):
    rows, width = queries.shape
    groups = width // PAIR
    parts = 2
    z_parts = min(groups, 4)
    shape = jax.ShapeDtypeStruct((rows, width), BF16)
    hbm = pl.BlockSpec(memory_space=pl.ANY)
    vmem = pl.BlockSpec(memory_space=pltpu.VMEM)
    dma = pltpu.SemaphoreType.DMA
    mid = len(MID)
    scratch = [
        pltpu.VMEM((4, ROWS, width), BF16),
        pltpu.VMEM((2, groups, 2 * ROWS, PAIR), BF16),
        pltpu.VMEM((2, groups, 2 * ROWS, PAIR), BF16),
        pltpu.VMEM((2, groups, 2 * ROWS, PAIR), BF16),
        pltpu.VMEM((groups, 2 * ROWS, PAIR), F32),
        pltpu.VMEM((2, ROWS, width), BF16),
        pltpu.VMEM((16, width), BF16),
        pltpu.VMEM((mid, 16, width), BF16),
        pltpu.VMEM((16, width // 2), BF16),
        pltpu.VMEM((Y - 1, 16, width // 2), BF16),
        pltpu.VMEM((2, 16, width), BF16),
        pltpu.VMEM((mid, 16, width), BF16),
        pltpu.VMEM((mid, 16, width), BF16),
        pltpu.VMEM((Z - 1, 2, 16, width), BF16),
        pltpu.VMEM((Z - 1, 2, 16, width), BF16),
        pltpu.VMEM((Y - 1, 16, width // 2), BF16),
        pltpu.VMEM((Y - 1, 16, width // 2), BF16),
        pltpu.VMEM((Z - 1, 2, 16, width), F32),
        pltpu.VMEM((ONE, ROWS), BF16),
        pltpu.VMEM((TWO, ROWS), BF16),
        pltpu.VMEM((16, ROWS), F32),
        pltpu.VMEM((16, width // 2), F32),
        pltpu.VMEM((2, 16, width), F32),
        pltpu.VMEM((COARSE, ROWS), F32),
        pltpu.VMEM((2 * ROWS, PAIR), BF16),
        pltpu.VMEM((2 * ROWS, PAIR), BF16),
        pltpu.VMEM((PAIR, PADDED), BF16),
        pltpu.VMEM((PAIR, PADDED), BF16),
        pltpu.VMEM((PAIR, ROWS), F32),
        pltpu.VMEM((2, KEYS, ROWS), F32),
        pltpu.VMEM((2, KEYS, ROWS), F32),
        pltpu.VMEM((PADDED, 2 * ROWS), BF16),
        pltpu.VMEM((PADDED, 2 * ROWS), BF16),
        pltpu.VMEM((PAIR, ROWS), F32),
        pltpu.VMEM((PAIR, ROWS), F32),
        pltpu.VMEM((2, 16, width), F32),
        pltpu.VMEM((ROWS, 16), BF16),
        dma((6,)),
        dma((2, 2, groups)), dma((2, 2, groups)),
        dma((2, groups)), dma((2, groups)),
        dma((mid,)), dma((mid,)),
        dma((Y - 1,)), dma((Y - 1,)),
        dma((Z - 2, z_parts)), dma((Z - 2, z_parts)), dma((2,)),
        dma((parts, mid)), dma((parts, mid)),
        dma((5, groups)), dma((5, groups)),
        dma((Y - 1,)), dma((Y - 1,)),
        pltpu.SemaphoreType.REGULAR((2,)),
    ]
    stage = pl.pallas_call(
        functools.partial(kernel, groups, parts, z_parts),
        out_shape=pltpu.VMEM((4, ROWS, width), BF16),
        in_specs=[hbm] * 6,
        out_specs=vmem,
        scratch_shapes=scratch,
        compiler_params=pltpu.CompilerParams(
            collective_id=0, has_side_effects=True, vmem_limit_bytes=56 * 1024 * 1024
        ),
    )(queries, keys, values, cotangent, restrict_one, restrict_two)
    return pl.pallas_call(
        write_out,
        out_shape=[shape] * 4,
        in_specs=[vmem],
        out_specs=[hbm] * 4,
        scratch_shapes=[dma((4,))],
    )(stage)


def solution(mesh):
    rows = P(("prompt", "seq"), None)
    return jax.shard_map(
        per_device, mesh=mesh, in_specs=(rows, rows, rows, rows, P(), P()),
        out_specs=(rows, rows, rows, rows), check_vma=False,
    )
```

```python
import functools
import math

import jax
import jax.numpy as jnp
from jax import lax
from jax.experimental import pallas as pl
from jax.experimental.pallas import tpu as pltpu
from jax.sharding import PartitionSpec as P

HEAD_DIM = 64
ROWS = 256
PAIR = 128
Y = 4
Z = 8
BLOCKS = Y * Z
ONE = 8
TWO = 4
MID = (-3, -2, 2, 3)
LAG = 3
LEAD = 4
FG_STEPS = (3, -1, 3, 2, 1)
Z_STEPS = {1: 1, 2: 2, 3: 3, 4: 1, 5: 2, 6: 3}
MID_ROWS = len(MID) * ONE
FAR_ROWS = (Z - 1) * Y * TWO
COARSE = MID_ROWS + FAR_ROWS
NEAR = 3 * ROWS
KEYS = NEAR + COARSE
PADDED = 4 * ROWS
CHUNK = 48
MASKED = -1e30
F32 = jnp.float32
BF16 = jnp.bfloat16
MESH = pl.DeviceIdType.MESH


def dot(a, b, ca, cb):
    return lax.dot_general(a, b, (((ca,), (cb,)), ((), ())), preferred_element_type=F32)


def group_max(x):
    return jnp.max(x.reshape(x.shape[0] // 8, 8, x.shape[1]), axis=0)


def group_sum(x):
    return jnp.sum(x.reshape(x.shape[0] // 8, 8, x.shape[1]), axis=0)


def kernel(
    groups, parts, z_parts,
    q_hbm, k_hbm, v_hbm, do_hbm, r1_hbm, r2_hbm,
    stage,
    own_in, near_kv, near_send, near_recv, own_grad, coarse,
    c1_send, c1_recv, c2_send, c2_recv, z_send, mg_send, mg_recv, fg_send, fg_recv, yg_send, yg_recv,
    fg_own, r1_in, r2_in, restrict, pack, gathered, bias, q_stack, do_stack, key_t, value_t, do_t, score, dots, stats, prob, grad,
    att_t, gq_t, coarse_sum, restrict_t,
    load_sem, near_send_sem, near_recv_sem, grad_send_sem, grad_recv_sem,
    c1_send_sem, c1_recv_sem, c2_send_sem, c2_recv_sem, z_send_sem, z_recv_sem, z_back_sem,
    mg_send_sem, mg_recv_sem, fg_send_sem, fg_recv_sem, yg_send_sem, yg_recv_sem,
):
    width = groups * PAIR
    half = width // 2
    part_groups = groups // parts
    part_width = width // parts
    z_groups = groups // z_parts
    z_width = width // z_parts
    me = lax.axis_index("seq")
    z = me // Y
    y = me % Y
    way = 1 - 2 * (y // 2)

    def at_block(offset):
        return lax.rem(me + offset + BLOCKS, BLOCKS)

    def at_y(offset):
        return z * Y + lax.rem(y + offset + Y, Y)

    def at_z(offset):
        return lax.rem(z + offset + Z, Z) * Y + y

    def remote(src, dst, send_sem, recv_sem, to):
        return pltpu.make_async_remote_copy(
            src_ref=src, dst_ref=dst, send_sem=send_sem, recv_sem=recv_sem,
            device_id={"seq": to}, device_id_type=MESH,
        )

    def columns(index, size):
        return pl.ds(pl.multiple_of(index * size, size), size)

    loads = [
        pltpu.make_async_copy(src, own_in.at[i], load_sem.at[i])
        for i, src in enumerate((k_hbm, v_hbm, q_hbm, do_hbm))
    ]
    loads.append(pltpu.make_async_copy(r1_hbm, r1_in, load_sem.at[4]))
    loads.append(pltpu.make_async_copy(r2_hbm, r2_in, load_sem.at[5]))
    for load in loads:
        load.start()

    barrier = pltpu.get_barrier_semaphore()
    partners = [at_block(o) for o in (-1, 1) + MID]
    partners += [at_y(j) for j in range(1, Y)] + [at_z(k) for k in (-3, -2, -1, 1, 2, 3)]
    for partner in partners:
        pl.semaphore_signal(barrier, inc=1, device_id={"seq": partner}, device_id_type=MESH)
    pl.semaphore_wait(barrier, len(partners))

    def near_copy(side, which, g):
        src = (k_hbm, v_hbm)[which].at[:, columns(g, PAIR)]
        return remote(
            src, near_kv.at[side, g, pl.ds(which * ROWS, ROWS)],
            near_send_sem.at[side, which, g], near_recv_sem.at[side, which, g],
            at_block(1 if side == 0 else -1),
        )

    def send_near(side, g, carry):
        for which in range(2):
            near_copy(side, which, g).start()
        return carry

    for side in range(2):
        send_near(side, 0, 0)

    restrict[...] = jnp.zeros_like(restrict)
    loads[4].wait()
    loads[5].wait()
    restrict[0:ONE, :] = r1_in[...].astype(F32)
    restrict[ONE:ONE + TWO, :] = r2_in[...].astype(F32)
    restrict_b = restrict[...].astype(BF16)
    restrict_t[...] = restrict[...].T.astype(BF16)
    loads[0].wait()
    loads[1].wait()
    coarse_k = dot(restrict_b, own_in[0], 1, 0)
    coarse_v = dot(restrict_b, own_in[1], 1, 0)
    gathered[0] = coarse_k
    gathered[1] = coarse_v

    def pack_rows(first):
        for which in range(2):
            for side in range(2):
                row = TWO * (2 * which + side)
                pack[row:row + TWO, :] = gathered[which, first:first + TWO, side * half:(side + 1) * half]
        return pack[...].astype(BF16)

    c2_send[...] = pack_rows(ONE)
    c1_send[...] = jnp.concatenate([coarse_k[0:ONE], coarse_v[0:ONE]], axis=0).astype(BF16)

    first_y, last_y, relay = y == 0, y == Y - 1, (y == 1) | (y == 2)
    same_z = 2 - y // 2

    def c2_copy(j):
        return remote(c2_send, c2_recv.at[j - 1], c2_send_sem.at[j - 1], c2_recv_sem.at[j - 1], at_y(j))

    def c1_copy(i):
        to, slot = ((at_y(2), 3 - same_z), (at_block(3), 0), (at_block(-3), 3))[i]
        return remote(c1_send, c1_recv.at[slot], c1_send_sem.at[i], c1_recv_sem.at[slot], to)

    def c1_on_z():
        slot = 3 - same_z
        return remote(
            c1_recv.at[same_z], c1_recv.at[slot], c1_send_sem.at[3], c1_recv_sem.at[slot], at_z(way)
        )

    def c2_on_y():
        slot = 2 * (y - 1)
        return remote(c2_recv.at[1], c2_recv.at[slot], c2_send_sem.at[3], c2_recv_sem.at[slot], at_y(2 * y - 3))

    def c1_on_y():
        slot = 3 * (2 - y)
        return remote(
            c1_recv.at[same_z], c1_recv.at[slot], c1_send_sem.at[4], c1_recv_sem.at[slot], at_y(2 * y - 3)
        )

    def small_copies(act):
        act(c2_copy(2))
        act(c1_copy(0))

        @pl.when(jnp.logical_not(first_y))
        def _():
            act(c2_copy(3))
            act(c1_copy(1))

        @pl.when(jnp.logical_not(last_y))
        def _():
            act(c2_copy(1))
            act(c1_copy(2))

    small_copies(lambda copy: copy.start())

    held = (y == 2, y == 1)
    on_z = (last_y, first_y)
    some = min(4, groups)
    for side in range(2):
        send_near(side, 1, 0)

        @pl.when(jnp.logical_not(held[side]))
        def _(side=side):
            lax.fori_loop(2, some, functools.partial(send_near, side), 0)

        @pl.when(jnp.logical_not(held[side] | on_z[side]))
        def _(side=side):
            lax.fori_loop(some, groups, functools.partial(send_near, side), 0)

    def c2_arrival(j):
        remote(c2_send, c2_recv.at[j - 1], c2_send_sem.at[j - 1], c2_recv_sem.at[j - 1], at_y(j)).wait_recv()

    def c1_arrival(slot):
        remote(c1_send, c1_recv.at[slot], c1_send_sem.at[0], c1_recv_sem.at[slot], at_y(2)).wait_recv()

    c2_arrival(2)
    c1_arrival(same_z)

    @pl.when(relay)
    def _():
        c2_on_y().start()
        c1_on_y().start()

    for side in range(2):
        @pl.when(held[side])
        def _(side=side):
            lax.fori_loop(2, groups, functools.partial(send_near, side), 0)

    c1_on_z().start()
    row = lax.broadcasted_iota(jnp.int32, (COARSE, ROWS), 0)
    slot = row >> 3
    offset = jnp.where(slot == 0, -3, jnp.where(slot == 1, -2, jnp.where(slot == 2, 2, 3)))
    place = me + offset
    middle = jnp.where((place >= 0) & (place < BLOCKS), math.log(32.0), MASKED)
    far_row = row - MID_ROWS
    far_z = (z - way * ((far_row >> 4) + 1)) & (Z - 1)
    far_y = (y - ((far_row >> 2) & 3)) & (Y - 1)
    distance = jnp.abs(far_z * Y + far_y - me)
    far = jnp.where(distance >= 4, math.log(64.0), MASKED)
    bias[...] = jnp.where(row < MID_ROWS, middle, far)
    left_bias = jnp.where(me >= 1, 0.0, MASKED).astype(F32)
    right_bias = jnp.where(me < BLOCKS - 1, 0.0, MASKED).astype(F32)
    for which in range(2):
        coarse[which, COARSE:ROWS, :] = jnp.zeros((ROWS - COARSE, width), BF16)
    prob[KEYS:PADDED, :] = jnp.zeros((PADDED - KEYS, 2 * ROWS), BF16)
    grad[KEYS:PADDED, :] = jnp.zeros((PADDED - KEYS, 2 * ROWS), BF16)

    c2_arrival(1)
    c2_arrival(3)

    for j in range(Y):
        if j == 0:
            block = c2_send[...]
        else:
            block = c2_recv[j - 1]
        pack[...] = block.astype(F32)
        for which in range(2):
            for side in range(2):
                first = TWO * (2 * which + side)
                gathered[which, TWO * j:TWO * (j + 1), side * half:(side + 1) * half] = pack[first:first + TWO, :]
    z_send[...] = gathered[...].astype(BF16)

    def far_slot(k):
        return pl.ds(MID_ROWS + (k - 1) * Y * TWO, Y * TWO)

    z_back = remote(z_send, coarse.at[:, far_slot(7), :], z_back_sem.at[0], z_back_sem.at[1], at_z(-way))
    z_back.start()
    for side in range(2):
        @pl.when(on_z[side])
        def _(side=side):
            lax.fori_loop(some, groups, functools.partial(send_near, side), 0)

    def z_copy(k, part):
        cols = columns(part, z_width)
        src = coarse.at[:, far_slot(3), cols] if k > 3 else z_send.at[:, :, cols]
        return remote(
            src, coarse.at[:, far_slot(k), cols],
            z_send_sem.at[k - 1, part], z_recv_sem.at[k - 1, part], at_z(way * Z_STEPS[k]),
        )

    def z_own(part):
        for k in (3, 2, 1):
            z_copy(k, part).start()

    def z_forward(part):
        z_copy(3, part).wait_recv()
        for k in (6, 5, 4):
            z_copy(k, part).start()

    z_own(0)
    z_own(1)
    for slot in (0, 3, 3 - same_z):
        c1_arrival(slot)
    for which in range(2):
        rows = [c1_recv[s].astype(F32)[which * ONE:(which + 1) * ONE] for s in range(len(MID))]
        coarse[which, 0:MID_ROWS, :] = jnp.concatenate(rows, axis=0).astype(BF16)
    loads[2].wait()
    loads[3].wait()
    def grad_copy(side, g):
        return remote(
            near_send.at[side, g], near_recv.at[1 - side, g],
            grad_send_sem.at[side, g], grad_recv_sem.at[1 - side, g],
            at_block(-1 if side == 0 else 1),
        )

    def mg_copy(s, part):
        cols = columns(part, part_width)
        return remote(
            mg_send.at[s, :, cols], mg_recv.at[s, :, cols],
            mg_send_sem.at[part, s], mg_recv_sem.at[part, s], at_block(MID[s]),
        )

    def fg_copy(i, g):
        cols = columns(g, PAIR)
        slots = pl.ds(0, 3) if i == 0 else pl.ds(2 + i, 1)
        return remote(
            fg_send.at[slots, :, :, cols], fg_recv.at[slots, :, :, cols],
            fg_send_sem.at[i, g], fg_recv_sem.at[i, g], at_z(way * FG_STEPS[i]),
        )

    def sum_first(g):
        cols = columns(g, PAIR)
        for i, k in enumerate((2, 3, 4, 1)):
            fg_send[i, :, :, cols] = fg_own[k - 1, :, :, cols].astype(BF16)
        for i in range(2):
            fg_copy(i, g).start()

    def sum_second(g):
        cols = columns(g, PAIR)
        fg_copy(0, g).wait_recv()
        for i in range(3):
            total = fg_own[4 + i, :, :, cols] + fg_recv[i, :, :, cols].astype(F32)
            fg_send[4 + i, :, :, cols] = total.astype(BF16)
            fg_copy(2 + i, g).start()

    def heads(g):
        cols = columns(g, PAIR)
        return lax.rem(g, LEAD), cols, own_in[2, :, cols], own_in[3, :, cols]

    def near_part(g):
        slot, cols, q, do = heads(g)
        for side in range(2):
            for which in range(2):
                near_copy(side, which, g).wait_recv()
        q = q.astype(F32) * (1.0 / math.sqrt(HEAD_DIM))
        do = do.astype(F32)
        lane = lax.broadcasted_iota(jnp.int32, (ROWS, PAIR), 1)
        for h in range(2):
            mine = (lane >= HEAD_DIM) if h else (lane < HEAD_DIM)
            q_stack[slot, h * ROWS:(h + 1) * ROWS, :] = jnp.where(mine, q, 0.0).astype(BF16)
            do_stack[slot, h * ROWS:(h + 1) * ROWS, :] = jnp.where(mine, do, 0.0).astype(BF16)
        do_t[slot] = do.T
        keys, values = (
            (
                near_kv[0, g, which * ROWS:(which + 1) * ROWS, :],
                own_in[which, :, cols],
                near_kv[1, g, which * ROWS:(which + 1) * ROWS, :],
            )
            for which in range(2)
        )
        for i in range(3):
            key_t[slot, :, i * ROWS:(i + 1) * ROWS] = keys[i].T
            value_t[slot, :, i * ROWS:(i + 1) * ROWS] = values[i].T
        biases = (left_bias, None, right_bias)
        for h in range(2):
            qh = q_stack[slot, h * ROWS:(h + 1) * ROWS, :]
            doh = do_stack[slot, h * ROWS:(h + 1) * ROWS, :]
            top = None
            for i in range(3):
                s = dot(keys[i], qh, 1, 1)
                if biases[i] is not None:
                    s = s + biases[i]
                score[slot, h, i * ROWS:(i + 1) * ROWS, :] = s
                m = group_max(s)
                top = m if top is None else jnp.maximum(top, m)
                dots[slot, h, i * ROWS:(i + 1) * ROWS, :] = dot(values[i], doh, 1, 1)
            top = jnp.max(top, axis=0, keepdims=True)
            total = jnp.zeros((8, ROWS), F32)
            for c in range(0, NEAR, CHUNK):
                p = jnp.exp(score[slot, h, c:c + CHUNK, :] - top)
                score[slot, h, c:c + CHUNK, :] = p
                total = total + group_sum(p)
            stats[slot, h, 0] = jnp.broadcast_to(top, (8, ROWS))
            stats[slot, h, 1] = total

    def pair(g):
        slot, cols, _, _ = heads(g)
        part = g // part_groups

        @pl.when(g == 0)
        def _():
            z_back.wait_recv()

        @pl.when(g % z_groups == 0)
        def _():
            for k in (1, 2, 4, 5, 6):
                z_copy(k, g // z_groups).wait_recv()

        @pl.when(g + 2 < z_parts)
        def _():
            z_forward(g + 2)

        key = coarse[0, :, cols]
        value = coarse[1, :, cols]
        key_t[slot, :, NEAR:PADDED] = key.T
        value_t[slot, :, NEAR:PADDED] = value.T
        for h in range(2):
            qh = q_stack[slot, h * ROWS:(h + 1) * ROWS, :]
            doh = do_stack[slot, h * ROWS:(h + 1) * ROWS, :]
            lanes = slice(h * ROWS, (h + 1) * ROWS)
            s = dot(key[:COARSE], qh, 1, 1) + bias[...]
            dots[slot, h, NEAR:KEYS, :] = dot(value[:COARSE], doh, 1, 1)
            near_top = stats[slot, h, 0, 0:1, :]
            top = jnp.maximum(near_top, jnp.max(group_max(s), axis=0, keepdims=True))
            p = jnp.exp(s - top)
            score[slot, h, NEAR:KEYS, :] = p
            shrink = jnp.exp(near_top - top)
            total = shrink * jnp.sum(stats[slot, h, 1], axis=0, keepdims=True)
            inverse = 1.0 / (total + jnp.sum(group_sum(p), axis=0, keepdims=True))
            near_inverse = shrink * inverse
            for c in range(0, KEYS, CHUNK):
                p = score[slot, h, c:c + CHUNK, :] * (near_inverse if c < NEAR else inverse)
                prob[c:c + CHUNK, lanes] = p.astype(BF16)
            head = slice(h * HEAD_DIM, (h + 1) * HEAD_DIM)
            att = dot(value_t[slot, head, :], prob[:, lanes], 1, 0).astype(BF16).astype(F32)
            att_t[head, :] = att
            delta = jnp.sum(att * do_t[slot, head, :], axis=0, keepdims=True)
            for c in range(0, KEYS, CHUNK):
                p = score[slot, h, c:c + CHUNK, :] * (near_inverse if c < NEAR else inverse)
                grad[c:c + CHUNK, lanes] = (p * (dots[slot, h, c:c + CHUNK, :] - delta)).astype(BF16)
            gq_t[head, :] = dot(key_t[slot, head, :], grad[:, lanes], 1, 0) * (1.0 / math.sqrt(HEAD_DIM))
        stage[0, :, cols] = att_t[...].T.astype(BF16)
        stage[1, :, cols] = gq_t[...].T.astype(BF16)

        def key_grads(first, n):
            return (
                dot(grad[first:first + n, :], q_stack[slot], 1, 0),
                dot(prob[first:first + n, :], do_stack[slot], 1, 0),
            )

        dk, dv = key_grads(NEAR, COARSE)
        for s in range(len(MID)):
            both = jnp.concatenate([dk[s * ONE:(s + 1) * ONE], dv[s * ONE:(s + 1) * ONE]], axis=0)
            mg_send[s, :, cols] = both.astype(BF16)
        for k in range(1, Z):
            first = MID_ROWS + (k - 1) * Y * TWO
            fg_own[k - 1, 0, :, cols] = dk[first:first + Y * TWO]
            fg_own[k - 1, 1, :, cols] = dv[first:first + Y * TWO]
        sum_first(g)

        @pl.when(g >= LAG)
        def _():
            sum_second(g - LAG)


        @pl.when(g % part_groups == part_groups - 1)
        def _():
            for s in range(len(MID)):
                mg_copy(s, part).start()

        for side in range(2):
            dk, dv = key_grads(2 * ROWS * side, ROWS)
            near_send[side, g, 0:ROWS, :] = dk.astype(BF16)
            near_send[side, g, ROWS:2 * ROWS, :] = dv.astype(BF16)
            grad_copy(side, g).start()
        dk, dv = key_grads(ROWS, ROWS)
        own_grad[g, 0:ROWS, :] = dk
        own_grad[g, ROWS:2 * ROWS, :] = dv
    lead = min(LEAD, groups)

    def turn(t, carry):
        @pl.when(t >= lead)
        def _():
            pair(t - lead)

        @pl.when(t < groups)
        def _():
            near_part(t)

        for part in range(2):
            @pl.when(t == min(part + 1, lead - 1))
            def _(part=part):
                z_forward(part)
                if part + 2 < z_parts:
                    z_own(part + 2)

        return carry

    lax.fori_loop(0, groups + lead, turn, 0)

    def add_near(g):
        for side in range(2):
            grad_copy(side, g).wait_recv()
        own_grad[g] = own_grad[g] + near_recv[0, g].astype(F32) + near_recv[1, g].astype(F32)

    def far_arrival(g, carry):
        for i in range(1, 5):
            fg_copy(i, g).wait_recv()
        return carry

    for g in range(max(groups - LAG, 0), groups):
        sum_second(g)
    lax.fori_loop(0, groups, far_arrival, 0)
    for which in range(2):
        total = fg_recv[3, which].astype(F32)
        for i in range(4, 7):
            total = total + fg_recv[i, which].astype(F32)
        gathered[which] = total
    yg_copies = [
        remote(yg_send.at[j - 1], yg_recv.at[j - 1], yg_send_sem.at[j - 1], yg_recv_sem.at[j - 1], at_y(-j))
        for j in range(1, Y)
    ]
    for j in range(1, Y):
        yg_send[j - 1] = pack_rows(TWO * j)
        yg_copies[j - 1].start()
    early = max(groups - 2, 0)
    for g in range(early):
        add_near(g)
    for part in range(parts):
        for s in range(len(MID)):
            mg_copy(s, part).wait_recv()
    middle_sum = mg_recv[0].astype(F32)
    for s in range(1, len(MID)):
        middle_sum = middle_sum + mg_recv[s].astype(F32)
    coarse_sum[...] = jnp.zeros_like(coarse_sum)
    for which in range(2):
        coarse_sum[which, 0:ONE, :] = middle_sum[which * ONE:(which + 1) * ONE]
        coarse_sum[which, ONE:ONE + TWO, :] = gathered[which, 0:TWO, :]
    for j in range(1, Y):
        yg_copies[j - 1].wait_recv()
        pack[...] = yg_recv[j - 1].astype(F32)
        for which in range(2):
            for side in range(2):
                first = TWO * (2 * which + side)
                cols = slice(side * half, (side + 1) * half)
                coarse_sum[which, ONE:ONE + TWO, cols] = (
                    coarse_sum[which, ONE:ONE + TWO, cols] + pack[first:first + TWO, :]
                )


    for g in range(early, groups):
        add_near(g)

    def finish(g, carry):
        cols = columns(g, PAIR)
        for which in range(2):
            rows = slice(which * ROWS, (which + 1) * ROWS)
            wide = coarse_sum[which, :, cols]
            high = wide.astype(BF16)
            low = (wide - high.astype(F32)).astype(BF16)
            total = own_grad[g, rows, :] + dot(restrict_t[...], high, 1, 0) + dot(restrict_t[...], low, 1, 0)
            stage[2 + which, :, cols] = total.astype(BF16)
        return carry

    lax.fori_loop(0, groups, finish, 0)

    def drain(g, carry):
        for side in range(2):
            for which in range(2):
                near_copy(side, which, g).wait_send()
            grad_copy(side, g).wait_send()
        for i in range(5):
            fg_copy(i, g).wait_send()
        return carry

    lax.fori_loop(0, groups, drain, 0)
    z_back.wait_send()
    for part in range(z_parts):
        for k in range(1, Z - 1):
            z_copy(k, part).wait_send()
    for copy in yg_copies:
        copy.wait_send()
    small_copies(lambda copy: copy.wait_send())
    c1_on_z().wait_send()

    @pl.when(relay)
    def _():
        c2_on_y().wait_send()
        c1_on_y().wait_send()

    for part in range(parts):
        for s in range(len(MID)):
            mg_copy(s, part).wait_send()


def per_device(queries, keys, values, cotangent, restrict_one, restrict_two):
    rows, width = queries.shape
    groups = width // PAIR
    parts = 2
    z_parts = min(groups, 4)
    hbm = pl.BlockSpec(memory_space=pl.ANY)
    vmem = pl.BlockSpec(memory_space=pltpu.VMEM)
    dma = pltpu.SemaphoreType.DMA
    mid = len(MID)
    scratch = [
        pltpu.VMEM((4, ROWS, width), BF16),
        pltpu.VMEM((2, groups, 2 * ROWS, PAIR), BF16),
        pltpu.VMEM((2, groups, 2 * ROWS, PAIR), BF16),
        pltpu.VMEM((2, groups, 2 * ROWS, PAIR), BF16),
        pltpu.VMEM((groups, 2 * ROWS, PAIR), F32),
        pltpu.VMEM((2, ROWS, width), BF16),
        pltpu.VMEM((16, width), BF16),
        pltpu.VMEM((mid, 16, width), BF16),
        pltpu.VMEM((16, width // 2), BF16),
        pltpu.VMEM((Y - 1, 16, width // 2), BF16),
        pltpu.VMEM((2, 16, width), BF16),
        pltpu.VMEM((mid, 16, width), BF16),
        pltpu.VMEM((mid, 16, width), BF16),
        pltpu.VMEM((Z - 1, 2, 16, width), BF16),
        pltpu.VMEM((Z - 1, 2, 16, width), BF16),
        pltpu.VMEM((Y - 1, 16, width // 2), BF16),
        pltpu.VMEM((Y - 1, 16, width // 2), BF16),
        pltpu.VMEM((Z - 1, 2, 16, width), F32),
        pltpu.VMEM((ONE, ROWS), BF16),
        pltpu.VMEM((TWO, ROWS), BF16),
        pltpu.VMEM((16, ROWS), F32),
        pltpu.VMEM((16, width // 2), F32),
        pltpu.VMEM((2, 16, width), F32),
        pltpu.VMEM((COARSE, ROWS), F32),
        pltpu.VMEM((LEAD, 2 * ROWS, PAIR), BF16),
        pltpu.VMEM((LEAD, 2 * ROWS, PAIR), BF16),
        pltpu.VMEM((LEAD, PAIR, PADDED), BF16),
        pltpu.VMEM((LEAD, PAIR, PADDED), BF16),
        pltpu.VMEM((LEAD, PAIR, ROWS), F32),
        pltpu.VMEM((LEAD, 2, KEYS, ROWS), F32),
        pltpu.VMEM((LEAD, 2, KEYS, ROWS), F32),
        pltpu.VMEM((LEAD, 2, 2, 8, ROWS), F32),
        pltpu.VMEM((PADDED, 2 * ROWS), BF16),
        pltpu.VMEM((PADDED, 2 * ROWS), BF16),
        pltpu.VMEM((PAIR, ROWS), F32),
        pltpu.VMEM((PAIR, ROWS), F32),
        pltpu.VMEM((2, 16, width), F32),
        pltpu.VMEM((ROWS, 16), BF16),
        dma((6,)),
        dma((2, 2, groups)), dma((2, 2, groups)),
        dma((2, groups)), dma((2, groups)),
        dma((5,)), dma((mid,)),
        dma((4,)), dma((Y - 1,)),
        dma((Z - 2, z_parts)), dma((Z - 2, z_parts)), dma((2,)),
        dma((parts, mid)), dma((parts, mid)),
        dma((5, groups)), dma((5, groups)),
        dma((Y - 1,)), dma((Y - 1,)),
    ]
    stage = pl.pallas_call(
        functools.partial(kernel, groups, parts, z_parts),
        out_shape=pltpu.VMEM((4, ROWS, width), BF16),
        in_specs=[hbm] * 6,
        out_specs=vmem,
        scratch_shapes=scratch,
        compiler_params=pltpu.CompilerParams(
            collective_id=0, has_side_effects=True, vmem_limit_bytes=56 * 1024 * 1024
        ),
    )(queries, keys, values, cotangent, restrict_one, restrict_two)
    return tuple(stage[i] for i in range(4))


def solution(mesh):
    rows = P(("prompt", "seq"), None)
    return jax.shard_map(
        per_device, mesh=mesh, in_specs=(rows, rows, rows, rows, P(), P()),
        out_specs=(rows, rows, rows, rows), check_vma=False,
    )
```

```python
import functools
import math

import jax
import jax.numpy as jnp
from jax import lax
from jax.experimental import pallas as pl
from jax.experimental.pallas import tpu as pltpu
from jax.sharding import PartitionSpec as P

HEAD_DIM = 64
ROWS = 256
PAIR = 128
Y = 4
Z = 8
BLOCKS = Y * Z
ONE = 8
TWO = 4
MID = (-3, -2, 2, 3)
LAG = 3
LEAD = 5
FG_STEPS = (3, -1, 3, 2, 1)
Z_STEPS = {1: 1, 2: 2, 3: 3, 4: 1, 5: 2, 6: 3}
MID_ROWS = len(MID) * ONE
FAR_ROWS = (Z - 1) * Y * TWO
COARSE = MID_ROWS + FAR_ROWS
NEAR = 3 * ROWS
KEYS = NEAR + COARSE
PADDED = 4 * ROWS
CHUNK = 48
MASKED = -1e30
F32 = jnp.float32
BF16 = jnp.bfloat16
MESH = pl.DeviceIdType.MESH


def dot(a, b, ca, cb):
    return lax.dot_general(a, b, (((ca,), (cb,)), ((), ())), preferred_element_type=F32)


def group_max(x):
    return jnp.max(x.reshape(x.shape[0] // 8, 8, x.shape[1]), axis=0)


def group_sum(x):
    return jnp.sum(x.reshape(x.shape[0] // 8, 8, x.shape[1]), axis=0)


def kernel(
    groups, parts, z_parts,
    q_hbm, k_hbm, v_hbm, do_hbm, r1_hbm, r2_hbm,
    stage,
    own_in, near_kv, near_send, near_recv, own_grad, coarse,
    c1_send, c1_recv, c2_send, c2_recv, z_send, mg_send, mg_recv, fg_send, fg_recv, yg_send, yg_recv,
    fg_own, r1_in, r2_in, restrict, pack, gathered, bias, q_stack, do_stack, key_t, value_t, do_t, score, dots, stats, prob, grad,
    att_t, gq_t, coarse_sum, restrict_t,
    load_sem, near_send_sem, near_recv_sem, grad_send_sem, grad_recv_sem,
    c1_send_sem, c1_recv_sem, c2_send_sem, c2_recv_sem, z_send_sem, z_recv_sem, z_back_sem,
    mg_send_sem, mg_recv_sem, fg_send_sem, fg_recv_sem, yg_send_sem, yg_recv_sem,
):
    width = groups * PAIR
    half = width // 2
    part_groups = groups // parts
    part_width = width // parts
    z_groups = groups // z_parts
    z_width = width // z_parts
    me = lax.axis_index("seq")
    z = me // Y
    y = me % Y
    way = 1 - 2 * (y // 2)

    def at_block(offset):
        return lax.rem(me + offset + BLOCKS, BLOCKS)

    def at_y(offset):
        return z * Y + lax.rem(y + offset + Y, Y)

    def at_z(offset):
        return lax.rem(z + offset + Z, Z) * Y + y

    def remote(src, dst, send_sem, recv_sem, to):
        return pltpu.make_async_remote_copy(
            src_ref=src, dst_ref=dst, send_sem=send_sem, recv_sem=recv_sem,
            device_id={"seq": to}, device_id_type=MESH,
        )

    def columns(index, size):
        return pl.ds(pl.multiple_of(index * size, size), size)

    loads = [
        pltpu.make_async_copy(src, own_in.at[i], load_sem.at[i])
        for i, src in enumerate((k_hbm, v_hbm, q_hbm, do_hbm))
    ]
    loads.append(pltpu.make_async_copy(r1_hbm, r1_in, load_sem.at[4]))
    loads.append(pltpu.make_async_copy(r2_hbm, r2_in, load_sem.at[5]))
    for load in loads:
        load.start()

    barrier = pltpu.get_barrier_semaphore()
    partners = [at_block(o) for o in (-1, 1) + MID]
    partners += [at_y(j) for j in range(1, Y)] + [at_z(k) for k in (-3, -2, -1, 1, 2, 3)]
    for partner in partners:
        pl.semaphore_signal(barrier, inc=1, device_id={"seq": partner}, device_id_type=MESH)
    pl.semaphore_wait(barrier, len(partners))

    def near_copy(side, which, g):
        src = (k_hbm, v_hbm)[which].at[:, columns(g, PAIR)]
        return remote(
            src, near_kv.at[side, g, pl.ds(which * ROWS, ROWS)],
            near_send_sem.at[side, which, g], near_recv_sem.at[side, which, g],
            at_block(1 if side == 0 else -1),
        )

    def send_near(side, g, carry):
        for which in range(2):
            near_copy(side, which, g).start()
        return carry

    for side in range(2):
        send_near(side, 0, 0)

    restrict[...] = jnp.zeros_like(restrict)
    loads[4].wait()
    loads[5].wait()
    restrict[0:ONE, :] = r1_in[...].astype(F32)
    restrict[ONE:ONE + TWO, :] = r2_in[...].astype(F32)
    restrict_b = restrict[...].astype(BF16)
    restrict_t[...] = jnp.concatenate([restrict[...], restrict[...]], axis=0).T.astype(BF16)
    loads[0].wait()
    loads[1].wait()
    coarse_k = dot(restrict_b, own_in[0], 1, 0)
    coarse_v = dot(restrict_b, own_in[1], 1, 0)
    gathered[0] = coarse_k
    gathered[1] = coarse_v

    def pack_rows(first):
        for which in range(2):
            for side in range(2):
                row = TWO * (2 * which + side)
                pack[row:row + TWO, :] = gathered[which, first:first + TWO, side * half:(side + 1) * half]
        return pack[...].astype(BF16)

    c2_send[...] = pack_rows(ONE)
    c1_send[...] = jnp.concatenate([coarse_k[0:ONE], coarse_v[0:ONE]], axis=0).astype(BF16)

    first_y, last_y, relay = y == 0, y == Y - 1, (y == 1) | (y == 2)
    same_z = 2 - y // 2

    def c2_copy(j):
        return remote(c2_send, c2_recv.at[j - 1], c2_send_sem.at[j - 1], c2_recv_sem.at[j - 1], at_y(j))

    def c1_copy(i):
        to, slot = ((at_y(2), 3 - same_z), (at_block(3), 0), (at_block(-3), 3))[i]
        return remote(c1_send, c1_recv.at[slot], c1_send_sem.at[i], c1_recv_sem.at[slot], to)

    def c1_on_z():
        slot = 3 - same_z
        return remote(
            c1_recv.at[same_z], c1_recv.at[slot], c1_send_sem.at[3], c1_recv_sem.at[slot], at_z(way)
        )

    def c2_on_y():
        slot = 2 * (y - 1)
        return remote(c2_recv.at[1], c2_recv.at[slot], c2_send_sem.at[3], c2_recv_sem.at[slot], at_y(2 * y - 3))

    def c1_on_y():
        slot = 3 * (2 - y)
        return remote(
            c1_recv.at[same_z], c1_recv.at[slot], c1_send_sem.at[4], c1_recv_sem.at[slot], at_y(2 * y - 3)
        )

    def small_copies(act):
        act(c2_copy(2))
        act(c1_copy(0))

        @pl.when(jnp.logical_not(first_y))
        def _():
            act(c2_copy(3))
            act(c1_copy(1))

        @pl.when(jnp.logical_not(last_y))
        def _():
            act(c2_copy(1))
            act(c1_copy(2))

    small_copies(lambda copy: copy.start())

    held = (y == 2, y == 1)
    on_z = (last_y, first_y)
    some = min(4, groups)
    for side in range(2):
        send_near(side, 1, 0)

        @pl.when(jnp.logical_not(held[side]))
        def _(side=side):
            lax.fori_loop(2, some, functools.partial(send_near, side), 0)

        @pl.when(jnp.logical_not(held[side] | on_z[side]))
        def _(side=side):
            lax.fori_loop(some, groups, functools.partial(send_near, side), 0)

    def c2_arrival(j):
        remote(c2_send, c2_recv.at[j - 1], c2_send_sem.at[j - 1], c2_recv_sem.at[j - 1], at_y(j)).wait_recv()

    def c1_arrival(slot):
        remote(c1_send, c1_recv.at[slot], c1_send_sem.at[0], c1_recv_sem.at[slot], at_y(2)).wait_recv()

    c2_arrival(2)
    c1_arrival(same_z)

    @pl.when(relay)
    def _():
        c2_on_y().start()
        c1_on_y().start()

    for side in range(2):
        @pl.when(held[side])
        def _(side=side):
            lax.fori_loop(2, groups, functools.partial(send_near, side), 0)

    c1_on_z().start()
    row = lax.broadcasted_iota(jnp.int32, (COARSE, ROWS), 0)
    slot = row >> 3
    offset = jnp.where(slot == 0, -3, jnp.where(slot == 1, -2, jnp.where(slot == 2, 2, 3)))
    place = me + offset
    middle = jnp.where((place >= 0) & (place < BLOCKS), math.log(32.0), MASKED)
    far_row = row - MID_ROWS
    far_z = (z - way * ((far_row >> 4) + 1)) & (Z - 1)
    far_y = (y - ((far_row >> 2) & 3)) & (Y - 1)
    distance = jnp.abs(far_z * Y + far_y - me)
    far = jnp.where(distance >= 4, math.log(64.0), MASKED)
    bias[...] = jnp.where(row < MID_ROWS, middle, far)
    left_bias = jnp.where(me >= 1, 0.0, MASKED).astype(F32)
    right_bias = jnp.where(me < BLOCKS - 1, 0.0, MASKED).astype(F32)
    for which in range(2):
        coarse[which, COARSE:ROWS, :] = jnp.zeros((ROWS - COARSE, width), BF16)
    prob[KEYS:PADDED, :] = jnp.zeros((PADDED - KEYS, 2 * ROWS), BF16)
    grad[KEYS:PADDED, :] = jnp.zeros((PADDED - KEYS, 2 * ROWS), BF16)

    c2_arrival(1)
    c2_arrival(3)

    for j in range(Y):
        if j == 0:
            block = c2_send[...]
        else:
            block = c2_recv[j - 1]
        pack[...] = block.astype(F32)
        for which in range(2):
            for side in range(2):
                first = TWO * (2 * which + side)
                gathered[which, TWO * j:TWO * (j + 1), side * half:(side + 1) * half] = pack[first:first + TWO, :]
    z_send[...] = gathered[...].astype(BF16)

    def far_slot(k):
        return pl.ds(MID_ROWS + (k - 1) * Y * TWO, Y * TWO)

    z_back = remote(z_send, coarse.at[:, far_slot(7), :], z_back_sem.at[0], z_back_sem.at[1], at_z(-way))
    z_back.start()
    for side in range(2):
        @pl.when(on_z[side])
        def _(side=side):
            lax.fori_loop(some, groups, functools.partial(send_near, side), 0)

    def z_copy(k, part):
        cols = columns(part, z_width)
        src = coarse.at[:, far_slot(3), cols] if k > 3 else z_send.at[:, :, cols]
        return remote(
            src, coarse.at[:, far_slot(k), cols],
            z_send_sem.at[k - 1, part], z_recv_sem.at[k - 1, part], at_z(way * Z_STEPS[k]),
        )

    def z_own(part):
        for k in (3, 2, 1):
            z_copy(k, part).start()

    def z_forward(part):
        z_copy(3, part).wait_recv()
        for k in (6, 5, 4):
            z_copy(k, part).start()

    z_own(0)
    z_own(1)
    for slot in (0, 3, 3 - same_z):
        c1_arrival(slot)
    for which in range(2):
        rows = [c1_recv[s].astype(F32)[which * ONE:(which + 1) * ONE] for s in range(len(MID))]
        coarse[which, 0:MID_ROWS, :] = jnp.concatenate(rows, axis=0).astype(BF16)
    loads[2].wait()
    loads[3].wait()
    def grad_copy(side, g):
        return remote(
            near_send.at[side, g], near_recv.at[1 - side, g],
            grad_send_sem.at[side, g], grad_recv_sem.at[1 - side, g],
            at_block(-1 if side == 0 else 1),
        )

    def mg_copy(s, part):
        cols = columns(part, part_width)
        return remote(
            mg_send.at[s, :, cols], mg_recv.at[s, :, cols],
            mg_send_sem.at[part, s], mg_recv_sem.at[part, s], at_block(MID[s]),
        )

    def fg_copy(i, g):
        cols = columns(g, PAIR)
        slots = pl.ds(0, 3) if i == 0 else pl.ds(2 + i, 1)
        return remote(
            fg_send.at[slots, :, :, cols], fg_recv.at[slots, :, :, cols],
            fg_send_sem.at[i, g], fg_recv_sem.at[i, g], at_z(way * FG_STEPS[i]),
        )

    def sum_first(g):
        cols = columns(g, PAIR)
        for i, k in enumerate((2, 3, 4, 1)):
            fg_send[i, :, :, cols] = fg_own[k - 1, :, :, cols].astype(BF16)
        for i in range(2):
            fg_copy(i, g).start()

    def sum_second(g):
        cols = columns(g, PAIR)
        fg_copy(0, g).wait_recv()
        for i in range(3):
            total = fg_own[4 + i, :, :, cols] + fg_recv[i, :, :, cols].astype(F32)
            fg_send[4 + i, :, :, cols] = total.astype(BF16)
            fg_copy(2 + i, g).start()

    def heads(g):
        cols = columns(g, PAIR)
        return lax.rem(g, LEAD), cols, own_in[2, :, cols], own_in[3, :, cols]

    def near_part(g):
        slot, cols, q, do = heads(g)
        for side in range(2):
            for which in range(2):
                near_copy(side, which, g).wait_recv()
        q = q.astype(F32) * (1.0 / math.sqrt(HEAD_DIM))
        do = do.astype(F32)
        lane = lax.broadcasted_iota(jnp.int32, (ROWS, PAIR), 1)
        for h in range(2):
            mine = (lane >= HEAD_DIM) if h else (lane < HEAD_DIM)
            q_stack[slot, h * ROWS:(h + 1) * ROWS, :] = jnp.where(mine, q, 0.0).astype(BF16)
            do_stack[slot, h * ROWS:(h + 1) * ROWS, :] = jnp.where(mine, do, 0.0).astype(BF16)
        do_t[slot] = do.T
        keys, values = (
            (
                near_kv[0, g, which * ROWS:(which + 1) * ROWS, :],
                own_in[which, :, cols],
                near_kv[1, g, which * ROWS:(which + 1) * ROWS, :],
            )
            for which in range(2)
        )
        for i in range(3):
            key_t[slot, :, i * ROWS:(i + 1) * ROWS] = keys[i].T
            value_t[slot, :, i * ROWS:(i + 1) * ROWS] = values[i].T
        biases = (left_bias, None, right_bias)
        for h in range(2):
            qh = q_stack[slot, h * ROWS:(h + 1) * ROWS, :]
            doh = do_stack[slot, h * ROWS:(h + 1) * ROWS, :]
            top = None
            for i in range(3):
                s = dot(keys[i], qh, 1, 1)
                if biases[i] is not None:
                    s = s + biases[i]
                score[slot, h, i * ROWS:(i + 1) * ROWS, :] = s
                m = group_max(s)
                top = m if top is None else jnp.maximum(top, m)
                dots[slot, h, i * ROWS:(i + 1) * ROWS, :] = dot(values[i], doh, 1, 1)
            top = jnp.max(top, axis=0, keepdims=True)
            total = jnp.zeros((8, ROWS), F32)
            for c in range(0, NEAR, CHUNK):
                p = jnp.exp(score[slot, h, c:c + CHUNK, :] - top)
                score[slot, h, c:c + CHUNK, :] = p
                total = total + group_sum(p)
            stats[slot, h, 0] = jnp.broadcast_to(top, (8, ROWS))
            stats[slot, h, 1] = total

    def pair(g):
        slot, cols, _, _ = heads(g)
        part = g // part_groups

        @pl.when(g == 0)
        def _():
            z_back.wait_recv()

        @pl.when(g % z_groups == 0)
        def _():
            for k in (1, 2, 4, 5, 6):
                z_copy(k, g // z_groups).wait_recv()

        @pl.when(g + 2 < z_parts)
        def _():
            z_forward(g + 2)

        key = coarse[0, :, cols]
        value = coarse[1, :, cols]
        key_t[slot, :, NEAR:PADDED] = key.T
        value_t[slot, :, NEAR:PADDED] = value.T
        for h in range(2):
            qh = q_stack[slot, h * ROWS:(h + 1) * ROWS, :]
            doh = do_stack[slot, h * ROWS:(h + 1) * ROWS, :]
            lanes = slice(h * ROWS, (h + 1) * ROWS)
            s = dot(key[:COARSE], qh, 1, 1) + bias[...]
            dots[slot, h, NEAR:KEYS, :] = dot(value[:COARSE], doh, 1, 1)
            near_top = stats[slot, h, 0, 0:1, :]
            top = jnp.maximum(near_top, jnp.max(group_max(s), axis=0, keepdims=True))
            p = jnp.exp(s - top)
            score[slot, h, NEAR:KEYS, :] = p
            shrink = jnp.exp(near_top - top)
            total = shrink * jnp.sum(stats[slot, h, 1], axis=0, keepdims=True)
            inverse = 1.0 / (total + jnp.sum(group_sum(p), axis=0, keepdims=True))
            near_inverse = shrink * inverse
            for c in range(0, KEYS, CHUNK):
                p = score[slot, h, c:c + CHUNK, :] * (near_inverse if c < NEAR else inverse)
                prob[c:c + CHUNK, lanes] = p.astype(BF16)
            head = slice(h * HEAD_DIM, (h + 1) * HEAD_DIM)
            att = dot(value_t[slot, head, :], prob[:, lanes], 1, 0).astype(BF16).astype(F32)
            att_t[head, :] = att
            delta = jnp.sum(att * do_t[slot, head, :], axis=0, keepdims=True)
            for c in range(0, KEYS, CHUNK):
                p = score[slot, h, c:c + CHUNK, :] * (near_inverse if c < NEAR else inverse)
                grad[c:c + CHUNK, lanes] = (p * (dots[slot, h, c:c + CHUNK, :] - delta)).astype(BF16)
            gq_t[head, :] = dot(key_t[slot, head, :], grad[:, lanes], 1, 0) * (1.0 / math.sqrt(HEAD_DIM))
        stage[0, :, cols] = att_t[...].T.astype(BF16)
        stage[1, :, cols] = gq_t[...].T.astype(BF16)

        def key_grads(first, n):
            return (
                dot(grad[first:first + n, :], q_stack[slot], 1, 0),
                dot(prob[first:first + n, :], do_stack[slot], 1, 0),
            )

        dk, dv = key_grads(NEAR, COARSE)
        for s in range(len(MID)):
            both = jnp.concatenate([dk[s * ONE:(s + 1) * ONE], dv[s * ONE:(s + 1) * ONE]], axis=0)
            mg_send[s, :, cols] = both.astype(BF16)
        for k in range(1, Z):
            first = MID_ROWS + (k - 1) * Y * TWO
            fg_own[k - 1, 0, :, cols] = dk[first:first + Y * TWO]
            fg_own[k - 1, 1, :, cols] = dv[first:first + Y * TWO]
        sum_first(g)

        @pl.when(g >= LAG)
        def _():
            sum_second(g - LAG)


        @pl.when(g % part_groups == part_groups - 1)
        def _():
            for s in range(len(MID)):
                mg_copy(s, part).start()

        for side in range(2):
            dk, dv = key_grads(2 * ROWS * side, ROWS)
            near_send[side, g, 0:ROWS, :] = dk.astype(BF16)
            near_send[side, g, ROWS:2 * ROWS, :] = dv.astype(BF16)
            grad_copy(side, g).start()
        dk, dv = key_grads(ROWS, ROWS)
        own_grad[g, 0:ROWS, :] = dk
        own_grad[g, ROWS:2 * ROWS, :] = dv
    lead = min(LEAD, groups)

    def turn(t, carry):
        @pl.when(t >= lead)
        def _():
            pair(t - lead)

        @pl.when(t < groups)
        def _():
            near_part(t)

        for part in range(2):
            @pl.when(t == min(part + 1, lead - 1))
            def _(part=part):
                z_forward(part)
                if part + 2 < z_parts:
                    z_own(part + 2)

        return carry

    lax.fori_loop(0, groups + lead, turn, 0)

    def add_near(g):
        for side in range(2):
            grad_copy(side, g).wait_recv()
        own_grad[g] = own_grad[g] + near_recv[0, g].astype(F32) + near_recv[1, g].astype(F32)

    def far_arrival(g, carry):
        for i in range(1, 5):
            fg_copy(i, g).wait_recv()
        return carry

    for g in range(max(groups - LAG, 0), groups):
        sum_second(g)
    lax.fori_loop(0, groups, far_arrival, 0)
    for which in range(2):
        total = fg_recv[3, which].astype(F32)
        for i in range(4, 7):
            total = total + fg_recv[i, which].astype(F32)
        gathered[which] = total
    yg_copies = [
        remote(yg_send.at[j - 1], yg_recv.at[j - 1], yg_send_sem.at[j - 1], yg_recv_sem.at[j - 1], at_y(-j))
        for j in range(1, Y)
    ]
    for j in range(1, Y):
        yg_send[j - 1] = pack_rows(TWO * j)
        yg_copies[j - 1].start()

    def drain(g, carry):
        for side in range(2):
            for which in range(2):
                near_copy(side, which, g).wait_send()
        for i in range(5):
            fg_copy(i, g).wait_send()
        return carry

    lax.fori_loop(0, groups, drain, 0)
    z_back.wait_send()
    for part in range(z_parts):
        for k in range(1, Z - 1):
            z_copy(k, part).wait_send()
    small_copies(lambda copy: copy.wait_send())
    c1_on_z().wait_send()

    @pl.when(relay)
    def _():
        c2_on_y().wait_send()
        c1_on_y().wait_send()

    for g in range(groups):
        add_near(g)
    for part in range(parts):
        for s in range(len(MID)):
            mg_copy(s, part).wait_recv()
    middle_sum = mg_recv[0].astype(F32)
    for s in range(1, len(MID)):
        middle_sum = middle_sum + mg_recv[s].astype(F32)
    coarse_sum[...] = jnp.zeros_like(coarse_sum)
    for which in range(2):
        coarse_sum[which, 0:ONE, :] = middle_sum[which * ONE:(which + 1) * ONE]
        coarse_sum[which, ONE:ONE + TWO, :] = gathered[which, 0:TWO, :]
    for j in range(1, Y):
        yg_copies[j - 1].wait_recv()
        pack[...] = yg_recv[j - 1].astype(F32)
        for which in range(2):
            for side in range(2):
                first = TWO * (2 * which + side)
                cols = slice(side * half, (side + 1) * half)
                coarse_sum[which, ONE:ONE + TWO, cols] = (
                    coarse_sum[which, ONE:ONE + TWO, cols] + pack[first:first + TWO, :]
                )


    for g in range(groups):
        cols = slice(g * PAIR, (g + 1) * PAIR)
        for which in range(2):
            wide = coarse_sum[which, :, cols]
            high = wide.astype(BF16)
            low = (wide - high.astype(F32)).astype(BF16)
            both = jnp.concatenate([high, low], axis=0)
            total = own_grad[g, which * ROWS:(which + 1) * ROWS, :] + dot(restrict_t[...], both, 1, 0)
            stage[2 + which, :, cols] = total.astype(BF16)
    for g in range(groups):
        for side in range(2):
            grad_copy(side, g).wait_send()
    for copy in yg_copies:
        copy.wait_send()
    for part in range(parts):
        for s in range(len(MID)):
            mg_copy(s, part).wait_send()


def per_device(queries, keys, values, cotangent, restrict_one, restrict_two):
    rows, width = queries.shape
    groups = width // PAIR
    parts = 2
    z_parts = min(groups, 4)
    hbm = pl.BlockSpec(memory_space=pl.ANY)
    vmem = pl.BlockSpec(memory_space=pltpu.VMEM)
    dma = pltpu.SemaphoreType.DMA
    mid = len(MID)
    scratch = [
        pltpu.VMEM((4, ROWS, width), BF16),
        pltpu.VMEM((2, groups, 2 * ROWS, PAIR), BF16),
        pltpu.VMEM((2, groups, 2 * ROWS, PAIR), BF16),
        pltpu.VMEM((2, groups, 2 * ROWS, PAIR), BF16),
        pltpu.VMEM((groups, 2 * ROWS, PAIR), F32),
        pltpu.VMEM((2, ROWS, width), BF16),
        pltpu.VMEM((16, width), BF16),
        pltpu.VMEM((mid, 16, width), BF16),
        pltpu.VMEM((16, width // 2), BF16),
        pltpu.VMEM((Y - 1, 16, width // 2), BF16),
        pltpu.VMEM((2, 16, width), BF16),
        pltpu.VMEM((mid, 16, width), BF16),
        pltpu.VMEM((mid, 16, width), BF16),
        pltpu.VMEM((Z - 1, 2, 16, width), BF16),
        pltpu.VMEM((Z - 1, 2, 16, width), BF16),
        pltpu.VMEM((Y - 1, 16, width // 2), BF16),
        pltpu.VMEM((Y - 1, 16, width // 2), BF16),
        pltpu.VMEM((Z - 1, 2, 16, width), F32),
        pltpu.VMEM((ONE, ROWS), BF16),
        pltpu.VMEM((TWO, ROWS), BF16),
        pltpu.VMEM((16, ROWS), F32),
        pltpu.VMEM((16, width // 2), F32),
        pltpu.VMEM((2, 16, width), F32),
        pltpu.VMEM((COARSE, ROWS), F32),
        pltpu.VMEM((LEAD, 2 * ROWS, PAIR), BF16),
        pltpu.VMEM((LEAD, 2 * ROWS, PAIR), BF16),
        pltpu.VMEM((LEAD, PAIR, PADDED), BF16),
        pltpu.VMEM((LEAD, PAIR, PADDED), BF16),
        pltpu.VMEM((LEAD, PAIR, ROWS), F32),
        pltpu.VMEM((LEAD, 2, KEYS, ROWS), F32),
        pltpu.VMEM((LEAD, 2, KEYS, ROWS), F32),
        pltpu.VMEM((LEAD, 2, 2, 8, ROWS), F32),
        pltpu.VMEM((PADDED, 2 * ROWS), BF16),
        pltpu.VMEM((PADDED, 2 * ROWS), BF16),
        pltpu.VMEM((PAIR, ROWS), F32),
        pltpu.VMEM((PAIR, ROWS), F32),
        pltpu.VMEM((2, 16, width), F32),
        pltpu.VMEM((ROWS, 32), BF16),
        dma((6,)),
        dma((2, 2, groups)), dma((2, 2, groups)),
        dma((2, groups)), dma((2, groups)),
        dma((5,)), dma((mid,)),
        dma((4,)), dma((Y - 1,)),
        dma((Z - 2, z_parts)), dma((Z - 2, z_parts)), dma((2,)),
        dma((parts, mid)), dma((parts, mid)),
        dma((5, groups)), dma((5, groups)),
        dma((Y - 1,)), dma((Y - 1,)),
    ]
    stage = pl.pallas_call(
        functools.partial(kernel, groups, parts, z_parts),
        out_shape=pltpu.VMEM((4, ROWS, width), BF16),
        in_specs=[hbm] * 6,
        out_specs=vmem,
        scratch_shapes=scratch,
        compiler_params=pltpu.CompilerParams(
            collective_id=0, has_side_effects=True, vmem_limit_bytes=56 * 1024 * 1024
        ),
    )(queries, keys, values, cotangent, restrict_one, restrict_two)
    return tuple(stage[i] for i in range(4))


def solution(mesh):
    rows = P(("prompt", "seq"), None)
    return jax.shard_map(
        per_device, mesh=mesh, in_specs=(rows, rows, rows, rows, P(), P()),
        out_specs=(rows, rows, rows, rows), check_vma=False,
    )
```

```python
import functools
import math

import jax
import jax.numpy as jnp
from jax import lax
from jax.experimental import pallas as pl
from jax.experimental.pallas import tpu as pltpu
from jax.sharding import PartitionSpec as P

HEAD_DIM = 64
ROWS = 256
PAIR = 128
Y = 4
Z = 8
BLOCKS = Y * Z
ONE = 8
TWO = 4
MID = (-3, -2, 2, 3)
LAG = 3
LEAD = 5
FG_STEPS = (3, -1, 3, 2, 1)
Z_STEPS = {1: 1, 2: 2, 3: 3, 4: 1, 5: 2, 6: 3}
MID_ROWS = len(MID) * ONE
FAR_ROWS = (Z - 1) * Y * TWO
COARSE = MID_ROWS + FAR_ROWS
NEAR = 3 * ROWS
KEYS = NEAR + COARSE
PADDED = 4 * ROWS
CHUNK = 48
MASKED = -1e30
F32 = jnp.float32
BF16 = jnp.bfloat16
MESH = pl.DeviceIdType.MESH


def dot(a, b, ca, cb):
    return lax.dot_general(a, b, (((ca,), (cb,)), ((), ())), preferred_element_type=F32)


def group_max(x):
    return jnp.max(x.reshape(x.shape[0] // 8, 8, x.shape[1]), axis=0)


def group_sum(x):
    return jnp.sum(x.reshape(x.shape[0] // 8, 8, x.shape[1]), axis=0)


def kernel(
    groups, parts, z_parts,
    q_hbm, k_hbm, v_hbm, do_hbm, r1_hbm, r2_hbm,
    stage,
    own_in, near_kv, near_send, near_recv, own_grad, coarse,
    c1_send, c1_recv, c2_send, c2_recv, z_send, mg_send, mg_recv, fg_send, fg_recv, yg_send, yg_recv,
    fg_own, r1_in, r2_in, restrict, pack, gathered, bias, q_stack, do_stack, key_t, value_t, do_t, score, dots, stats, prob, grad,
    att_t, gq_t, coarse_sum, restrict_t,
    load_sem, near_send_sem, near_recv_sem, grad_send_sem, grad_recv_sem,
    c1_send_sem, c1_recv_sem, c2_send_sem, c2_recv_sem, z_send_sem, z_recv_sem, z_back_sem,
    mg_send_sem, mg_recv_sem, fg_send_sem, fg_recv_sem, yg_send_sem, yg_recv_sem,
):
    width = groups * PAIR
    half = width // 2
    part_groups = groups // parts
    part_width = width // parts
    z_groups = groups // z_parts
    z_width = width // z_parts
    me = lax.axis_index("seq")
    z = me // Y
    y = me % Y
    way = 1 - 2 * (y // 2)

    def at_block(offset):
        return lax.rem(me + offset + BLOCKS, BLOCKS)

    def at_y(offset):
        return z * Y + lax.rem(y + offset + Y, Y)

    def at_z(offset):
        return lax.rem(z + offset + Z, Z) * Y + y

    def remote(src, dst, send_sem, recv_sem, to):
        return pltpu.make_async_remote_copy(
            src_ref=src, dst_ref=dst, send_sem=send_sem, recv_sem=recv_sem,
            device_id={"seq": to}, device_id_type=MESH,
        )

    def columns(index, size):
        return pl.ds(pl.multiple_of(index * size, size), size)

    barrier = pltpu.get_barrier_semaphore()
    partners = [at_block(o) for o in (-1, 1) + MID]
    partners += [at_y(j) for j in range(1, Y)] + [at_z(k) for k in (-3, -2, -1, 1, 2, 3)]
    for partner in partners:
        pl.semaphore_signal(barrier, inc=1, device_id={"seq": partner}, device_id_type=MESH)
    loads = [
        pltpu.make_async_copy(src, own_in.at[i], load_sem.at[i])
        for i, src in enumerate((k_hbm, v_hbm, q_hbm, do_hbm))
    ]
    loads.append(pltpu.make_async_copy(r1_hbm, r1_in, load_sem.at[4]))
    loads.append(pltpu.make_async_copy(r2_hbm, r2_in, load_sem.at[5]))
    for load in loads:
        load.start()
    pl.semaphore_wait(barrier, len(partners))

    def near_copy(side, which, g):
        src = (k_hbm, v_hbm)[which].at[:, columns(g, PAIR)]
        return remote(
            src, near_kv.at[side, g, pl.ds(which * ROWS, ROWS)],
            near_send_sem.at[side, which, g], near_recv_sem.at[side, which, g],
            at_block(1 if side == 0 else -1),
        )

    def send_near(side, g, carry):
        for which in range(2):
            near_copy(side, which, g).start()
        return carry

    for side in range(2):
        send_near(side, 0, 0)

    restrict[...] = jnp.zeros_like(restrict)
    loads[4].wait()
    loads[5].wait()
    restrict[0:ONE, :] = r1_in[...].astype(F32)
    restrict[ONE:ONE + TWO, :] = r2_in[...].astype(F32)
    restrict_b = restrict[...].astype(BF16)
    restrict_t[...] = jnp.concatenate([restrict[...], restrict[...]], axis=0).T.astype(BF16)
    loads[0].wait()
    loads[1].wait()
    coarse_k = dot(restrict_b, own_in[0], 1, 0)
    coarse_v = dot(restrict_b, own_in[1], 1, 0)
    gathered[0] = coarse_k
    gathered[1] = coarse_v

    def pack_rows(first):
        for which in range(2):
            for side in range(2):
                row = TWO * (2 * which + side)
                pack[row:row + TWO, :] = gathered[which, first:first + TWO, side * half:(side + 1) * half]
        return pack[...].astype(BF16)

    c2_send[...] = pack_rows(ONE)
    c1_send[...] = jnp.concatenate([coarse_k[0:ONE], coarse_v[0:ONE]], axis=0).astype(BF16)

    first_y, last_y, relay = y == 0, y == Y - 1, (y == 1) | (y == 2)
    same_z = 2 - y // 2

    def c2_copy(j):
        return remote(c2_send, c2_recv.at[j - 1], c2_send_sem.at[j - 1], c2_recv_sem.at[j - 1], at_y(j))

    def c1_copy(i):
        to, slot = ((at_y(2), 3 - same_z), (at_block(3), 0), (at_block(-3), 3))[i]
        return remote(c1_send, c1_recv.at[slot], c1_send_sem.at[i], c1_recv_sem.at[slot], to)

    def c1_on_z():
        slot = 3 - same_z
        return remote(
            c1_recv.at[same_z], c1_recv.at[slot], c1_send_sem.at[3], c1_recv_sem.at[slot], at_z(way)
        )

    def c2_on_y():
        slot = 2 * (y - 1)
        return remote(c2_recv.at[1], c2_recv.at[slot], c2_send_sem.at[3], c2_recv_sem.at[slot], at_y(2 * y - 3))

    def c1_on_y():
        slot = 3 * (2 - y)
        return remote(
            c1_recv.at[same_z], c1_recv.at[slot], c1_send_sem.at[4], c1_recv_sem.at[slot], at_y(2 * y - 3)
        )

    def small_copies(act):
        act(c2_copy(2))
        act(c1_copy(0))

        @pl.when(jnp.logical_not(first_y))
        def _():
            act(c2_copy(3))
            act(c1_copy(1))

        @pl.when(jnp.logical_not(last_y))
        def _():
            act(c2_copy(1))
            act(c1_copy(2))

    small_copies(lambda copy: copy.start())

    held = (y == 2, y == 1)
    on_z = (last_y, first_y)
    some = min(4, groups)
    for side in range(2):
        send_near(side, 1, 0)

        @pl.when(jnp.logical_not(held[side]))
        def _(side=side):
            lax.fori_loop(2, some, functools.partial(send_near, side), 0)

        @pl.when(jnp.logical_not(held[side] | on_z[side]))
        def _(side=side):
            lax.fori_loop(some, groups, functools.partial(send_near, side), 0)

    def c2_arrival(j):
        remote(c2_send, c2_recv.at[j - 1], c2_send_sem.at[j - 1], c2_recv_sem.at[j - 1], at_y(j)).wait_recv()

    def c1_arrival(slot):
        remote(c1_send, c1_recv.at[slot], c1_send_sem.at[0], c1_recv_sem.at[slot], at_y(2)).wait_recv()

    c2_arrival(2)
    c1_arrival(same_z)

    @pl.when(relay)
    def _():
        c2_on_y().start()
        c1_on_y().start()

    for side in range(2):
        @pl.when(held[side])
        def _(side=side):
            lax.fori_loop(2, groups, functools.partial(send_near, side), 0)

    c1_on_z().start()
    row = lax.broadcasted_iota(jnp.int32, (COARSE, ROWS), 0)
    slot = row >> 3
    offset = jnp.where(slot == 0, -3, jnp.where(slot == 1, -2, jnp.where(slot == 2, 2, 3)))
    place = me + offset
    middle = jnp.where((place >= 0) & (place < BLOCKS), math.log(32.0), MASKED)
    far_row = row - MID_ROWS
    far_z = (z - way * ((far_row >> 4) + 1)) & (Z - 1)
    far_y = (y - ((far_row >> 2) & 3)) & (Y - 1)
    distance = jnp.abs(far_z * Y + far_y - me)
    far = jnp.where(distance >= 4, math.log(64.0), MASKED)
    bias[...] = jnp.where(row < MID_ROWS, middle, far)
    left_bias = jnp.where(me >= 1, 0.0, MASKED).astype(F32)
    right_bias = jnp.where(me < BLOCKS - 1, 0.0, MASKED).astype(F32)
    for which in range(2):
        coarse[which, COARSE:ROWS, :] = jnp.zeros((ROWS - COARSE, width), BF16)
    prob[KEYS:PADDED, :] = jnp.zeros((PADDED - KEYS, 2 * ROWS), BF16)
    grad[KEYS:PADDED, :] = jnp.zeros((PADDED - KEYS, 2 * ROWS), BF16)

    c2_arrival(1)
    c2_arrival(3)

    for j in range(Y):
        if j == 0:
            block = c2_send[...]
        else:
            block = c2_recv[j - 1]
        pack[...] = block.astype(F32)
        for which in range(2):
            for side in range(2):
                first = TWO * (2 * which + side)
                gathered[which, TWO * j:TWO * (j + 1), side * half:(side + 1) * half] = pack[first:first + TWO, :]
    z_send[...] = gathered[...].astype(BF16)

    def far_slot(k):
        return pl.ds(MID_ROWS + (k - 1) * Y * TWO, Y * TWO)

    z_back = remote(z_send, coarse.at[:, far_slot(7), :], z_back_sem.at[0], z_back_sem.at[1], at_z(-way))
    z_back.start()
    for side in range(2):
        @pl.when(on_z[side])
        def _(side=side):
            lax.fori_loop(some, groups, functools.partial(send_near, side), 0)

    def z_copy(k, part):
        cols = columns(part, z_width)
        src = coarse.at[:, far_slot(3), cols] if k > 3 else z_send.at[:, :, cols]
        return remote(
            src, coarse.at[:, far_slot(k), cols],
            z_send_sem.at[k - 1, part], z_recv_sem.at[k - 1, part], at_z(way * Z_STEPS[k]),
        )

    def z_own(part):
        for k in (3, 2, 1):
            z_copy(k, part).start()

    def z_forward(part):
        z_copy(3, part).wait_recv()
        for k in (6, 5, 4):
            z_copy(k, part).start()

    z_own(0)
    z_own(1)
    for slot in (0, 3, 3 - same_z):
        c1_arrival(slot)
    for which in range(2):
        rows = [c1_recv[s].astype(F32)[which * ONE:(which + 1) * ONE] for s in range(len(MID))]
        coarse[which, 0:MID_ROWS, :] = jnp.concatenate(rows, axis=0).astype(BF16)
    loads[2].wait()
    loads[3].wait()
    def grad_copy(side, g):
        return remote(
            near_send.at[side, g], near_recv.at[1 - side, g],
            grad_send_sem.at[side, g], grad_recv_sem.at[1 - side, g],
            at_block(-1 if side == 0 else 1),
        )

    def mg_copy(s, part):
        cols = columns(part, part_width)
        return remote(
            mg_send.at[s, :, cols], mg_recv.at[s, :, cols],
            mg_send_sem.at[part, s], mg_recv_sem.at[part, s], at_block(MID[s]),
        )

    def fg_copy(i, g):
        cols = columns(g, PAIR)
        slots = pl.ds(0, 3) if i == 0 else pl.ds(2 + i, 1)
        return remote(
            fg_send.at[slots, :, :, cols], fg_recv.at[slots, :, :, cols],
            fg_send_sem.at[i, g], fg_recv_sem.at[i, g], at_z(way * FG_STEPS[i]),
        )

    def sum_first(g):
        cols = columns(g, PAIR)
        for i, k in enumerate((2, 3, 4, 1)):
            fg_send[i, :, :, cols] = fg_own[k - 1, :, :, cols].astype(BF16)
        for i in range(2):
            fg_copy(i, g).start()

    def sum_second(g):
        cols = columns(g, PAIR)
        fg_copy(0, g).wait_recv()
        for i in range(3):
            total = fg_own[4 + i, :, :, cols] + fg_recv[i, :, :, cols].astype(F32)
            fg_send[4 + i, :, :, cols] = total.astype(BF16)
            fg_copy(2 + i, g).start()

    def heads(g):
        cols = columns(g, PAIR)
        return lax.rem(g, LEAD), cols, own_in[2, :, cols], own_in[3, :, cols]

    def near_part(g):
        slot, cols, q, do = heads(g)
        for side in range(2):
            for which in range(2):
                near_copy(side, which, g).wait_recv()
        q = q.astype(F32) * (1.0 / math.sqrt(HEAD_DIM))
        do = do.astype(F32)
        lane = lax.broadcasted_iota(jnp.int32, (ROWS, PAIR), 1)
        for h in range(2):
            mine = (lane >= HEAD_DIM) if h else (lane < HEAD_DIM)
            q_stack[slot, h * ROWS:(h + 1) * ROWS, :] = jnp.where(mine, q, 0.0).astype(BF16)
            do_stack[slot, h * ROWS:(h + 1) * ROWS, :] = jnp.where(mine, do, 0.0).astype(BF16)
        do_t[slot] = do.T
        keys, values = (
            (
                near_kv[0, g, which * ROWS:(which + 1) * ROWS, :],
                own_in[which, :, cols],
                near_kv[1, g, which * ROWS:(which + 1) * ROWS, :],
            )
            for which in range(2)
        )
        for i in range(3):
            key_t[slot, :, i * ROWS:(i + 1) * ROWS] = keys[i].T
            value_t[slot, :, i * ROWS:(i + 1) * ROWS] = values[i].T
        biases = (left_bias, None, right_bias)
        for h in range(2):
            qh = q_stack[slot, h * ROWS:(h + 1) * ROWS, :]
            doh = do_stack[slot, h * ROWS:(h + 1) * ROWS, :]
            top = None
            for i in range(3):
                s = dot(keys[i], qh, 1, 1)
                if biases[i] is not None:
                    s = s + biases[i]
                score[slot, h, i * ROWS:(i + 1) * ROWS, :] = s
                m = group_max(s)
                top = m if top is None else jnp.maximum(top, m)
                dots[slot, h, i * ROWS:(i + 1) * ROWS, :] = dot(values[i], doh, 1, 1)
            top = jnp.max(top, axis=0, keepdims=True)
            total = jnp.zeros((8, ROWS), F32)
            for c in range(0, NEAR, CHUNK):
                p = jnp.exp(score[slot, h, c:c + CHUNK, :] - top)
                score[slot, h, c:c + CHUNK, :] = p
                total = total + group_sum(p)
            stats[slot, h, 0] = jnp.broadcast_to(top, (8, ROWS))
            stats[slot, h, 1] = total

    def pair(g):
        slot, cols, _, _ = heads(g)
        part = g // part_groups

        @pl.when(g == 0)
        def _():
            z_back.wait_recv()

        @pl.when(g % z_groups == 0)
        def _():
            for k in (1, 2, 4, 5, 6):
                z_copy(k, g // z_groups).wait_recv()

        @pl.when(g + 2 < z_parts)
        def _():
            z_forward(g + 2)

        key = coarse[0, :, cols]
        value = coarse[1, :, cols]
        key_t[slot, :, NEAR:PADDED] = key.T
        value_t[slot, :, NEAR:PADDED] = value.T
        for h in range(2):
            qh = q_stack[slot, h * ROWS:(h + 1) * ROWS, :]
            doh = do_stack[slot, h * ROWS:(h + 1) * ROWS, :]
            lanes = slice(h * ROWS, (h + 1) * ROWS)
            s = dot(key[:COARSE], qh, 1, 1) + bias[...]
            dots[slot, h, NEAR:KEYS, :] = dot(value[:COARSE], doh, 1, 1)
            near_top = stats[slot, h, 0, 0:1, :]
            top = jnp.maximum(near_top, jnp.max(group_max(s), axis=0, keepdims=True))
            p = jnp.exp(s - top)
            score[slot, h, NEAR:KEYS, :] = p
            shrink = jnp.exp(near_top - top)
            total = shrink * jnp.sum(stats[slot, h, 1], axis=0, keepdims=True)
            inverse = 1.0 / (total + jnp.sum(group_sum(p), axis=0, keepdims=True))
            near_inverse = shrink * inverse
            for c in range(0, KEYS, CHUNK):
                p = score[slot, h, c:c + CHUNK, :] * (near_inverse if c < NEAR else inverse)
                prob[c:c + CHUNK, lanes] = p.astype(BF16)
            head = slice(h * HEAD_DIM, (h + 1) * HEAD_DIM)
            att = dot(value_t[slot, head, :], prob[:, lanes], 1, 0).astype(BF16).astype(F32)
            att_t[head, :] = att
            delta = jnp.sum(att * do_t[slot, head, :], axis=0, keepdims=True)
            for c in range(0, KEYS, CHUNK):
                p = score[slot, h, c:c + CHUNK, :] * (near_inverse if c < NEAR else inverse)
                grad[c:c + CHUNK, lanes] = (p * (dots[slot, h, c:c + CHUNK, :] - delta)).astype(BF16)
        def key_grads(first, n):
            return (
                dot(grad[first:first + n, :], q_stack[slot], 1, 0),
                dot(prob[first:first + n, :], do_stack[slot], 1, 0),
            )

        dk, dv = key_grads(NEAR, COARSE)
        for s in range(len(MID)):
            both = jnp.concatenate([dk[s * ONE:(s + 1) * ONE], dv[s * ONE:(s + 1) * ONE]], axis=0)
            mg_send[s, :, cols] = both.astype(BF16)
        for k in range(1, Z):
            first = MID_ROWS + (k - 1) * Y * TWO
            fg_own[k - 1, 0, :, cols] = dk[first:first + Y * TWO]
            fg_own[k - 1, 1, :, cols] = dv[first:first + Y * TWO]
        sum_first(g)

        @pl.when(g >= LAG)
        def _():
            sum_second(g - LAG)


        @pl.when(g % part_groups == part_groups - 1)
        def _():
            for s in range(len(MID)):
                mg_copy(s, part).start()

        for side in range(2):
            dk, dv = key_grads(2 * ROWS * side, ROWS)
            near_send[side, g, 0:ROWS, :] = dk.astype(BF16)
            near_send[side, g, ROWS:2 * ROWS, :] = dv.astype(BF16)
            grad_copy(side, g).start()
        dk, dv = key_grads(ROWS, ROWS)
        own_grad[g, 0:ROWS, :] = dk
        own_grad[g, ROWS:2 * ROWS, :] = dv
        for h in range(2):
            head = slice(h * HEAD_DIM, (h + 1) * HEAD_DIM)
            gq = dot(key_t[slot, head, :], grad[:, h * ROWS:(h + 1) * ROWS], 1, 0)
            gq_t[head, :] = gq * (1.0 / math.sqrt(HEAD_DIM))
        stage[0, :, cols] = att_t[...].T.astype(BF16)
        stage[1, :, cols] = gq_t[...].T.astype(BF16)
    lead = min(LEAD, groups)

    def turn(t, carry):
        @pl.when(t >= lead)
        def _():
            pair(t - lead)

        @pl.when(t < groups)
        def _():
            near_part(t)

        for part in range(2):
            @pl.when(t == min(part + 1, lead - 1))
            def _(part=part):
                z_forward(part)
                if part + 2 < z_parts:
                    z_own(part + 2)

        return carry

    lax.fori_loop(0, groups + lead, turn, 0)

    def add_near(g):
        for side in range(2):
            grad_copy(side, g).wait_recv()
        own_grad[g] = own_grad[g] + near_recv[0, g].astype(F32) + near_recv[1, g].astype(F32)

    def far_arrival(g, carry):
        for i in range(1, 5):
            fg_copy(i, g).wait_recv()
        return carry

    for g in range(max(groups - LAG, 0), groups):
        sum_second(g)
    lax.fori_loop(0, groups, far_arrival, 0)
    for which in range(2):
        total = fg_recv[3, which].astype(F32)
        for i in range(4, 7):
            total = total + fg_recv[i, which].astype(F32)
        gathered[which] = total
    yg_copies = [
        remote(yg_send.at[j - 1], yg_recv.at[j - 1], yg_send_sem.at[j - 1], yg_recv_sem.at[j - 1], at_y(-j))
        for j in range(1, Y)
    ]
    for j in range(1, Y):
        yg_send[j - 1] = pack_rows(TWO * j)
        yg_copies[j - 1].start()

    def drain(g, carry):
        for side in range(2):
            for which in range(2):
                near_copy(side, which, g).wait_send()
        for i in range(5):
            fg_copy(i, g).wait_send()
        return carry

    lax.fori_loop(0, groups, drain, 0)
    z_back.wait_send()
    for part in range(z_parts):
        for k in range(1, Z - 1):
            z_copy(k, part).wait_send()
    small_copies(lambda copy: copy.wait_send())
    c1_on_z().wait_send()

    @pl.when(relay)
    def _():
        c2_on_y().wait_send()
        c1_on_y().wait_send()

    for g in range(groups):
        add_near(g)
    for part in range(parts):
        for s in range(len(MID)):
            mg_copy(s, part).wait_recv()
    middle_sum = mg_recv[0].astype(F32)
    for s in range(1, len(MID)):
        middle_sum = middle_sum + mg_recv[s].astype(F32)
    coarse_sum[...] = jnp.zeros_like(coarse_sum)
    for which in range(2):
        coarse_sum[which, 0:ONE, :] = middle_sum[which * ONE:(which + 1) * ONE]
        coarse_sum[which, ONE:ONE + TWO, :] = gathered[which, 0:TWO, :]
    for j in range(1, Y):
        yg_copies[j - 1].wait_recv()
        pack[...] = yg_recv[j - 1].astype(F32)
        for which in range(2):
            for side in range(2):
                first = TWO * (2 * which + side)
                cols = slice(side * half, (side + 1) * half)
                coarse_sum[which, ONE:ONE + TWO, cols] = (
                    coarse_sum[which, ONE:ONE + TWO, cols] + pack[first:first + TWO, :]
                )


    for g in range(groups):
        cols = slice(g * PAIR, (g + 1) * PAIR)
        for which in range(2):
            wide = coarse_sum[which, :, cols]
            high = wide.astype(BF16)
            low = (wide - high.astype(F32)).astype(BF16)
            both = jnp.concatenate([high, low], axis=0)
            total = own_grad[g, which * ROWS:(which + 1) * ROWS, :] + dot(restrict_t[...], both, 1, 0)
            stage[2 + which, :, cols] = total.astype(BF16)
    for g in range(groups):
        for side in range(2):
            grad_copy(side, g).wait_send()
    for copy in yg_copies:
        copy.wait_send()
    for part in range(parts):
        for s in range(len(MID)):
            mg_copy(s, part).wait_send()


def per_device(queries, keys, values, cotangent, restrict_one, restrict_two):
    rows, width = queries.shape
    groups = width // PAIR
    parts = 2
    z_parts = min(groups, 4)
    hbm = pl.BlockSpec(memory_space=pl.ANY)
    vmem = pl.BlockSpec(memory_space=pltpu.VMEM)
    dma = pltpu.SemaphoreType.DMA
    mid = len(MID)
    scratch = [
        pltpu.VMEM((4, ROWS, width), BF16),
        pltpu.VMEM((2, groups, 2 * ROWS, PAIR), BF16),
        pltpu.VMEM((2, groups, 2 * ROWS, PAIR), BF16),
        pltpu.VMEM((2, groups, 2 * ROWS, PAIR), BF16),
        pltpu.VMEM((groups, 2 * ROWS, PAIR), F32),
        pltpu.VMEM((2, ROWS, width), BF16),
        pltpu.VMEM((16, width), BF16),
        pltpu.VMEM((mid, 16, width), BF16),
        pltpu.VMEM((16, width // 2), BF16),
        pltpu.VMEM((Y - 1, 16, width // 2), BF16),
        pltpu.VMEM((2, 16, width), BF16),
        pltpu.VMEM((mid, 16, width), BF16),
        pltpu.VMEM((mid, 16, width), BF16),
        pltpu.VMEM((Z - 1, 2, 16, width), BF16),
        pltpu.VMEM((Z - 1, 2, 16, width), BF16),
        pltpu.VMEM((Y - 1, 16, width // 2), BF16),
        pltpu.VMEM((Y - 1, 16, width // 2), BF16),
        pltpu.VMEM((Z - 1, 2, 16, width), F32),
        pltpu.VMEM((ONE, ROWS), BF16),
        pltpu.VMEM((TWO, ROWS), BF16),
        pltpu.VMEM((16, ROWS), F32),
        pltpu.VMEM((16, width // 2), F32),
        pltpu.VMEM((2, 16, width), F32),
        pltpu.VMEM((COARSE, ROWS), F32),
        pltpu.VMEM((LEAD, 2 * ROWS, PAIR), BF16),
        pltpu.VMEM((LEAD, 2 * ROWS, PAIR), BF16),
        pltpu.VMEM((LEAD, PAIR, PADDED), BF16),
        pltpu.VMEM((LEAD, PAIR, PADDED), BF16),
        pltpu.VMEM((LEAD, PAIR, ROWS), F32),
        pltpu.VMEM((LEAD, 2, KEYS, ROWS), F32),
        pltpu.VMEM((LEAD, 2, KEYS, ROWS), F32),
        pltpu.VMEM((LEAD, 2, 2, 8, ROWS), F32),
        pltpu.VMEM((PADDED, 2 * ROWS), BF16),
        pltpu.VMEM((PADDED, 2 * ROWS), BF16),
        pltpu.VMEM((PAIR, ROWS), F32),
        pltpu.VMEM((PAIR, ROWS), F32),
        pltpu.VMEM((2, 16, width), F32),
        pltpu.VMEM((ROWS, 32), BF16),
        dma((6,)),
        dma((2, 2, groups)), dma((2, 2, groups)),
        dma((2, groups)), dma((2, groups)),
        dma((5,)), dma((mid,)),
        dma((4,)), dma((Y - 1,)),
        dma((Z - 2, z_parts)), dma((Z - 2, z_parts)), dma((2,)),
        dma((parts, mid)), dma((parts, mid)),
        dma((5, groups)), dma((5, groups)),
        dma((Y - 1,)), dma((Y - 1,)),
    ]
    stage = pl.pallas_call(
        functools.partial(kernel, groups, parts, z_parts),
        out_shape=pltpu.VMEM((4, ROWS, width), BF16),
        in_specs=[hbm] * 6,
        out_specs=vmem,
        scratch_shapes=scratch,
        compiler_params=pltpu.CompilerParams(
            collective_id=0, has_side_effects=True, vmem_limit_bytes=56 * 1024 * 1024
        ),
    )(queries, keys, values, cotangent, restrict_one, restrict_two)
    return tuple(stage[i] for i in range(4))


def solution(mesh):
    rows = P(("prompt", "seq"), None)
    return jax.shard_map(
        per_device, mesh=mesh, in_specs=(rows, rows, rows, rows, P(), P()),
        out_specs=(rows, rows, rows, rows), check_vma=False,
    )
```

```python
import functools
import math

import jax
import jax.numpy as jnp
from jax import lax
from jax.experimental import pallas as pl
from jax.experimental.pallas import tpu as pltpu
from jax.sharding import PartitionSpec as P

HEAD_DIM = 64
ROWS = 256
PAIR = 128
Y = 4
Z = 8
BLOCKS = Y * Z
ONE = 8
TWO = 4
MID = (-3, -2, 2, 3)
LAG = 5
LEAD = 5
FG_STEPS = (3, -1, 3, 2, 1)
Z_STEPS = {1: 1, 2: 2, 3: 3, 4: 1, 5: 2, 6: 3}
MID_ROWS = len(MID) * ONE
FAR_ROWS = (Z - 1) * Y * TWO
COARSE = MID_ROWS + FAR_ROWS
NEAR = 3 * ROWS
KEYS = NEAR + COARSE
PADDED = 4 * ROWS
CHUNK = 48
MASKED = -1e30
F32 = jnp.float32
BF16 = jnp.bfloat16
MESH = pl.DeviceIdType.MESH


def dot(a, b, ca, cb):
    return lax.dot_general(a, b, (((ca,), (cb,)), ((), ())), preferred_element_type=F32)


def group_max(x):
    return jnp.max(x.reshape(x.shape[0] // 8, 8, x.shape[1]), axis=0)


def group_sum(x):
    return jnp.sum(x.reshape(x.shape[0] // 8, 8, x.shape[1]), axis=0)


def kernel(
    groups, parts, z_parts,
    q_hbm, k_hbm, v_hbm, do_hbm, r1_hbm, r2_hbm,
    stage,
    own_in, near_kv, near_send, near_recv, own_grad, coarse,
    c1_send, c1_recv, c2_send, c2_recv, z_send, mg_send, mg_recv, fg_send, fg_recv, yg_send, yg_recv,
    fg_own, r1_in, r2_in, restrict, pack, gathered, bias, q_stack, do_stack, key_t, value_t, do_t, score, dots, stats, prob, grad,
    att_t, gq_t, coarse_sum, restrict_t,
    load_sem, near_send_sem, near_recv_sem, grad_send_sem, grad_recv_sem,
    c1_send_sem, c1_recv_sem, c2_send_sem, c2_recv_sem, z_send_sem, z_recv_sem, z_back_sem,
    mg_send_sem, mg_recv_sem, fg_send_sem, fg_recv_sem, yg_send_sem, yg_recv_sem,
):
    width = groups * PAIR
    half = width // 2
    part_groups = groups // parts
    part_width = width // parts
    z_groups = groups // z_parts
    z_width = width // z_parts
    me = lax.axis_index("seq")
    z = me // Y
    y = me % Y
    way = 1 - 2 * (y // 2)

    def at_block(offset):
        return lax.rem(me + offset + BLOCKS, BLOCKS)

    def at_y(offset):
        return z * Y + lax.rem(y + offset + Y, Y)

    def at_z(offset):
        return lax.rem(z + offset + Z, Z) * Y + y

    def remote(src, dst, send_sem, recv_sem, to):
        return pltpu.make_async_remote_copy(
            src_ref=src, dst_ref=dst, send_sem=send_sem, recv_sem=recv_sem,
            device_id={"seq": to}, device_id_type=MESH,
        )

    def columns(index, size):
        return pl.ds(pl.multiple_of(index * size, size), size)

    barrier = pltpu.get_barrier_semaphore()
    partners = [at_block(o) for o in (-1, 1) + MID]
    partners += [at_y(j) for j in range(1, Y)] + [at_z(k) for k in (-3, -2, -1, 1, 2, 3)]
    for partner in partners:
        pl.semaphore_signal(barrier, inc=1, device_id={"seq": partner}, device_id_type=MESH)
    loads = [
        pltpu.make_async_copy(src, own_in.at[i], load_sem.at[i])
        for i, src in enumerate((k_hbm, v_hbm, q_hbm, do_hbm))
    ]
    loads.append(pltpu.make_async_copy(r1_hbm, r1_in, load_sem.at[4]))
    loads.append(pltpu.make_async_copy(r2_hbm, r2_in, load_sem.at[5]))
    for load in loads:
        load.start()
    pl.semaphore_wait(barrier, len(partners))

    def near_copy(side, which, g):
        src = (k_hbm, v_hbm)[which].at[:, columns(g, PAIR)]
        return remote(
            src, near_kv.at[side, g, pl.ds(which * ROWS, ROWS)],
            near_send_sem.at[side, which, g], near_recv_sem.at[side, which, g],
            at_block(1 if side == 0 else -1),
        )

    def send_near(side, g, carry):
        for which in range(2):
            near_copy(side, which, g).start()
        return carry

    for side in range(2):
        send_near(side, 0, 0)

    restrict[...] = jnp.zeros_like(restrict)
    loads[4].wait()
    loads[5].wait()
    restrict[0:ONE, :] = r1_in[...].astype(F32)
    restrict[ONE:ONE + TWO, :] = r2_in[...].astype(F32)
    restrict_b = restrict[...].astype(BF16)
    restrict_t[...] = jnp.concatenate([restrict[...], restrict[...]], axis=0).T.astype(BF16)
    loads[0].wait()
    loads[1].wait()
    coarse_k = dot(restrict_b, own_in[0], 1, 0)
    coarse_v = dot(restrict_b, own_in[1], 1, 0)
    gathered[0] = coarse_k
    gathered[1] = coarse_v

    def pack_rows(first):
        for which in range(2):
            for side in range(2):
                row = TWO * (2 * which + side)
                pack[row:row + TWO, :] = gathered[which, first:first + TWO, side * half:(side + 1) * half]
        return pack[...].astype(BF16)

    c2_send[...] = pack_rows(ONE)
    c1_send[...] = jnp.concatenate([coarse_k[0:ONE], coarse_v[0:ONE]], axis=0).astype(BF16)

    first_y, last_y, relay = y == 0, y == Y - 1, (y == 1) | (y == 2)
    same_z = 2 - y // 2

    def c2_copy(j):
        return remote(c2_send, c2_recv.at[j - 1], c2_send_sem.at[j - 1], c2_recv_sem.at[j - 1], at_y(j))

    def c1_copy(i):
        to, slot = ((at_y(2), 3 - same_z), (at_block(3), 0), (at_block(-3), 3))[i]
        return remote(c1_send, c1_recv.at[slot], c1_send_sem.at[i], c1_recv_sem.at[slot], to)

    def c1_on_z():
        slot = 3 - same_z
        return remote(
            c1_recv.at[same_z], c1_recv.at[slot], c1_send_sem.at[3], c1_recv_sem.at[slot], at_z(way)
        )

    def c2_on_y():
        slot = 2 * (y - 1)
        return remote(c2_recv.at[1], c2_recv.at[slot], c2_send_sem.at[3], c2_recv_sem.at[slot], at_y(2 * y - 3))

    def c1_on_y():
        slot = 3 * (2 - y)
        return remote(
            c1_recv.at[same_z], c1_recv.at[slot], c1_send_sem.at[4], c1_recv_sem.at[slot], at_y(2 * y - 3)
        )

    def small_copies(act):
        act(c2_copy(2))
        act(c1_copy(0))

        @pl.when(jnp.logical_not(first_y))
        def _():
            act(c2_copy(3))
            act(c1_copy(1))

        @pl.when(jnp.logical_not(last_y))
        def _():
            act(c2_copy(1))
            act(c1_copy(2))

    small_copies(lambda copy: copy.start())

    held = (y == 2, y == 1)
    on_z = (last_y, first_y)
    some = min(4, groups)
    for side in range(2):
        send_near(side, 1, 0)

        @pl.when(jnp.logical_not(held[side]))
        def _(side=side):
            lax.fori_loop(2, some, functools.partial(send_near, side), 0)

        @pl.when(jnp.logical_not(held[side] | on_z[side]))
        def _(side=side):
            lax.fori_loop(some, groups, functools.partial(send_near, side), 0)

    def c2_arrival(j):
        remote(c2_send, c2_recv.at[j - 1], c2_send_sem.at[j - 1], c2_recv_sem.at[j - 1], at_y(j)).wait_recv()

    def c1_arrival(slot):
        remote(c1_send, c1_recv.at[slot], c1_send_sem.at[0], c1_recv_sem.at[slot], at_y(2)).wait_recv()

    c2_arrival(2)
    c1_arrival(same_z)

    @pl.when(relay)
    def _():
        c2_on_y().start()
        c1_on_y().start()

    for side in range(2):
        @pl.when(held[side])
        def _(side=side):
            lax.fori_loop(2, groups, functools.partial(send_near, side), 0)

    c1_on_z().start()
    row = lax.broadcasted_iota(jnp.int32, (COARSE, ROWS), 0)
    slot = row >> 3
    offset = jnp.where(slot == 0, -3, jnp.where(slot == 1, -2, jnp.where(slot == 2, 2, 3)))
    place = me + offset
    middle = jnp.where((place >= 0) & (place < BLOCKS), math.log(32.0), MASKED)
    far_row = row - MID_ROWS
    far_z = (z - way * ((far_row >> 4) + 1)) & (Z - 1)
    far_y = (y - ((far_row >> 2) & 3)) & (Y - 1)
    distance = jnp.abs(far_z * Y + far_y - me)
    far = jnp.where(distance >= 4, math.log(64.0), MASKED)
    bias[...] = jnp.where(row < MID_ROWS, middle, far)
    left_bias = jnp.where(me >= 1, 0.0, MASKED).astype(F32)
    right_bias = jnp.where(me < BLOCKS - 1, 0.0, MASKED).astype(F32)
    for which in range(2):
        coarse[which, COARSE:ROWS, :] = jnp.zeros((ROWS - COARSE, width), BF16)
    prob[KEYS:PADDED, :] = jnp.zeros((PADDED - KEYS, 2 * ROWS), BF16)
    grad[KEYS:PADDED, :] = jnp.zeros((PADDED - KEYS, 2 * ROWS), BF16)

    c2_arrival(1)
    c2_arrival(3)

    for j in range(Y):
        if j == 0:
            block = c2_send[...]
        else:
            block = c2_recv[j - 1]
        pack[...] = block.astype(F32)
        for which in range(2):
            for side in range(2):
                first = TWO * (2 * which + side)
                gathered[which, TWO * j:TWO * (j + 1), side * half:(side + 1) * half] = pack[first:first + TWO, :]
    z_send[...] = gathered[...].astype(BF16)

    def far_slot(k):
        return pl.ds(MID_ROWS + (k - 1) * Y * TWO, Y * TWO)

    z_back = remote(z_send, coarse.at[:, far_slot(7), :], z_back_sem.at[0], z_back_sem.at[1], at_z(-way))
    z_back.start()
    for side in range(2):
        @pl.when(on_z[side])
        def _(side=side):
            lax.fori_loop(some, groups, functools.partial(send_near, side), 0)

    def z_copy(k, part):
        cols = columns(part, z_width)
        src = coarse.at[:, far_slot(3), cols] if k > 3 else z_send.at[:, :, cols]
        return remote(
            src, coarse.at[:, far_slot(k), cols],
            z_send_sem.at[k - 1, part], z_recv_sem.at[k - 1, part], at_z(way * Z_STEPS[k]),
        )

    def z_own(part):
        for k in (3, 2, 1):
            z_copy(k, part).start()

    def z_forward(part):
        z_copy(3, part).wait_recv()
        for k in (6, 5, 4):
            z_copy(k, part).start()

    z_own(0)
    z_own(1)
    for slot in (0, 3, 3 - same_z):
        c1_arrival(slot)
    for which in range(2):
        rows = [c1_recv[s].astype(F32)[which * ONE:(which + 1) * ONE] for s in range(len(MID))]
        coarse[which, 0:MID_ROWS, :] = jnp.concatenate(rows, axis=0).astype(BF16)
    loads[2].wait()
    loads[3].wait()
    def grad_copy(side, g):
        return remote(
            near_send.at[side, g], near_recv.at[1 - side, g],
            grad_send_sem.at[side, g], grad_recv_sem.at[1 - side, g],
            at_block(-1 if side == 0 else 1),
        )

    def mg_copy(s, part):
        cols = columns(part, part_width)
        return remote(
            mg_send.at[s, :, cols], mg_recv.at[s, :, cols],
            mg_send_sem.at[part, s], mg_recv_sem.at[part, s], at_block(MID[s]),
        )

    def fg_copy(i, g):
        cols = columns(g, PAIR)
        slots = pl.ds(0, 3) if i == 0 else pl.ds(2 + i, 1)
        return remote(
            fg_send.at[slots, :, :, cols], fg_recv.at[slots, :, :, cols],
            fg_send_sem.at[i, g], fg_recv_sem.at[i, g], at_z(way * FG_STEPS[i]),
        )

    def sum_first(g):
        cols = columns(g, PAIR)
        for i, k in enumerate((2, 3, 4, 1)):
            fg_send[i, :, :, cols] = fg_own[k - 1, :, :, cols].astype(BF16)
        for i in range(2):
            fg_copy(i, g).start()

    def sum_second(g):
        cols = columns(g, PAIR)
        fg_copy(0, g).wait_recv()
        for i in range(3):
            total = fg_own[4 + i, :, :, cols] + fg_recv[i, :, :, cols].astype(F32)
            fg_send[4 + i, :, :, cols] = total.astype(BF16)
            fg_copy(2 + i, g).start()

    def heads(g):
        cols = columns(g, PAIR)
        return lax.rem(g, LEAD), cols, own_in[2, :, cols], own_in[3, :, cols]

    def near_part(g):
        slot, cols, q, do = heads(g)
        for side in range(2):
            for which in range(2):
                near_copy(side, which, g).wait_recv()
        q = q.astype(F32) * (1.0 / math.sqrt(HEAD_DIM))
        do = do.astype(F32)
        lane = lax.broadcasted_iota(jnp.int32, (ROWS, PAIR), 1)
        for h in range(2):
            mine = (lane >= HEAD_DIM) if h else (lane < HEAD_DIM)
            q_stack[slot, h * ROWS:(h + 1) * ROWS, :] = jnp.where(mine, q, 0.0).astype(BF16)
            do_stack[slot, h * ROWS:(h + 1) * ROWS, :] = jnp.where(mine, do, 0.0).astype(BF16)
        do_t[slot] = do.T
        keys, values = (
            (
                near_kv[0, g, which * ROWS:(which + 1) * ROWS, :],
                own_in[which, :, cols],
                near_kv[1, g, which * ROWS:(which + 1) * ROWS, :],
            )
            for which in range(2)
        )
        for i in range(3):
            key_t[slot, :, i * ROWS:(i + 1) * ROWS] = keys[i].T
            value_t[slot, :, i * ROWS:(i + 1) * ROWS] = values[i].T
        biases = (left_bias, None, right_bias)
        for h in range(2):
            qh = q_stack[slot, h * ROWS:(h + 1) * ROWS, :]
            doh = do_stack[slot, h * ROWS:(h + 1) * ROWS, :]
            top = None
            for i in range(3):
                s = dot(keys[i], qh, 1, 1)
                if biases[i] is not None:
                    s = s + biases[i]
                score[slot, h, i * ROWS:(i + 1) * ROWS, :] = s
                m = group_max(s)
                top = m if top is None else jnp.maximum(top, m)
                dots[slot, h, i * ROWS:(i + 1) * ROWS, :] = dot(values[i], doh, 1, 1)
            top = jnp.max(top, axis=0, keepdims=True)
            total = jnp.zeros((8, ROWS), F32)
            for c in range(0, NEAR, CHUNK):
                p = jnp.exp(score[slot, h, c:c + CHUNK, :] - top)
                score[slot, h, c:c + CHUNK, :] = p
                total = total + group_sum(p)
            stats[slot, h, 0] = jnp.broadcast_to(top, (8, ROWS))
            stats[slot, h, 1] = total

    def pair(g):
        slot, cols, _, _ = heads(g)
        part = g // part_groups

        @pl.when(g == 0)
        def _():
            z_back.wait_recv()

        @pl.when(g % z_groups == 0)
        def _():
            for k in (1, 2, 4, 5, 6):
                z_copy(k, g // z_groups).wait_recv()

        @pl.when(g + 2 < z_parts)
        def _():
            z_forward(g + 2)

        key = coarse[0, :, cols]
        value = coarse[1, :, cols]
        key_t[slot, :, NEAR:PADDED] = key.T
        value_t[slot, :, NEAR:PADDED] = value.T
        for h in range(2):
            qh = q_stack[slot, h * ROWS:(h + 1) * ROWS, :]
            doh = do_stack[slot, h * ROWS:(h + 1) * ROWS, :]
            lanes = slice(h * ROWS, (h + 1) * ROWS)
            s = dot(key[:COARSE], qh, 1, 1) + bias[...]
            dots[slot, h, NEAR:KEYS, :] = dot(value[:COARSE], doh, 1, 1)
            near_top = stats[slot, h, 0, 0:1, :]
            top = jnp.maximum(near_top, jnp.max(group_max(s), axis=0, keepdims=True))
            p = jnp.exp(s - top)
            score[slot, h, NEAR:KEYS, :] = p
            shrink = jnp.exp(near_top - top)
            total = shrink * jnp.sum(stats[slot, h, 1], axis=0, keepdims=True)
            inverse = 1.0 / (total + jnp.sum(group_sum(p), axis=0, keepdims=True))
            near_inverse = shrink * inverse
            for c in range(0, KEYS, CHUNK):
                p = score[slot, h, c:c + CHUNK, :] * (near_inverse if c < NEAR else inverse)
                prob[c:c + CHUNK, lanes] = p.astype(BF16)
            head = slice(h * HEAD_DIM, (h + 1) * HEAD_DIM)
            att = dot(value_t[slot, head, :], prob[:, lanes], 1, 0).astype(BF16).astype(F32)
            att_t[head, :] = att
            delta = jnp.sum(att * do_t[slot, head, :], axis=0, keepdims=True)
            for c in range(0, KEYS, CHUNK):
                p = score[slot, h, c:c + CHUNK, :] * (near_inverse if c < NEAR else inverse)
                grad[c:c + CHUNK, lanes] = (p * (dots[slot, h, c:c + CHUNK, :] - delta)).astype(BF16)
        def key_grads(first, n):
            return (
                dot(grad[first:first + n, :], q_stack[slot], 1, 0),
                dot(prob[first:first + n, :], do_stack[slot], 1, 0),
            )

        dk, dv = key_grads(NEAR, COARSE)
        for s in range(len(MID)):
            both = jnp.concatenate([dk[s * ONE:(s + 1) * ONE], dv[s * ONE:(s + 1) * ONE]], axis=0)
            mg_send[s, :, cols] = both.astype(BF16)
        for k in range(1, Z):
            first = MID_ROWS + (k - 1) * Y * TWO
            fg_own[k - 1, 0, :, cols] = dk[first:first + Y * TWO]
            fg_own[k - 1, 1, :, cols] = dv[first:first + Y * TWO]
        sum_first(g)

        @pl.when(g >= LAG)
        def _():
            sum_second(g - LAG)


        for side in range(2):
            dk, dv = key_grads(2 * ROWS * side, ROWS)
            near_send[side, g, 0:ROWS, :] = dk.astype(BF16)
            near_send[side, g, ROWS:2 * ROWS, :] = dv.astype(BF16)
            grad_copy(side, g).start()
        @pl.when(g % part_groups == part_groups - 1)
        def _():
            for s in range(len(MID)):
                mg_copy(s, part).start()

        dk, dv = key_grads(ROWS, ROWS)
        own_grad[g, 0:ROWS, :] = dk
        own_grad[g, ROWS:2 * ROWS, :] = dv
        for h in range(2):
            head = slice(h * HEAD_DIM, (h + 1) * HEAD_DIM)
            gq = dot(key_t[slot, head, :], grad[:, h * ROWS:(h + 1) * ROWS], 1, 0)
            gq_t[head, :] = gq * (1.0 / math.sqrt(HEAD_DIM))
        stage[0, :, cols] = att_t[...].T.astype(BF16)
        stage[1, :, cols] = gq_t[...].T.astype(BF16)
    lead = min(LEAD, groups)

    def turn(t, carry):
        @pl.when(t >= lead)
        def _():
            pair(t - lead)

        @pl.when(t < groups)
        def _():
            near_part(t)

        for part in range(2):
            @pl.when(t == min(part + 1, lead - 1))
            def _(part=part):
                z_forward(part)
                if part + 2 < z_parts:
                    z_own(part + 2)

        return carry

    lax.fori_loop(0, groups + lead, turn, 0)

    def add_near(g):
        for side in range(2):
            grad_copy(side, g).wait_recv()
        own_grad[g] = own_grad[g] + near_recv[0, g].astype(F32) + near_recv[1, g].astype(F32)

    def far_arrival(g, carry):
        for i in range(1, 5):
            fg_copy(i, g).wait_recv()
        return carry

    for g in range(max(groups - LAG, 0), groups):
        sum_second(g)
    lax.fori_loop(0, groups, far_arrival, 0)
    for which in range(2):
        total = fg_recv[3, which].astype(F32)
        for i in range(4, 7):
            total = total + fg_recv[i, which].astype(F32)
        gathered[which] = total
    yg_copies = [
        remote(yg_send.at[j - 1], yg_recv.at[j - 1], yg_send_sem.at[j - 1], yg_recv_sem.at[j - 1], at_y(-j))
        for j in range(1, Y)
    ]
    for j in range(1, Y):
        yg_send[j - 1] = pack_rows(TWO * j)
        yg_copies[j - 1].start()

    def drain(g, carry):
        for side in range(2):
            for which in range(2):
                near_copy(side, which, g).wait_send()
        for i in range(5):
            fg_copy(i, g).wait_send()
        return carry

    lax.fori_loop(0, groups, drain, 0)
    z_back.wait_send()
    for part in range(z_parts):
        for k in range(1, Z - 1):
            z_copy(k, part).wait_send()
    small_copies(lambda copy: copy.wait_send())
    c1_on_z().wait_send()

    @pl.when(relay)
    def _():
        c2_on_y().wait_send()
        c1_on_y().wait_send()

    for g in range(groups):
        add_near(g)
    for part in range(parts):
        for s in range(len(MID)):
            mg_copy(s, part).wait_recv()
    middle_sum = mg_recv[0].astype(F32)
    for s in range(1, len(MID)):
        middle_sum = middle_sum + mg_recv[s].astype(F32)
    coarse_sum[...] = jnp.zeros_like(coarse_sum)
    for which in range(2):
        coarse_sum[which, 0:ONE, :] = middle_sum[which * ONE:(which + 1) * ONE]
        coarse_sum[which, ONE:ONE + TWO, :] = gathered[which, 0:TWO, :]
    for j in range(1, Y):
        yg_copies[j - 1].wait_recv()
        pack[...] = yg_recv[j - 1].astype(F32)
        for which in range(2):
            for side in range(2):
                first = TWO * (2 * which + side)
                cols = slice(side * half, (side + 1) * half)
                coarse_sum[which, ONE:ONE + TWO, cols] = (
                    coarse_sum[which, ONE:ONE + TWO, cols] + pack[first:first + TWO, :]
                )


    for g in range(groups):
        cols = slice(g * PAIR, (g + 1) * PAIR)
        for which in range(2):
            wide = coarse_sum[which, :, cols]
            high = wide.astype(BF16)
            low = (wide - high.astype(F32)).astype(BF16)
            both = jnp.concatenate([high, low], axis=0)
            total = own_grad[g, which * ROWS:(which + 1) * ROWS, :] + dot(restrict_t[...], both, 1, 0)
            stage[2 + which, :, cols] = total.astype(BF16)
    for g in range(groups):
        for side in range(2):
            grad_copy(side, g).wait_send()
    for copy in yg_copies:
        copy.wait_send()
    for part in range(parts):
        for s in range(len(MID)):
            mg_copy(s, part).wait_send()


def per_device(queries, keys, values, cotangent, restrict_one, restrict_two):
    rows, width = queries.shape
    groups = width // PAIR
    parts = 2
    z_parts = min(groups, 4)
    hbm = pl.BlockSpec(memory_space=pl.ANY)
    vmem = pl.BlockSpec(memory_space=pltpu.VMEM)
    dma = pltpu.SemaphoreType.DMA
    mid = len(MID)
    scratch = [
        pltpu.VMEM((4, ROWS, width), BF16),
        pltpu.VMEM((2, groups, 2 * ROWS, PAIR), BF16),
        pltpu.VMEM((2, groups, 2 * ROWS, PAIR), BF16),
        pltpu.VMEM((2, groups, 2 * ROWS, PAIR), BF16),
        pltpu.VMEM((groups, 2 * ROWS, PAIR), F32),
        pltpu.VMEM((2, ROWS, width), BF16),
        pltpu.VMEM((16, width), BF16),
        pltpu.VMEM((mid, 16, width), BF16),
        pltpu.VMEM((16, width // 2), BF16),
        pltpu.VMEM((Y - 1, 16, width // 2), BF16),
        pltpu.VMEM((2, 16, width), BF16),
        pltpu.VMEM((mid, 16, width), BF16),
        pltpu.VMEM((mid, 16, width), BF16),
        pltpu.VMEM((Z - 1, 2, 16, width), BF16),
        pltpu.VMEM((Z - 1, 2, 16, width), BF16),
        pltpu.VMEM((Y - 1, 16, width // 2), BF16),
        pltpu.VMEM((Y - 1, 16, width // 2), BF16),
        pltpu.VMEM((Z - 1, 2, 16, width), F32),
        pltpu.VMEM((ONE, ROWS), BF16),
        pltpu.VMEM((TWO, ROWS), BF16),
        pltpu.VMEM((16, ROWS), F32),
        pltpu.VMEM((16, width // 2), F32),
        pltpu.VMEM((2, 16, width), F32),
        pltpu.VMEM((COARSE, ROWS), F32),
        pltpu.VMEM((LEAD, 2 * ROWS, PAIR), BF16),
        pltpu.VMEM((LEAD, 2 * ROWS, PAIR), BF16),
        pltpu.VMEM((LEAD, PAIR, PADDED), BF16),
        pltpu.VMEM((LEAD, PAIR, PADDED), BF16),
        pltpu.VMEM((LEAD, PAIR, ROWS), F32),
        pltpu.VMEM((LEAD, 2, KEYS, ROWS), F32),
        pltpu.VMEM((LEAD, 2, KEYS, ROWS), F32),
        pltpu.VMEM((LEAD, 2, 2, 8, ROWS), F32),
        pltpu.VMEM((PADDED, 2 * ROWS), BF16),
        pltpu.VMEM((PADDED, 2 * ROWS), BF16),
        pltpu.VMEM((PAIR, ROWS), F32),
        pltpu.VMEM((PAIR, ROWS), F32),
        pltpu.VMEM((2, 16, width), F32),
        pltpu.VMEM((ROWS, 32), BF16),
        dma((6,)),
        dma((2, 2, groups)), dma((2, 2, groups)),
        dma((2, groups)), dma((2, groups)),
        dma((5,)), dma((mid,)),
        dma((4,)), dma((Y - 1,)),
        dma((Z - 2, z_parts)), dma((Z - 2, z_parts)), dma((2,)),
        dma((parts, mid)), dma((parts, mid)),
        dma((5, groups)), dma((5, groups)),
        dma((Y - 1,)), dma((Y - 1,)),
    ]
    stage = pl.pallas_call(
        functools.partial(kernel, groups, parts, z_parts),
        out_shape=pltpu.VMEM((4, ROWS, width), BF16),
        in_specs=[hbm] * 6,
        out_specs=vmem,
        scratch_shapes=scratch,
        compiler_params=pltpu.CompilerParams(
            collective_id=0, has_side_effects=True, vmem_limit_bytes=56 * 1024 * 1024
        ),
    )(queries, keys, values, cotangent, restrict_one, restrict_two)
    return tuple(stage[i] for i in range(4))


def solution(mesh):
    rows = P(("prompt", "seq"), None)
    return jax.shard_map(
        per_device, mesh=mesh, in_specs=(rows, rows, rows, rows, P(), P()),
        out_specs=(rows, rows, rows, rows), check_vma=False,
    )
```

```python
import functools
import math

import jax
import jax.numpy as jnp
from jax import lax
from jax.experimental import pallas as pl
from jax.experimental.pallas import tpu as pltpu
from jax.sharding import PartitionSpec as P

HEAD_DIM = 64
ROWS = 256
PAIR = 128
Y = 4
Z = 8
BLOCKS = Y * Z
ONE = 8
TWO = 4
MID = (-3, -2, 2, 3)
LAG = 8
LEAD = 5
FG_STEPS = (3, -1, 3, 2, 1)
Z_STEPS = {1: 1, 2: 2, 3: 3, 4: 1, 5: 2, 6: 3}
MID_ROWS = len(MID) * ONE
FAR_ROWS = (Z - 1) * Y * TWO
COARSE = MID_ROWS + FAR_ROWS
NEAR = 3 * ROWS
KEYS = NEAR + COARSE
PADDED = 4 * ROWS
CHUNK = 48
MASKED = -1e30
F32 = jnp.float32
BF16 = jnp.bfloat16
MESH = pl.DeviceIdType.MESH


def dot(a, b, ca, cb):
    return lax.dot_general(a, b, (((ca,), (cb,)), ((), ())), preferred_element_type=F32)


def group_max(x):
    return jnp.max(x.reshape(x.shape[0] // 8, 8, x.shape[1]), axis=0)


def group_sum(x):
    return jnp.sum(x.reshape(x.shape[0] // 8, 8, x.shape[1]), axis=0)


def kernel(
    groups, parts, z_parts,
    q_hbm, k_hbm, v_hbm, do_hbm, r1_hbm, r2_hbm,
    stage,
    own_in, near_kv, near_send, near_recv, own_grad, coarse,
    c1_send, c1_recv, c2_send, c2_recv, z_send, mg_send, mg_recv, fg_send, fg_recv, yg_send, yg_recv,
    fg_own, r1_in, r2_in, restrict, pack, gathered, bias, q_stack, do_stack, key_t, value_t, do_t, score, dots, stats, prob, grad,
    att_t, gq_t, coarse_sum, restrict_t,
    load_sem, near_send_sem, near_recv_sem, grad_send_sem, grad_recv_sem,
    c1_send_sem, c1_recv_sem, c2_send_sem, c2_recv_sem, z_send_sem, z_recv_sem, z_back_sem,
    mg_send_sem, mg_recv_sem, fg_send_sem, fg_recv_sem, yg_send_sem, yg_recv_sem,
):
    width = groups * PAIR
    half = width // 2
    part_groups = groups // parts
    part_width = width // parts
    z_groups = groups // z_parts
    z_width = width // z_parts
    me = lax.axis_index("seq")
    z = me // Y
    y = me % Y
    way = 1 - 2 * (y // 2)

    def at_block(offset):
        return lax.rem(me + offset + BLOCKS, BLOCKS)

    def at_y(offset):
        return z * Y + lax.rem(y + offset + Y, Y)

    def at_z(offset):
        return lax.rem(z + offset + Z, Z) * Y + y

    def remote(src, dst, send_sem, recv_sem, to):
        return pltpu.make_async_remote_copy(
            src_ref=src, dst_ref=dst, send_sem=send_sem, recv_sem=recv_sem,
            device_id={"seq": to}, device_id_type=MESH,
        )

    def columns(index, size):
        return pl.ds(pl.multiple_of(index * size, size), size)

    barrier = pltpu.get_barrier_semaphore()
    partners = [at_block(o) for o in (-1, 1) + MID]
    partners += [at_y(j) for j in range(1, Y)] + [at_z(k) for k in (-3, -2, -1, 1, 2, 3)]
    for partner in partners:
        pl.semaphore_signal(barrier, inc=1, device_id={"seq": partner}, device_id_type=MESH)
    loads = [
        pltpu.make_async_copy(src, own_in.at[i], load_sem.at[i])
        for i, src in enumerate((k_hbm, v_hbm, q_hbm, do_hbm))
    ]
    loads.append(pltpu.make_async_copy(r1_hbm, r1_in, load_sem.at[4]))
    loads.append(pltpu.make_async_copy(r2_hbm, r2_in, load_sem.at[5]))
    for load in loads:
        load.start()
    pl.semaphore_wait(barrier, len(partners))

    def near_copy(side, which, g):
        src = (k_hbm, v_hbm)[which].at[:, columns(g, PAIR)]
        return remote(
            src, near_kv.at[side, g, pl.ds(which * ROWS, ROWS)],
            near_send_sem.at[side, which, g], near_recv_sem.at[side, which, g],
            at_block(1 if side == 0 else -1),
        )

    def send_near(side, g, carry):
        for which in range(2):
            near_copy(side, which, g).start()
        return carry

    for side in range(2):
        send_near(side, 0, 0)

    restrict[...] = jnp.zeros_like(restrict)
    loads[4].wait()
    loads[5].wait()
    restrict[0:ONE, :] = r1_in[...].astype(F32)
    restrict[ONE:ONE + TWO, :] = r2_in[...].astype(F32)
    restrict_b = restrict[...].astype(BF16)
    restrict_t[...] = jnp.concatenate([restrict[...], restrict[...]], axis=0).T.astype(BF16)
    loads[0].wait()
    loads[1].wait()
    coarse_k = dot(restrict_b, own_in[0], 1, 0)
    coarse_v = dot(restrict_b, own_in[1], 1, 0)
    gathered[0] = coarse_k
    gathered[1] = coarse_v

    def pack_rows(first):
        for which in range(2):
            for side in range(2):
                row = TWO * (2 * which + side)
                pack[row:row + TWO, :] = gathered[which, first:first + TWO, side * half:(side + 1) * half]
        return pack[...].astype(BF16)

    c2_send[...] = pack_rows(ONE)
    c1_send[...] = jnp.concatenate([coarse_k[0:ONE], coarse_v[0:ONE]], axis=0).astype(BF16)

    first_y, last_y, relay = y == 0, y == Y - 1, (y == 1) | (y == 2)
    same_z = 2 - y // 2

    def c2_copy(j):
        return remote(c2_send, c2_recv.at[j - 1], c2_send_sem.at[j - 1], c2_recv_sem.at[j - 1], at_y(j))

    def c1_copy(i):
        to, slot = ((at_y(2), 3 - same_z), (at_block(3), 0), (at_block(-3), 3))[i]
        return remote(c1_send, c1_recv.at[slot], c1_send_sem.at[i], c1_recv_sem.at[slot], to)

    def c1_on_z():
        slot = 3 - same_z
        return remote(
            c1_recv.at[same_z], c1_recv.at[slot], c1_send_sem.at[3], c1_recv_sem.at[slot], at_z(way)
        )

    def c2_on_y():
        slot = 2 * (y - 1)
        return remote(c2_recv.at[1], c2_recv.at[slot], c2_send_sem.at[3], c2_recv_sem.at[slot], at_y(2 * y - 3))

    def c1_on_y():
        slot = 3 * (2 - y)
        return remote(
            c1_recv.at[same_z], c1_recv.at[slot], c1_send_sem.at[4], c1_recv_sem.at[slot], at_y(2 * y - 3)
        )

    def small_copies(act):
        act(c2_copy(2))
        act(c1_copy(0))

        @pl.when(jnp.logical_not(first_y))
        def _():
            act(c2_copy(3))
            act(c1_copy(1))

        @pl.when(jnp.logical_not(last_y))
        def _():
            act(c2_copy(1))
            act(c1_copy(2))

    small_copies(lambda copy: copy.start())

    held = (y == 2, y == 1)
    on_z = (last_y, first_y)
    some = min(4, groups)
    for side in range(2):
        send_near(side, 1, 0)

        @pl.when(jnp.logical_not(held[side]))
        def _(side=side):
            lax.fori_loop(2, some, functools.partial(send_near, side), 0)

        @pl.when(jnp.logical_not(held[side] | on_z[side]))
        def _(side=side):
            lax.fori_loop(some, groups, functools.partial(send_near, side), 0)

    def c2_arrival(j):
        remote(c2_send, c2_recv.at[j - 1], c2_send_sem.at[j - 1], c2_recv_sem.at[j - 1], at_y(j)).wait_recv()

    def c1_arrival(slot):
        remote(c1_send, c1_recv.at[slot], c1_send_sem.at[0], c1_recv_sem.at[slot], at_y(2)).wait_recv()

    c2_arrival(2)
    c1_arrival(same_z)

    @pl.when(relay)
    def _():
        c2_on_y().start()
        c1_on_y().start()

    for side in range(2):
        @pl.when(held[side])
        def _(side=side):
            lax.fori_loop(2, groups, functools.partial(send_near, side), 0)

    c1_on_z().start()
    row = lax.broadcasted_iota(jnp.int32, (COARSE, ROWS), 0)
    slot = row >> 3
    offset = jnp.where(slot == 0, -3, jnp.where(slot == 1, -2, jnp.where(slot == 2, 2, 3)))
    place = me + offset
    middle = jnp.where((place >= 0) & (place < BLOCKS), math.log(32.0), MASKED)
    far_row = row - MID_ROWS
    far_z = (z - way * ((far_row >> 4) + 1)) & (Z - 1)
    far_y = (y - ((far_row >> 2) & 3)) & (Y - 1)
    distance = jnp.abs(far_z * Y + far_y - me)
    far = jnp.where(distance >= 4, math.log(64.0), MASKED)
    bias[...] = jnp.where(row < MID_ROWS, middle, far)
    left_bias = jnp.where(me >= 1, 0.0, MASKED).astype(F32)
    right_bias = jnp.where(me < BLOCKS - 1, 0.0, MASKED).astype(F32)
    for which in range(2):
        coarse[which, COARSE:ROWS, :] = jnp.zeros((ROWS - COARSE, width), BF16)
    prob[KEYS:PADDED, :] = jnp.zeros((PADDED - KEYS, 2 * ROWS), BF16)
    grad[KEYS:PADDED, :] = jnp.zeros((PADDED - KEYS, 2 * ROWS), BF16)

    c2_arrival(1)
    c2_arrival(3)

    for j in range(Y):
        if j == 0:
            block = c2_send[...]
        else:
            block = c2_recv[j - 1]
        pack[...] = block.astype(F32)
        for which in range(2):
            for side in range(2):
                first = TWO * (2 * which + side)
                gathered[which, TWO * j:TWO * (j + 1), side * half:(side + 1) * half] = pack[first:first + TWO, :]
    z_send[...] = gathered[...].astype(BF16)

    def far_slot(k):
        return pl.ds(MID_ROWS + (k - 1) * Y * TWO, Y * TWO)

    z_back = remote(z_send, coarse.at[:, far_slot(7), :], z_back_sem.at[0], z_back_sem.at[1], at_z(-way))
    z_back.start()
    for side in range(2):
        @pl.when(on_z[side])
        def _(side=side):
            lax.fori_loop(some, groups, functools.partial(send_near, side), 0)

    def z_copy(k, part):
        cols = columns(part, z_width)
        src = coarse.at[:, far_slot(3), cols] if k > 3 else z_send.at[:, :, cols]
        return remote(
            src, coarse.at[:, far_slot(k), cols],
            z_send_sem.at[k - 1, part], z_recv_sem.at[k - 1, part], at_z(way * Z_STEPS[k]),
        )

    def z_own(part):
        for k in (3, 2, 1):
            z_copy(k, part).start()

    def z_forward(part):
        z_copy(3, part).wait_recv()
        for k in (6, 5, 4):
            z_copy(k, part).start()

    z_own(0)
    z_own(1)
    for slot in (0, 3, 3 - same_z):
        c1_arrival(slot)
    for which in range(2):
        rows = [c1_recv[s].astype(F32)[which * ONE:(which + 1) * ONE] for s in range(len(MID))]
        coarse[which, 0:MID_ROWS, :] = jnp.concatenate(rows, axis=0).astype(BF16)
    loads[2].wait()
    loads[3].wait()
    def grad_copy(side, g):
        return remote(
            near_send.at[side, g], near_recv.at[1 - side, g],
            grad_send_sem.at[side, g], grad_recv_sem.at[1 - side, g],
            at_block(-1 if side == 0 else 1),
        )

    def mg_copy(s, part):
        cols = columns(part, part_width)
        return remote(
            mg_send.at[s, :, cols], mg_recv.at[s, :, cols],
            mg_send_sem.at[part, s], mg_recv_sem.at[part, s], at_block(MID[s]),
        )

    def fg_copy(i, g):
        cols = columns(g, PAIR)
        slots = pl.ds(0, 3) if i == 0 else pl.ds(2 + i, 1)
        return remote(
            fg_send.at[slots, :, :, cols], fg_recv.at[slots, :, :, cols],
            fg_send_sem.at[i, g], fg_recv_sem.at[i, g], at_z(way * FG_STEPS[i]),
        )

    def sum_first(g):
        cols = columns(g, PAIR)
        for i, k in enumerate((2, 3, 4, 1)):
            fg_send[i, :, :, cols] = fg_own[k - 1, :, :, cols].astype(BF16)
        for i in range(2):
            fg_copy(i, g).start()

    def sum_second(g):
        cols = columns(g, PAIR)
        fg_copy(0, g).wait_recv()
        for i in range(3):
            total = fg_own[4 + i, :, :, cols] + fg_recv[i, :, :, cols].astype(F32)
            fg_send[4 + i, :, :, cols] = total.astype(BF16)
            fg_copy(2 + i, g).start()

    def heads(g):
        cols = columns(g, PAIR)
        return lax.rem(g, LEAD), cols, own_in[2, :, cols], own_in[3, :, cols]

    def near_part(g):
        slot, cols, q, do = heads(g)
        for side in range(2):
            for which in range(2):
                near_copy(side, which, g).wait_recv()
        q = q.astype(F32) * (1.0 / math.sqrt(HEAD_DIM))
        do = do.astype(F32)
        lane = lax.broadcasted_iota(jnp.int32, (ROWS, PAIR), 1)
        for h in range(2):
            mine = (lane >= HEAD_DIM) if h else (lane < HEAD_DIM)
            q_stack[slot, h * ROWS:(h + 1) * ROWS, :] = jnp.where(mine, q, 0.0).astype(BF16)
            do_stack[slot, h * ROWS:(h + 1) * ROWS, :] = jnp.where(mine, do, 0.0).astype(BF16)
        do_t[slot] = do.T
        keys, values = (
            (
                near_kv[0, g, which * ROWS:(which + 1) * ROWS, :],
                own_in[which, :, cols],
                near_kv[1, g, which * ROWS:(which + 1) * ROWS, :],
            )
            for which in range(2)
        )
        for i in range(3):
            key_t[slot, :, i * ROWS:(i + 1) * ROWS] = keys[i].T
            value_t[slot, :, i * ROWS:(i + 1) * ROWS] = values[i].T
        biases = (left_bias, None, right_bias)
        for h in range(2):
            qh = q_stack[slot, h * ROWS:(h + 1) * ROWS, :]
            doh = do_stack[slot, h * ROWS:(h + 1) * ROWS, :]
            top = None
            for i in range(3):
                s = dot(keys[i], qh, 1, 1)
                if biases[i] is not None:
                    s = s + biases[i]
                score[slot, h, i * ROWS:(i + 1) * ROWS, :] = s
                m = group_max(s)
                top = m if top is None else jnp.maximum(top, m)
                dots[slot, h, i * ROWS:(i + 1) * ROWS, :] = dot(values[i], doh, 1, 1)
            top = jnp.max(top, axis=0, keepdims=True)
            total = jnp.zeros((8, ROWS), F32)
            for c in range(0, NEAR, CHUNK):
                p = jnp.exp(score[slot, h, c:c + CHUNK, :] - top)
                score[slot, h, c:c + CHUNK, :] = p
                total = total + group_sum(p)
            stats[slot, h, 0] = jnp.broadcast_to(top, (8, ROWS))
            stats[slot, h, 1] = total

    def pair(g):
        slot, cols, _, _ = heads(g)
        part = g // part_groups

        @pl.when(g == 0)
        def _():
            z_back.wait_recv()

        @pl.when(g % z_groups == 0)
        def _():
            for k in (1, 2, 4, 5, 6):
                z_copy(k, g // z_groups).wait_recv()

        @pl.when(g + 2 < z_parts)
        def _():
            z_forward(g + 2)

        key = coarse[0, :, cols]
        value = coarse[1, :, cols]
        key_t[slot, :, NEAR:PADDED] = key.T
        value_t[slot, :, NEAR:PADDED] = value.T
        for h in range(2):
            qh = q_stack[slot, h * ROWS:(h + 1) * ROWS, :]
            doh = do_stack[slot, h * ROWS:(h + 1) * ROWS, :]
            lanes = slice(h * ROWS, (h + 1) * ROWS)
            s = dot(key[:COARSE], qh, 1, 1) + bias[...]
            dots[slot, h, NEAR:KEYS, :] = dot(value[:COARSE], doh, 1, 1)
            near_top = stats[slot, h, 0, 0:1, :]
            top = jnp.maximum(near_top, jnp.max(group_max(s), axis=0, keepdims=True))
            p = jnp.exp(s - top)
            score[slot, h, NEAR:KEYS, :] = p
            shrink = jnp.exp(near_top - top)
            total = shrink * jnp.sum(stats[slot, h, 1], axis=0, keepdims=True)
            inverse = 1.0 / (total + jnp.sum(group_sum(p), axis=0, keepdims=True))
            near_inverse = shrink * inverse
            for c in range(0, KEYS, CHUNK):
                p = score[slot, h, c:c + CHUNK, :] * (near_inverse if c < NEAR else inverse)
                prob[c:c + CHUNK, lanes] = p.astype(BF16)
            head = slice(h * HEAD_DIM, (h + 1) * HEAD_DIM)
            att = dot(value_t[slot, head, :], prob[:, lanes], 1, 0).astype(BF16).astype(F32)
            att_t[head, :] = att
            delta = jnp.sum(att * do_t[slot, head, :], axis=0, keepdims=True)
            for c in range(0, KEYS, CHUNK):
                p = score[slot, h, c:c + CHUNK, :] * (near_inverse if c < NEAR else inverse)
                grad[c:c + CHUNK, lanes] = (p * (dots[slot, h, c:c + CHUNK, :] - delta)).astype(BF16)
        def key_grads(first, n):
            return (
                dot(grad[first:first + n, :], q_stack[slot], 1, 0),
                dot(prob[first:first + n, :], do_stack[slot], 1, 0),
            )

        dk, dv = key_grads(NEAR, COARSE)
        for s in range(len(MID)):
            both = jnp.concatenate([dk[s * ONE:(s + 1) * ONE], dv[s * ONE:(s + 1) * ONE]], axis=0)
            mg_send[s, :, cols] = both.astype(BF16)
        for k in range(1, Z):
            first = MID_ROWS + (k - 1) * Y * TWO
            fg_own[k - 1, 0, :, cols] = dk[first:first + Y * TWO]
            fg_own[k - 1, 1, :, cols] = dv[first:first + Y * TWO]
        sum_first(g)

        @pl.when(g >= LAG)
        def _():
            sum_second(g - LAG)


        for side in range(2):
            dk, dv = key_grads(2 * ROWS * side, ROWS)
            near_send[side, g, 0:ROWS, :] = dk.astype(BF16)
            near_send[side, g, ROWS:2 * ROWS, :] = dv.astype(BF16)
            grad_copy(side, g).start()
        @pl.when(g % part_groups == part_groups - 1)
        def _():
            for s in range(len(MID)):
                mg_copy(s, part).start()

        dk, dv = key_grads(ROWS, ROWS)
        own_grad[g, 0:ROWS, :] = dk
        own_grad[g, ROWS:2 * ROWS, :] = dv
        for h in range(2):
            head = slice(h * HEAD_DIM, (h + 1) * HEAD_DIM)
            gq = dot(key_t[slot, head, :], grad[:, h * ROWS:(h + 1) * ROWS], 1, 0)
            gq_t[head, :] = gq * (1.0 / math.sqrt(HEAD_DIM))
        stage[0, :, cols] = att_t[...].T.astype(BF16)
        stage[1, :, cols] = gq_t[...].T.astype(BF16)
    lead = min(LEAD, groups)

    def turn(t, carry):
        @pl.when(t >= lead)
        def _():
            pair(t - lead)

        @pl.when(t < groups)
        def _():
            near_part(t)

        for part in range(2):
            @pl.when(t == min(part + 1, lead - 1))
            def _(part=part):
                z_forward(part)
                if part + 2 < z_parts:
                    z_own(part + 2)

        return carry

    lax.fori_loop(0, groups + lead, turn, 0)

    def add_near(g):
        for side in range(2):
            grad_copy(side, g).wait_recv()
        own_grad[g] = own_grad[g] + near_recv[0, g].astype(F32) + near_recv[1, g].astype(F32)

    def far_arrival(g, carry):
        for i in range(1, 5):
            fg_copy(i, g).wait_recv()
        return carry

    for g in range(max(groups - LAG, 0), groups):
        sum_second(g)
    lax.fori_loop(0, groups, far_arrival, 0)
    for which in range(2):
        total = fg_recv[3, which].astype(F32)
        for i in range(4, 7):
            total = total + fg_recv[i, which].astype(F32)
        gathered[which] = total
    yg_copies = [
        remote(yg_send.at[j - 1], yg_recv.at[j - 1], yg_send_sem.at[j - 1], yg_recv_sem.at[j - 1], at_y(-j))
        for j in range(1, Y)
    ]
    for j in range(1, Y):
        yg_send[j - 1] = pack_rows(TWO * j)
        yg_copies[j - 1].start()

    def drain(g, carry):
        for side in range(2):
            for which in range(2):
                near_copy(side, which, g).wait_send()
        for i in range(5):
            fg_copy(i, g).wait_send()
        return carry

    lax.fori_loop(0, groups, drain, 0)
    z_back.wait_send()
    for part in range(z_parts):
        for k in range(1, Z - 1):
            z_copy(k, part).wait_send()
    small_copies(lambda copy: copy.wait_send())
    c1_on_z().wait_send()

    @pl.when(relay)
    def _():
        c2_on_y().wait_send()
        c1_on_y().wait_send()

    for g in range(groups):
        add_near(g)
    for part in range(parts):
        for s in range(len(MID)):
            mg_copy(s, part).wait_recv()
    middle_sum = mg_recv[0].astype(F32)
    for s in range(1, len(MID)):
        middle_sum = middle_sum + mg_recv[s].astype(F32)
    coarse_sum[...] = jnp.zeros_like(coarse_sum)
    for which in range(2):
        coarse_sum[which, 0:ONE, :] = middle_sum[which * ONE:(which + 1) * ONE]
        coarse_sum[which, ONE:ONE + TWO, :] = gathered[which, 0:TWO, :]
    for j in range(1, Y):
        yg_copies[j - 1].wait_recv()
        pack[...] = yg_recv[j - 1].astype(F32)
        for which in range(2):
            for side in range(2):
                first = TWO * (2 * which + side)
                cols = slice(side * half, (side + 1) * half)
                coarse_sum[which, ONE:ONE + TWO, cols] = (
                    coarse_sum[which, ONE:ONE + TWO, cols] + pack[first:first + TWO, :]
                )


    for g in range(groups):
        cols = slice(g * PAIR, (g + 1) * PAIR)
        for which in range(2):
            wide = coarse_sum[which, :, cols]
            high = wide.astype(BF16)
            low = (wide - high.astype(F32)).astype(BF16)
            both = jnp.concatenate([high, low], axis=0)
            total = own_grad[g, which * ROWS:(which + 1) * ROWS, :] + dot(restrict_t[...], both, 1, 0)
            stage[2 + which, :, cols] = total.astype(BF16)
    for g in range(groups):
        for side in range(2):
            grad_copy(side, g).wait_send()
    for copy in yg_copies:
        copy.wait_send()
    for part in range(parts):
        for s in range(len(MID)):
            mg_copy(s, part).wait_send()


def per_device(queries, keys, values, cotangent, restrict_one, restrict_two):
    rows, width = queries.shape
    groups = width // PAIR
    parts = 2
    z_parts = min(groups, 4)
    hbm = pl.BlockSpec(memory_space=pl.ANY)
    vmem = pl.BlockSpec(memory_space=pltpu.VMEM)
    dma = pltpu.SemaphoreType.DMA
    mid = len(MID)
    scratch = [
        pltpu.VMEM((4, ROWS, width), BF16),
        pltpu.VMEM((2, groups, 2 * ROWS, PAIR), BF16),
        pltpu.VMEM((2, groups, 2 * ROWS, PAIR), BF16),
        pltpu.VMEM((2, groups, 2 * ROWS, PAIR), BF16),
        pltpu.VMEM((groups, 2 * ROWS, PAIR), F32),
        pltpu.VMEM((2, ROWS, width), BF16),
        pltpu.VMEM((16, width), BF16),
        pltpu.VMEM((mid, 16, width), BF16),
        pltpu.VMEM((16, width // 2), BF16),
        pltpu.VMEM((Y - 1, 16, width // 2), BF16),
        pltpu.VMEM((2, 16, width), BF16),
        pltpu.VMEM((mid, 16, width), BF16),
        pltpu.VMEM((mid, 16, width), BF16),
        pltpu.VMEM((Z - 1, 2, 16, width), BF16),
        pltpu.VMEM((Z - 1, 2, 16, width), BF16),
        pltpu.VMEM((Y - 1, 16, width // 2), BF16),
        pltpu.VMEM((Y - 1, 16, width // 2), BF16),
        pltpu.VMEM((Z - 1, 2, 16, width), F32),
        pltpu.VMEM((ONE, ROWS), BF16),
        pltpu.VMEM((TWO, ROWS), BF16),
        pltpu.VMEM((16, ROWS), F32),
        pltpu.VMEM((16, width // 2), F32),
        pltpu.VMEM((2, 16, width), F32),
        pltpu.VMEM((COARSE, ROWS), F32),
        pltpu.VMEM((LEAD, 2 * ROWS, PAIR), BF16),
        pltpu.VMEM((LEAD, 2 * ROWS, PAIR), BF16),
        pltpu.VMEM((LEAD, PAIR, PADDED), BF16),
        pltpu.VMEM((LEAD, PAIR, PADDED), BF16),
        pltpu.VMEM((LEAD, PAIR, ROWS), F32),
        pltpu.VMEM((LEAD, 2, KEYS, ROWS), F32),
        pltpu.VMEM((LEAD, 2, KEYS, ROWS), F32),
        pltpu.VMEM((LEAD, 2, 2, 8, ROWS), F32),
        pltpu.VMEM((PADDED, 2 * ROWS), BF16),
        pltpu.VMEM((PADDED, 2 * ROWS), BF16),
        pltpu.VMEM((PAIR, ROWS), F32),
        pltpu.VMEM((PAIR, ROWS), F32),
        pltpu.VMEM((2, 16, width), F32),
        pltpu.VMEM((ROWS, 32), BF16),
        dma((6,)),
        dma((2, 2, groups)), dma((2, 2, groups)),
        dma((2, groups)), dma((2, groups)),
        dma((5,)), dma((mid,)),
        dma((4,)), dma((Y - 1,)),
        dma((Z - 2, z_parts)), dma((Z - 2, z_parts)), dma((2,)),
        dma((parts, mid)), dma((parts, mid)),
        dma((5, groups)), dma((5, groups)),
        dma((Y - 1,)), dma((Y - 1,)),
    ]
    stage = pl.pallas_call(
        functools.partial(kernel, groups, parts, z_parts),
        out_shape=pltpu.VMEM((4, ROWS, width), BF16),
        in_specs=[hbm] * 6,
        out_specs=vmem,
        scratch_shapes=scratch,
        compiler_params=pltpu.CompilerParams(
            collective_id=0, has_side_effects=True, vmem_limit_bytes=56 * 1024 * 1024
        ),
    )(queries, keys, values, cotangent, restrict_one, restrict_two)
    return tuple(stage[i] for i in range(4))


def solution(mesh):
    rows = P(("prompt", "seq"), None)
    return jax.shard_map(
        per_device, mesh=mesh, in_specs=(rows, rows, rows, rows, P(), P()),
        out_specs=(rows, rows, rows, rows), check_vma=False,
    )
```
